32 devices in a mesh: gx: 4 (over y, core), gy: 2 (over x), gz: 4 (over z).
Axes of the slice: x: 2, y: 2, z: 4, core: 2. Of those that a mesh axis runs over, the one named last changes fastest.
Arguments:
- positions: float32 [3, 4, 2, 4, 512], P(None, 'gx', 'gy', 'gz'), may hold values from 0 to 1
- velocities: float32 [3, 4, 2, 4, 512], P(None, 'gx', 'gy', 'gz'), may hold values from -1.8 to 1.8
- forces: float32 [3, 4, 2, 4, 512], P(None, 'gx', 'gy', 'gz'), may hold values from -6 to 6
- charges: float32 [4, 2, 4, 512], P('gx', 'gy', 'gz'), may hold values from -4 to 4
- atom_types: int32 [4, 2, 4, 512], P('gx', 'gy', 'gz'), may hold values from 0 to 31
- tile_counts: int32 [4, 2, 4], P('gx', 'gy', 'gz'), may hold values from 1 to 4, as said below
- pair_epsilon: float32 [32], replicated, may hold values from 0.01 to 0.1
- pair_sigma: float32 [32], replicated, may hold values from 0.1 to 0.15
Outputs:
- final_positions: float32 [3, 4, 2, 4, 512], P(None, 'gx', 'gy', 'gz')
- final_velocities: float32 [3, 4, 2, 4, 512], P(None, 'gx', 'gy', 'gz')
- final_forces: float32 [3, 4, 2, 4, 512], P(None, 'gx', 'gy', 'gz')
The draws below stay inside these ranges and needn't reach their ends.
Inputs may be any that keep to these rules, and one draw needn't show every extreme that they name: The live atoms of a box are its first 128 times tile_counts slots; some box has 4 live tiles in every draw.
All inputs are finite; a program needn't handle non-finite values.
Results may differ from the reference program's by a relative error of at most 0.0003.
Values sent between devices are 32-bit elements; how exact they have to be, the bound alone decides.
No kernel may reach another device: no remote copies, remote signals or barrier semaphores. Data moves between devices by JAX's collectives and lax.ppermute only.
A program may use at most 64 MiB of HBM per device.

```python
import math
import jax
import jax.numpy as jnp
from jax import lax

TILE = 128
TILES_MAX = 4
NTYPES = 32
STEPS = 2
SLOTS = 512
NGX = 4
NGY = 2
NGZ = 4


def draw_tile_counts(key, part):
    first, second = jax.random.split(key)
    heavy = jax.random.randint(first, (NGX, NGY, NGZ), 0, 4) == 0
    light = jax.random.randint(second, (NGX, NGY, NGZ), 1, max(TILES_MAX, 2))
    counts = jnp.where(heavy, TILES_MAX, light).astype(jnp.int32)
    return counts.at[0, 0, 0].set(TILES_MAX)


def touch_ends(entries, key, low, high):
    spot = [jax.random.randint(jax.random.fold_in(key, axis), (), 0, length) for axis, length in enumerate(entries.shape)]
    main_axis = entries.shape.index(max(entries.shape))
    beside = spot[:main_axis] + [(spot[main_axis] + 1) % entries.shape[main_axis]] + spot[main_axis + 1:]
    return entries.at[tuple(spot)].set(low).at[tuple(beside)].set(high)


def levels(rng, dims, cuts, least, largest):
    factor_of, own = 1.0, jax.random.fold_in(rng, 6)
    for dim, parts in cuts:
        draws = jnp.exp(jax.random.uniform(jax.random.fold_in(own, dim), (parts,), jnp.float32, least / len(cuts), largest / len(cuts)))
        factor_of = factor_of * jnp.repeat(draws, dims[dim] // parts).reshape([-1 if axis == dim else 1 for axis in range(len(dims))])
    return factor_of


def noise(key, dims, spread, most, cuts=(), held_as=jnp.bfloat16):
    values = jax.random.normal(key, dims, jnp.float32) * spread
    if len(cuts) > 0:
        values = levels(key, dims, cuts, -0.22, 0.18) * values
    return jnp.clip(values, min=-most, max=most).astype(held_as)


def setup_inputs(seed: int = 0) -> dict:
    keys = jax.random.split(jax.random.key(seed), 9)
    positions = jnp.clip(1.0 * jax.random.uniform(keys[0], (3, NGX, NGY, NGZ, SLOTS), jnp.float32) ** levels(keys[0], (3, NGX, NGY, NGZ, SLOTS), ((1, 4), (2, 2), (3, 4)), -0.2, 0.2), 0.0, 1.0)
    velocities = noise(keys[1], (3, NGX, NGY, NGZ, SLOTS), 0.3, 1.8, ((1, 4), (2, 2), (3, 4)), jnp.float32)
    forces = noise(keys[2], (3, NGX, NGY, NGZ, SLOTS), 1.0, 6.0, ((1, 4), (2, 2), (3, 4)), jnp.float32)
    charges = noise(keys[3], (NGX, NGY, NGZ, SLOTS), 1.0, 4.0, ((0, 4), (1, 2), (2, 4)), jnp.float32)
    atom_types = touch_ends(jax.random.randint(keys[4], (NGX, NGY, NGZ, SLOTS), 0, NTYPES), jax.random.fold_in(keys[4], 1), 0, NTYPES - 1).astype(jnp.int32)
    tile_counts = draw_tile_counts(jax.random.fold_in(keys[8], 71), 0)
    pair_epsilon = jnp.clip(jnp.exp(jax.random.uniform(keys[6], (NTYPES,), jnp.float32, math.log(0.01), math.log(0.1))), 0.01, 0.1)
    pair_sigma = jnp.clip(jax.random.uniform(keys[7], (NTYPES,), jnp.float32, 0.1, 0.15), 0.1, 0.15)
    return dict(positions=positions, velocities=velocities, forces=forces, charges=charges, atom_types=atom_types, tile_counts=tile_counts, pair_epsilon=pair_epsilon, pair_sigma=pair_sigma)


COULOMB = 0.02
KAPPA = 2.0
SOFTEN = 0.0225
CUTOFF = 0.81
TIME_STEP = 0.05
HALF_STEP = 0.025
HALF_PLATE = ((1, 0), (1, 1), (0, 1), (-1, 1))

def pair_energy(left_pos, right_pos, left_par, right_par, weight):
    diff = left_pos[:, :, None] - right_pos[:, None, :]
    distance = lax.optimization_barrier(jnp.sum(diff * diff, axis=0))
    soft_sq = distance + SOFTEN
    soft = jnp.sqrt(soft_sq)
    coulomb = COULOMB * left_par[0][:, None] * right_par[0][None, :] * jnp.exp(-KAPPA * soft) / soft
    sigma = 0.5 * (left_par[2][:, None] + right_par[2][None, :])
    ratio = sigma * sigma / soft_sq
    cubed = ratio * ratio * ratio
    lennard = 4.0 * left_par[1][:, None] * right_par[1][None, :] * (cubed * cubed - cubed)
    switch = jnp.square(jnp.maximum(1.0 - distance / CUTOFF, 0.0))
    return jnp.sum(weight * (coulomb + lennard) * switch)

def tile_pair(left, right, weight):

    def energy(left_pos, right_pos):
        return pair_energy(left_pos, right_pos, left[3:], right[3:], weight)
    value, pull = jax.vjp(energy, left[:3], right[:3])
    grad_left, grad_right = pull(jnp.ones_like(value))
    return (-grad_left, -grad_right)

def padded_forces(left, right, halve):
    tiles = left.shape[1] // TILE
    width = right.shape[1]
    pieces = left.reshape(6, tiles, TILE).transpose(1, 0, 2)
    starts = jnp.arange(tiles, dtype=jnp.int32) * TILE

    def visit(carry, item):
        piece, start = item
        if halve:
            rows = start + lax.broadcasted_iota(jnp.int32, (TILE, width), 0)
            cols = lax.broadcasted_iota(jnp.int32, (TILE, width), 1)
            weight = jnp.where(rows != cols, 0.5, 0.0).astype(left.dtype)
        else:
            weight = jnp.ones((), left.dtype)
        force_left, force_right = tile_pair(piece, right, weight)
        return (carry + force_right, force_left)
    force_right, stacked = lax.scan(visit, jnp.zeros((3, width), left.dtype), (pieces, starts))
    return (stacked.transpose(1, 0, 2).reshape(3, tiles * TILE), force_right)

def box_forces(tower, plate, own, above):
    force_tower, force_plate = padded_forces(tower, plate, False)
    force_above, force_own = padded_forces(above, own, False)
    self_left, self_right = padded_forces(own, own, True)
    return (force_tower, force_plate, force_above, force_own + self_left + self_right)

def neighbour(record, along_x, along_y, along_z):
    moved = jnp.roll(record, (-along_x, -along_y, -along_z), axis=(1, 2, 3))
    shift = jnp.array([along_x, along_y, along_z], dtype=record.dtype)
    return jnp.concatenate([moved[:3] + shift[:, None, None, None, None], moved[3:]], 0)

def total_forces(record):
    boxes = NGX * NGY * NGZ
    group = math.gcd(boxes, 16)
    slots = record.shape[-1]
    below = neighbour(record, 0, 0, -1)
    above = neighbour(record, 0, 0, 1)
    tower = jnp.concatenate([below, record, above], 4)
    plate = jnp.concatenate([neighbour(record, along_x, along_y, 0) for along_x, along_y in HALF_PLATE], 4)

    def flatten(array):
        width = array.shape[-1]
        return array.reshape(6, boxes, width).transpose(1, 0, 2).reshape(boxes // group, group, 6, width)

    def unflatten(array):
        width = array.shape[-1]
        return array.reshape(boxes, 3, width).transpose(1, 0, 2).reshape(3, NGX, NGY, NGZ, width)

    def batch(items):
        return jax.vmap(box_forces)(*items)
    force_tower, force_plate, force_above, force_own = lax.map(batch, (flatten(tower), flatten(plate), flatten(record), flatten(above)))
    force_tower = unflatten(force_tower)
    force_plate = unflatten(force_plate)
    total = unflatten(force_own) + force_tower[..., slots:2 * slots]
    total = total + jnp.roll(force_tower[..., :slots], -1, axis=3)
    total = total + jnp.roll(force_tower[..., 2 * slots:] + unflatten(force_above), 1, axis=3)
    for number, (along_x, along_y) in enumerate(HALF_PLATE):
        part = force_plate[..., number * slots:(number + 1) * slots]
        total = total + jnp.roll(part, (along_x, along_y), axis=(1, 2))
    return total

def reference(positions, velocities, forces, charges, atom_types, tile_counts, pair_epsilon, pair_sigma):
    index = jnp.arange(SLOTS, dtype=jnp.int32)
    live = (index < tile_counts[..., None] * TILE).astype(positions.dtype)
    kinds = jnp.arange(NTYPES, dtype=jnp.int32)[:, None, None, None, None]
    member = (atom_types[None] == kinds).astype(positions.dtype)
    root = lax.optimization_barrier(jnp.sum(member * jnp.sqrt(pair_epsilon)[:, None, None, None, None], 0)) * live
    sigma = lax.optimization_barrier(jnp.sum(member * pair_sigma[:, None, None, None, None], 0))
    params = jnp.stack([charges * live, root, sigma], 0)
    places, velocity, pushing = (positions, velocities, forces)
    for step in range(STEPS):
        velocity = velocity + HALF_STEP * pushing
        places = places + TIME_STEP * velocity
        pushing = total_forces(jnp.concatenate([places, params], 0))
        velocity = velocity + HALF_STEP * pushing
    return (places, velocity, pushing)
```

```python
import functools

import jax
import jax.numpy as jnp
from jax import lax
from jax.experimental import pallas as pl
from jax.experimental.pallas import tpu as pltpu
from jax.sharding import PartitionSpec as P

TILE = 128
STEPS = 2

COULOMB = 0.02
SOFTEN = 0.0225
CUTOFF = 0.81
TIME_STEP = 0.05
HALF_STEP = 0.025
HALF_PLATE = ((1, 0), (1, 1), (0, 1), (-1, 1))
REACH = 4.0 * (CUTOFF + SOFTEN)
SCALE = 1.0 / (4.0 * CUTOFF * CUTOFF)

F32 = jnp.float32
BF16 = jnp.bfloat16


def start_kernel(count, epsilon, sigma, pos, vel, frc, charge, kinds, record, half):
    live_tiles = count[0, 0]
    slots = pos.shape[1]
    live = lax.broadcasted_iota(jnp.int32, (1, slots), 1) < live_tiles * TILE
    kind = kinds[...]
    depth = jnp.zeros((1, slots), F32)
    size = jnp.zeros((1, slots), F32)
    for k in range(epsilon.shape[1]):
        same = kind == k
        depth = jnp.where(same, epsilon[0, k], depth)
        size = jnp.where(same, sigma[0, k], size)
    velocity = vel[...] + HALF_STEP * frc[...]
    places = pos[...] + TIME_STEP * velocity
    half[...] = velocity
    record[...] = jnp.concatenate(
        [
            places,
            jnp.where(live, charge[...], 0.0),
            jnp.where(live, jnp.sqrt(depth), 0.0),
            size,
            jnp.full((1, slots), live_tiles.astype(F32)),
            jnp.zeros((1, slots), F32),
        ],
        0,
    )


def split(value):
    high = value.astype(BF16).astype(F32)
    rest = value - high
    middle = rest.astype(BF16).astype(F32)
    return high, middle, rest - middle


def coordinates(record, shift):
    places = record[0:3, :]
    row = lax.broadcasted_iota(jnp.int32, places.shape, 0)
    moved = jnp.zeros_like(places)
    for axis in range(3):
        moved = jnp.where(row == axis, places + (shift[axis] - 0.5), moved)
    return moved


def moments(places):
    high, middle, low = split(places)
    one = jnp.ones((1, places.shape[1]), F32)
    zero = jnp.zeros((6, places.shape[1]), F32)
    return jnp.concatenate([high, middle, low, one, zero], 0).astype(BF16)


def norm(places):
    return 4.0 * jnp.sum(places * places, axis=0, keepdims=True)


def left_rows(record, places):
    charge, root, size = record[3:4, :], record[4:5, :], record[5:6, :]
    one = jnp.ones_like(charge)
    zero = jnp.zeros((7, charge.shape[1]), F32)
    rows = jnp.concatenate(
        [places, charge, root, size, norm(places) + 4.0 * SOFTEN, one, size * size, zero], 0
    )
    high, middle, low = split(rows)
    return jnp.concatenate([high, high, high, middle, middle, low], 0)


def right_stack(rows):
    high, middle, low = split(rows)
    return jnp.concatenate([high, middle, low, high, middle, high], 0).astype(BF16)


def right_rows(record, places):
    charge, root, size = record[3:4, :], record[4:5, :], record[5:6, :]
    slots = charge.shape[1]
    one = jnp.ones_like(charge)

    def zero(count):
        return jnp.zeros((count, slots), F32)

    length = [-8.0 * places, zero(3), one, norm(places), zero(8)]
    coulomb = [zero(3), 2.0 * COULOMB * charge, zero(12)]
    lennard = [zero(4), 4.0 * root, zero(11)]
    contact = [zero(5), 2.0 * size, zero(1), size * size, one, zero(7)]
    return [right_stack(jnp.concatenate(r, 0)) for r in (length, coulomb, lennard, contact)]


def pair_force(length, coulomb, lennard, contact):
    inverse = lax.rsqrt(length)
    inverse_sq = inverse * inverse
    screened = coulomb * jnp.exp(-(length * inverse)) * inverse
    ratio = contact * inverse_sq
    cubed = ratio * ratio * ratio
    depth = lennard * cubed
    less = cubed - 1.0
    slope = screened * inverse + inverse_sq * (screened + 6.0 * (depth * (cubed + less)))
    switch = jnp.maximum(REACH - length, 0.0)
    return switch * (switch * slope + 4.0 * (screened + depth * less))


def halves(force):
    high = force.astype(BF16)
    return high, (force - high.astype(F32)).astype(BF16)


def dot(a, b):
    return jnp.dot(a, b, preferred_element_type=F32)


def dot_rows(a, b):
    return lax.dot_general(a, b, (((1,), (1,)), ((), ())), preferred_element_type=F32)


def resolve(acc, places):
    turned = acc[0:3, :] + acc[3:6, :] + acc[6:9, :]
    return SCALE * (places * acc[9:10, :] - turned)


def force_kernel(*refs):
    own, below, above, plates = refs[0], refs[1], refs[2], refs[3:7]
    out_own, out_below, out_above, out_plates = refs[7], refs[8], refs[9], refs[10:14]
    left, left_x, left_acc, right, right_x, right_acc = refs[14:]
    slots = own.shape[1]
    tiles = slots // TILE

    def live(ref):
        return jnp.max(ref[6:7, 0:TILE]).astype(jnp.int32)

    n_own, n_below, n_above = live(own), live(below), live(above)
    n_plates = [live(ref) for ref in plates]

    own_x = coordinates(own, (0, 0, 0))
    below_x = coordinates(below, (0, 0, -1))
    above_x = coordinates(above, (0, 0, 1))
    plate_x = [coordinates(ref, (dx, dy, 0)) for ref, (dx, dy) in zip(plates, HALF_PLATE)]

    def cut(array, tile):
        return array[:, tile * TILE : (tile + 1) * TILE]

    start = jnp.int32(0)
    left_start = []
    for ref, places, count in (
        (below, below_x, n_below),
        (own, own_x, n_own),
        (above, above_x, n_above),
    ):
        rows = left_rows(ref, places)
        rows = jnp.concatenate([rows, jnp.zeros((TILE - rows.shape[0], slots), F32)], 0)
        dots = moments(places)
        for tile in range(tiles):
            left[start + tile] = cut(rows, tile).T.astype(BF16)
            left_x[start + tile] = cut(dots, tile)
        left_start.append(start)
        start = start + count
    n_left = start

    start = jnp.int32(0)
    right_start = []
    for ref, places, count in zip(plates, plate_x, n_plates):
        parts = right_rows(ref, places)
        dots = moments(places)
        for tile in range(tiles):
            for number, part in enumerate(parts):
                right[start + tile, number] = cut(part, tile)
            right_x[start + tile] = cut(dots, tile)
        right_start.append(start)
        start = start + count
    n_plate = start
    parts = right_rows(own, own_x)
    dots = moments(own_x)
    for tile in range(tiles):

        @pl.when(tile < n_own)
        def _():
            spot = n_plate + n_own - 1 - tile
            for number, part in enumerate(parts):
                right[spot, number] = cut(part, tile)
            right_x[spot] = cut(dots, tile)

    empty = n_plate + n_own
    right[empty, 0] = cut(parts[0], 0)
    for number in range(1, 4):
        right[empty, number] = jnp.zeros(right.shape[2:], BF16)
    right_x[empty] = cut(dots, 0)
    right_acc[...] = jnp.zeros(right_acc.shape, F32)

    first_own, first_above = left_start[1], left_start[2]
    depth = right.shape[2]

    def per_left(t, carry):
        mine = left[t][:, :depth]
        mine_x = left_x[t]
        extent = n_plate + jnp.where(
            t < first_own, 0, jnp.where(t < first_above, n_own - 1 - (t - first_own), n_own)
        )

        def per_pair(p, acc):
            one = 2 * p
            two = jnp.where(one + 1 < extent, one + 1, empty)
            parts = [
                dot(mine, jnp.concatenate([right[one, number], right[two, number]], 1))
                for number in range(4)
            ]
            high, low = halves(pair_force(*parts))
            theirs_x = jnp.concatenate([right_x[one], right_x[two]], 1)
            acc = acc + dot_rows(theirs_x, high) + dot_rows(theirs_x, low)
            back = dot(mine_x, high) + dot(mine_x, low)
            right_acc[one] = right_acc[one] + back[:, :TILE]
            right_acc[two] = right_acc[two] + back[:, TILE:]
            return acc

        left_acc[t] = lax.fori_loop(
            0, (extent + 1) // 2, per_pair, jnp.zeros(left_acc.shape[1:], F32)
        )
        return carry

    lax.fori_loop(0, n_left, per_left, 0)

    def per_self(tile, carry):
        t = first_own + tile
        spot = n_plate + n_own - 1 - tile
        mine = left[t][:, :depth]
        force = pair_force(*[dot(mine, right[spot, number]) for number in range(4)])
        row = lax.broadcasted_iota(jnp.int32, force.shape, 0)
        col = lax.broadcasted_iota(jnp.int32, force.shape, 1)
        high, low = halves(jnp.where(row == col, 0.0, force))
        theirs_x = right_x[spot]
        left_acc[t] = left_acc[t] + dot_rows(theirs_x, high) + dot_rows(theirs_x, low)
        return carry

    lax.fori_loop(0, n_own, per_self, 0)

    def give(out, tile, count, acc, places):
        force = resolve(acc, cut(places, tile))
        out[:, tile * TILE : (tile + 1) * TILE] = jnp.where(tile < count, force, 0.0)

    for tile in range(tiles):
        give(out_below, tile, n_below, left_acc[left_start[0] + tile], below_x)
        give(out_above, tile, n_above, left_acc[left_start[2] + tile], above_x)
        spot = jnp.maximum(n_plate + n_own - 1 - tile, 0)
        give(out_own, tile, n_own, left_acc[left_start[1] + tile] + right_acc[spot], own_x)
        for out, first, count, places in zip(out_plates, right_start, n_plates, plate_x):
            give(out, tile, count, right_acc[first + tile], places)


def middle_kernel(record, half, own, *refs):
    others, (new_record, new_half) = refs[:6], refs[6:]
    force = own[...]
    for ref in others:
        force = force + ref[...]
    velocity = half[...] + HALF_STEP * force
    velocity = velocity + HALF_STEP * force
    new_half[...] = velocity
    new_record[3:8, :] = record[3:8, :]
    new_record[0:3, :] = record[0:3, :] + TIME_STEP * velocity


def last_kernel(record, half, own, *refs):
    others, (places, velocity, pushing) = refs[:6], refs[6:]
    force = own[...]
    for ref in others:
        force = force + ref[...]
    places[...] = record[0:3, :]
    velocity[...] = half[...] + HALF_STEP * force
    pushing[...] = force


VMEM = pltpu.VMEM
SMEM = pltpu.SMEM


def shape(*dims):
    return jax.ShapeDtypeStruct(dims, F32)


def whole(space=VMEM):
    return pl.BlockSpec(memory_space=space)


def box_forces(own, below, above, plates):
    slots = own.shape[1]
    tiles = slots // TILE
    pairs = 20 * tiles * tiles * TILE * TILE
    return pl.pallas_call(
        force_kernel,
        out_shape=[shape(3, slots)] * 7,
        in_specs=[whole()] * 7,
        out_specs=[whole()] * 7,
        scratch_shapes=[
            VMEM((3 * tiles, TILE, TILE), BF16),
            VMEM((3 * tiles, 16, TILE), BF16),
            VMEM((3 * tiles, 16, TILE), F32),
            VMEM((5 * tiles + 1, 4, 96, TILE), BF16),
            VMEM((5 * tiles + 1, 16, TILE), BF16),
            VMEM((5 * tiles + 1, 16, TILE), F32),
        ],
        compiler_params=pltpu.CompilerParams(vmem_limit_bytes=32 * 1024 * 1024),
        cost_estimate=pl.CostEstimate(
            flops=50 * pairs, bytes_accessed=14 * 4 * 8 * slots, transcendentals=2 * pairs
        ),
    )(own, below, above, *plates)


def neighbours(mesh_axes):
    nx, ny, nz = mesh_axes

    def pairs(dx, dy, dz):
        table = []
        for x in range(nx):
            for y in range(ny):
                for z in range(nz):
                    source = (((x + dx) % nx) * ny + (y + dy) % ny) * nz + (z + dz) % nz
                    table.append((source, (x * ny + y) * nz + z))
        return table

    offsets = [(0, 0, -1), (0, 0, 1)] + [(dx, dy, 0) for dx, dy in HALF_PLATE]
    imports = [pairs(*offset) for offset in offsets]
    returns = [[(target, source) for source, target in table] for table in imports]
    return imports, returns


def on_device(axes, positions, velocities, forces, charges, types, counts, epsilon, sigma):
    slots = positions.shape[-1]
    names = ("gx", "gy", "gz")
    imports, returns = neighbours(axes)
    record, half = pl.pallas_call(
        start_kernel,
        out_shape=[shape(8, slots), shape(3, slots)],
        in_specs=[whole(SMEM)] * 3 + [whole()] * 5,
        out_specs=[whole()] * 2,
    )(
        counts.reshape(1, 1),
        epsilon.reshape(1, -1),
        sigma.reshape(1, -1),
        positions.reshape(3, slots),
        velocities.reshape(3, slots),
        forces.reshape(3, slots),
        charges.reshape(1, slots),
        types.reshape(1, slots),
    )
    for step in range(STEPS):
        received = [lax.ppermute(record, names, table) for table in imports]
        parts = box_forces(record, received[0], received[1], received[2:])
        returned = [lax.ppermute(part, names, table) for part, table in zip(parts[1:], returns)]
        if step < STEPS - 1:
            record, half = pl.pallas_call(
                middle_kernel,
                out_shape=[shape(8, slots), shape(3, slots)],
                in_specs=[whole()] * 9,
                out_specs=[whole()] * 2,
            )(record, half, parts[0], *returned)
        else:
            outs = pl.pallas_call(
                last_kernel,
                out_shape=[shape(3, slots)] * 3,
                in_specs=[whole()] * 9,
                out_specs=[whole()] * 3,
            )(record, half, parts[0], *returned)
    return tuple(out.reshape(3, 1, 1, 1, slots) for out in outs)


def solution(mesh):
    boxes = P(None, "gx", "gy", "gz", None)
    slot = P("gx", "gy", "gz", None)
    in_specs = (boxes, boxes, boxes, slot, slot, P("gx", "gy", "gz"), P(), P())
    axes = tuple(mesh.shape[name] for name in ("gx", "gy", "gz"))
    return jax.shard_map(
        functools.partial(on_device, axes),
        mesh=mesh,
        in_specs=in_specs,
        out_specs=(boxes, boxes, boxes),
        check_vma=False,
    )
```

```python
import functools

import jax
import jax.numpy as jnp
from jax import lax
from jax.experimental import pallas as pl
from jax.experimental.pallas import tpu as pltpu
from jax.sharding import PartitionSpec as P

TILE = 128
STEPS = 2

COULOMB = 0.02
SOFTEN = 0.0225
CUTOFF = 0.81
TIME_STEP = 0.05
HALF_STEP = 0.025
HALF_PLATE = ((1, 0), (1, 1), (0, 1), (-1, 1))
REACH = 4.0 * (CUTOFF + SOFTEN)
SCALE = 1.0 / (4.0 * CUTOFF * CUTOFF)

F32 = jnp.float32
BF16 = jnp.bfloat16


def start_kernel(count, epsilon, sigma, pos, vel, frc, charge, kinds, record, half):
    live_tiles = count[0, 0]
    slots = pos.shape[1]
    live = lax.broadcasted_iota(jnp.int32, (1, slots), 1) < live_tiles * TILE
    kind = kinds[...]
    depth = jnp.zeros((1, slots), F32)
    size = jnp.zeros((1, slots), F32)
    for k in range(epsilon.shape[1]):
        same = kind == k
        depth = jnp.where(same, epsilon[0, k], depth)
        size = jnp.where(same, sigma[0, k], size)
    velocity = vel[...] + HALF_STEP * frc[...]
    places = pos[...] + TIME_STEP * velocity
    half[...] = velocity
    record[...] = jnp.concatenate(
        [
            places,
            jnp.where(live, charge[...], 0.0),
            jnp.where(live, jnp.sqrt(depth), 0.0),
            size,
            jnp.full((1, slots), live_tiles.astype(F32)),
            jnp.zeros((1, slots), F32),
        ],
        0,
    )


def split(value):
    high = value.astype(BF16).astype(F32)
    rest = value - high
    middle = rest.astype(BF16).astype(F32)
    return high, middle, rest - middle


def coordinates(record, shift):
    places = record[0:3, :]
    row = lax.broadcasted_iota(jnp.int32, places.shape, 0)
    moved = jnp.zeros_like(places)
    for axis in range(3):
        moved = jnp.where(row == axis, places + (shift[axis] - 0.5), moved)
    return moved


def moments(places):
    high, middle, low = split(places)
    one = jnp.ones((1, places.shape[1]), F32)
    zero = jnp.zeros((6, places.shape[1]), F32)
    return jnp.concatenate([high, middle, low, one, zero], 0).astype(BF16)


def norm(places):
    return 4.0 * jnp.sum(places * places, axis=0, keepdims=True)


def left_rows(record, places):
    charge, root, size = record[3:4, :], record[4:5, :], record[5:6, :]
    one = jnp.ones_like(charge)
    zero = jnp.zeros((7, charge.shape[1]), F32)
    rows = jnp.concatenate(
        [places, charge, root, size, norm(places) + 4.0 * SOFTEN, one, size * size, zero], 0
    )
    high, middle, low = split(rows)
    return jnp.concatenate([high, high, high, middle, middle, low], 0)


def right_stack(rows):
    high, middle, low = split(rows)
    return jnp.concatenate([high, middle, low, high, middle, high], 0).astype(BF16)


def right_rows(record, places):
    charge, root, size = record[3:4, :], record[4:5, :], record[5:6, :]
    slots = charge.shape[1]
    one = jnp.ones_like(charge)

    def zero(count):
        return jnp.zeros((count, slots), F32)

    length = [-8.0 * places, zero(3), one, norm(places), zero(8)]
    coulomb = [zero(3), 2.0 * COULOMB * charge, zero(12)]
    lennard = [zero(4), 4.0 * root, zero(11)]
    contact = [zero(5), 2.0 * size, zero(1), size * size, one, zero(7)]
    return [right_stack(jnp.concatenate(r, 0)) for r in (length, coulomb, lennard, contact)]


def pair_force(length, coulomb, lennard, contact):
    inverse = lax.rsqrt(length)
    inverse_sq = inverse * inverse
    screened = coulomb * jnp.exp(-(length * inverse)) * inverse
    ratio = contact * inverse_sq
    cubed = ratio * ratio * ratio
    depth = lennard * cubed
    less = cubed - 1.0
    slope = screened * inverse + inverse_sq * (screened + 6.0 * (depth * (cubed + less)))
    switch = jnp.maximum(REACH - length, 0.0)
    return switch * (switch * slope + 4.0 * (screened + depth * less))


def halves(force):
    high = force.astype(BF16)
    return high, (force - high.astype(F32)).astype(BF16)


def dot(a, b):
    return jnp.dot(a, b, preferred_element_type=F32)


def dot_rows(a, b):
    return lax.dot_general(a, b, (((1,), (1,)), ((), ())), preferred_element_type=F32)


def resolve(acc, places):
    turned = acc[0:3, :] + acc[3:6, :] + acc[6:9, :]
    return SCALE * (places * acc[9:10, :] - turned)


def force_kernel(*refs):
    own, below, above, plates = refs[0], refs[1], refs[2], refs[3:7]
    out_own, out_below, out_above, out_plates = refs[7], refs[8], refs[9], refs[10:14]
    left, left_x, left_acc, right, right_x, right_acc = refs[14:20]
    parts_a, parts_b, force_a, force_b = refs[20:]
    slots = own.shape[1]
    tiles = slots // TILE

    def live(ref):
        return jnp.max(ref[6:7, 0:TILE]).astype(jnp.int32)

    n_own, n_below, n_above = live(own), live(below), live(above)
    n_plates = [live(ref) for ref in plates]

    own_x = coordinates(own, (0, 0, 0))
    below_x = coordinates(below, (0, 0, -1))
    above_x = coordinates(above, (0, 0, 1))
    plate_x = [coordinates(ref, (dx, dy, 0)) for ref, (dx, dy) in zip(plates, HALF_PLATE)]

    def cut(array, tile):
        return array[:, tile * TILE : (tile + 1) * TILE]

    start = jnp.int32(0)
    left_start = []
    for ref, places, count in (
        (below, below_x, n_below),
        (own, own_x, n_own),
        (above, above_x, n_above),
    ):
        rows = left_rows(ref, places)
        dots = moments(places)
        for tile in range(tiles):
            left[start + tile] = cut(rows, tile).T.astype(BF16)
            left_x[start + tile] = cut(dots, tile)
        left_start.append(start)
        start = start + count
    n_left = start

    start = jnp.int32(0)
    right_start = []
    for ref, places, count in zip(plates, plate_x, n_plates):
        parts = right_rows(ref, places)
        dots = moments(places)
        for tile in range(tiles):
            for number, part in enumerate(parts):
                right[start + tile, number] = cut(part, tile)
            right_x[start + tile] = cut(dots, tile)
        right_start.append(start)
        start = start + count
    n_plate = start
    parts = right_rows(own, own_x)
    dots = moments(own_x)
    for tile in range(tiles):

        @pl.when(tile < n_own)
        def _():
            spot = n_plate + n_own - 1 - tile
            for number, part in enumerate(parts):
                right[spot, number] = cut(part, tile)
            right_x[spot] = cut(dots, tile)

    empty = n_plate + n_own
    right[empty, 0] = cut(parts[0], 0)
    for number in range(1, 4):
        right[empty, number] = jnp.zeros(right.shape[2:], BF16)
    right_x[empty] = cut(dots, 0)
    right_acc[...] = jnp.zeros(right_acc.shape, F32)

    first_own, first_above = left_start[1], left_start[2]

    def extent(t):
        own_part = jnp.where(t < first_above, n_own - 1 - (t - first_own), n_own)
        return n_plate + jnp.where(t < first_own, 0, own_part)

    def following(block):
        t, p = block
        step = 2 * p + 2 < extent(t)
        return jnp.where(step, t, jnp.minimum(t + 1, n_left)), jnp.where(step, p + 1, 0)

    def place(block):
        t, p = block
        inside = t < n_left
        one = jnp.where(inside, 2 * p, empty)
        two = jnp.where(inside & (2 * p + 1 < extent(t)), 2 * p + 1, empty)
        return jnp.where(inside, t, 0), one, two

    def spread(spots, parts):
        t, one, two = spots
        mine = left[t]
        for number in range(4):
            theirs = jnp.concatenate([right[one, number], right[two, number]], 1)
            parts[number] = dot(mine, theirs)

    def work(parts, split_force):
        high, low = halves(pair_force(*[parts[number] for number in range(4)]))
        split_force[0] = high
        split_force[1] = low

    def gather(spots, split_force):
        t, one, two = spots
        high, low = split_force[0], split_force[1]
        theirs_x = jnp.concatenate([right_x[one], right_x[two]], 1)
        mine_x = left_x[t]
        left_acc[t] = left_acc[t] + (dot_rows(theirs_x, high) + dot_rows(theirs_x, low))
        back = dot(mine_x, high) + dot(mine_x, low)
        right_acc[one] = right_acc[one] + back[:, :TILE]
        right_acc[two] = right_acc[two] + back[:, TILE:]

    def two_blocks(_, carry):
        block, before = carry
        spots = place(block)
        block = following(block)
        middle = place(block)
        block = following(block)
        spread(middle, parts_b)
        work(parts_a, force_a)
        gather(before, force_b)
        spread(place(block), parts_a)
        work(parts_b, force_b)
        gather(spots, force_a)
        return block, middle

    def pairs_of(count):
        return (count + 1) // 2

    blocks = n_below * pairs_of(n_plate) + n_above * pairs_of(n_plate + n_own)
    for tile in range(tiles):
        blocks = blocks + jnp.where(tile < n_own, pairs_of(n_plate + tile), 0)
    left_acc[...] = jnp.zeros(left_acc.shape, F32)
    force_b[...] = jnp.zeros(force_b.shape, BF16)
    zero = jnp.int32(0)
    first = (zero, zero)
    spread(place(first), parts_a)
    _, last = lax.fori_loop(0, pairs_of(blocks), two_blocks, (first, (zero, empty, empty)))
    gather(last, force_b)

    for tile in range(tiles):
        t = first_own + tile
        spot = jnp.maximum(n_plate + n_own - 1 - tile, 0)
        mine = left[t]
        force = pair_force(*[dot(mine, right[spot, number]) for number in range(4)])
        row = lax.broadcasted_iota(jnp.int32, force.shape, 0)
        col = lax.broadcasted_iota(jnp.int32, force.shape, 1)
        high, low = halves(jnp.where((row != col) & (tile < n_own), force, 0.0))
        theirs_x = right_x[spot]
        left_acc[t] = left_acc[t] + dot_rows(theirs_x, high) + dot_rows(theirs_x, low)

    def give(out, tile, count, acc, places):
        force = resolve(acc, cut(places, tile))
        out[:, tile * TILE : (tile + 1) * TILE] = jnp.where(tile < count, force, 0.0)

    for tile in range(tiles):
        give(out_below, tile, n_below, left_acc[left_start[0] + tile], below_x)
        give(out_above, tile, n_above, left_acc[left_start[2] + tile], above_x)
        spot = jnp.maximum(n_plate + n_own - 1 - tile, 0)
        give(out_own, tile, n_own, left_acc[left_start[1] + tile] + right_acc[spot], own_x)
        for out, first, count, places in zip(out_plates, right_start, n_plates, plate_x):
            give(out, tile, count, right_acc[first + tile], places)


def middle_kernel(record, half, own, *refs):
    others, (new_record, new_half) = refs[:6], refs[6:]
    force = own[...]
    for ref in others:
        force = force + ref[...]
    velocity = half[...] + HALF_STEP * force
    velocity = velocity + HALF_STEP * force
    new_half[...] = velocity
    new_record[3:8, :] = record[3:8, :]
    new_record[0:3, :] = record[0:3, :] + TIME_STEP * velocity


def last_kernel(record, half, own, *refs):
    others, (places, velocity, pushing) = refs[:6], refs[6:]
    force = own[...]
    for ref in others:
        force = force + ref[...]
    places[...] = record[0:3, :]
    velocity[...] = half[...] + HALF_STEP * force
    pushing[...] = force


VMEM = pltpu.VMEM
SMEM = pltpu.SMEM


def shape(*dims):
    return jax.ShapeDtypeStruct(dims, F32)


def whole(space=VMEM):
    return pl.BlockSpec(memory_space=space)


def box_forces(own, below, above, plates):
    slots = own.shape[1]
    tiles = slots // TILE
    pairs = 20 * tiles * tiles * TILE * TILE
    return pl.pallas_call(
        force_kernel,
        out_shape=[shape(3, slots)] * 7,
        in_specs=[whole()] * 7,
        out_specs=[whole()] * 7,
        scratch_shapes=[
            VMEM((3 * tiles, TILE, 96), BF16),
            VMEM((3 * tiles, 16, TILE), BF16),
            VMEM((3 * tiles, 16, TILE), F32),
            VMEM((5 * tiles + 1, 4, 96, TILE), BF16),
            VMEM((5 * tiles + 1, 16, TILE), BF16),
            VMEM((5 * tiles + 1, 16, TILE), F32),
            VMEM((4, TILE, 2 * TILE), F32),
            VMEM((4, TILE, 2 * TILE), F32),
            VMEM((2, TILE, 2 * TILE), BF16),
            VMEM((2, TILE, 2 * TILE), BF16),
        ],
        compiler_params=pltpu.CompilerParams(vmem_limit_bytes=32 * 1024 * 1024),
        cost_estimate=pl.CostEstimate(
            flops=50 * pairs, bytes_accessed=14 * 4 * 8 * slots, transcendentals=2 * pairs
        ),
    )(own, below, above, *plates)


def neighbours(mesh_axes):
    nx, ny, nz = mesh_axes

    def pairs(dx, dy, dz):
        table = []
        for x in range(nx):
            for y in range(ny):
                for z in range(nz):
                    source = (((x + dx) % nx) * ny + (y + dy) % ny) * nz + (z + dz) % nz
                    table.append((source, (x * ny + y) * nz + z))
        return table

    offsets = [(0, 0, -1), (0, 0, 1)] + [(dx, dy, 0) for dx, dy in HALF_PLATE]
    imports = [pairs(*offset) for offset in offsets]
    returns = [[(target, source) for source, target in table] for table in imports]
    return imports, returns


def on_device(axes, positions, velocities, forces, charges, types, counts, epsilon, sigma):
    slots = positions.shape[-1]
    names = ("gx", "gy", "gz")
    imports, returns = neighbours(axes)
    record, half = pl.pallas_call(
        start_kernel,
        out_shape=[shape(8, slots), shape(3, slots)],
        in_specs=[whole(SMEM)] * 3 + [whole()] * 5,
        out_specs=[whole()] * 2,
    )(
        counts.reshape(1, 1),
        epsilon.reshape(1, -1),
        sigma.reshape(1, -1),
        positions.reshape(3, slots),
        velocities.reshape(3, slots),
        forces.reshape(3, slots),
        charges.reshape(1, slots),
        types.reshape(1, slots),
    )
    for step in range(STEPS):
        received = [lax.ppermute(record, names, table) for table in imports]
        parts = box_forces(record, received[0], received[1], received[2:])
        returned = [lax.ppermute(part, names, table) for part, table in zip(parts[1:], returns)]
        if step < STEPS - 1:
            record, half = pl.pallas_call(
                middle_kernel,
                out_shape=[shape(8, slots), shape(3, slots)],
                in_specs=[whole()] * 9,
                out_specs=[whole()] * 2,
            )(record, half, parts[0], *returned)
        else:
            outs = pl.pallas_call(
                last_kernel,
                out_shape=[shape(3, slots)] * 3,
                in_specs=[whole()] * 9,
                out_specs=[whole()] * 3,
            )(record, half, parts[0], *returned)
    return tuple(out.reshape(3, 1, 1, 1, slots) for out in outs)


def solution(mesh):
    boxes = P(None, "gx", "gy", "gz", None)
    slot = P("gx", "gy", "gz", None)
    in_specs = (boxes, boxes, boxes, slot, slot, P("gx", "gy", "gz"), P(), P())
    axes = tuple(mesh.shape[name] for name in ("gx", "gy", "gz"))
    return jax.shard_map(
        functools.partial(on_device, axes),
        mesh=mesh,
        in_specs=in_specs,
        out_specs=(boxes, boxes, boxes),
        check_vma=False,
    )
```

```python
import functools

import jax
import jax.numpy as jnp
from jax import lax
from jax.experimental import pallas as pl
from jax.experimental.pallas import tpu as pltpu
from jax.sharding import PartitionSpec as P

TILE = 128
STEPS = 2

COULOMB = 0.02
SOFTEN = 0.0225
CUTOFF = 0.81
TIME_STEP = 0.05
HALF_STEP = 0.025
REACH = 4.0 * (CUTOFF + SOFTEN)
SCALE = 1.0 / (4.0 * CUTOFF * CUTOFF)

F32 = jnp.float32
BF16 = jnp.bfloat16


def start_kernel(count, epsilon, sigma, pos, vel, frc, charge, kinds, record, half):
    live_tiles = count[0, 0, 0]
    slots = pos.shape[4]
    live = lax.broadcasted_iota(jnp.int32, (1, slots), 1) < live_tiles * TILE
    kind = kinds[0, 0]
    depth = jnp.zeros((1, slots), F32)
    size = jnp.zeros((1, slots), F32)
    for k in range(epsilon.shape[0]):
        same = kind == k
        depth = jnp.where(same, epsilon[k], depth)
        size = jnp.where(same, sigma[k], size)
    places = []
    for axis in range(3):
        velocity = vel[axis, 0, 0] + HALF_STEP * frc[axis, 0, 0]
        places.append(pos[axis, 0, 0] + TIME_STEP * velocity)
        half[axis : axis + 1, :] = velocity
    record[...] = jnp.concatenate(
        [
            *places,
            jnp.where(live, (2.0 * COULOMB) ** 0.5 * charge[0, 0], 0.0),
            jnp.where(live, 2.0 * jnp.sqrt(depth), 0.0),
            size,
            jnp.full((1, slots), live_tiles.astype(F32)),
            jnp.zeros((1, slots), F32),
        ],
        0,
    )


def split(value):
    high = value.astype(BF16).astype(F32)
    rest = value - high
    middle = rest.astype(BF16).astype(F32)
    return high, middle, rest - middle


def choose(row, *cases):
    value = 0.0
    for test, case in reversed(cases):
        value = jnp.where(test(row), case, value)
    return value


class Box:
    def __init__(self, record, shift):
        rows = record[...]
        row = lax.broadcasted_iota(jnp.int32, rows.shape, 0)
        self.row = row
        moved = [rows + (value - 0.5) if value != 0.5 else rows for value in shift]
        self.rows = choose(
            row,
            (lambda r: r == 0, moved[0]),
            (lambda r: r == 1, moved[1]),
            (lambda r: r == 2, moved[2]),
            (lambda r: r < 6, rows),
        )
        self.live = jnp.max(record[6:7, 0:TILE]).astype(jnp.int32)
        self.pieces = split(self.rows)
        square = self.rows * self.rows
        length = jnp.sum(jnp.where(row < 3, square, 0.0), axis=0, keepdims=True)
        self.length = jnp.broadcast_to(4.0 * length, rows.shape)
        size = jnp.sum(jnp.where(row == 5, square, 0.0), axis=0, keepdims=True)
        self.size = split(jnp.broadcast_to(size, rows.shape))

    def sided(self, pieces, first):
        start = 0 if first else 3
        return choose(
            self.row,
            (lambda r: r == start, pieces[0]),
            (lambda r: r == start + 1, pieces[1]),
            (lambda r: r == start + 2, pieces[2]),
            (lambda r: r < 6, 1.0),
        )

    def left(self):
        high, middle, low = self.pieces
        length = self.sided(split(self.length + 4.0 * SOFTEN), True)
        size = self.sided(self.size, True)
        return jnp.concatenate([high, high, high, middle, middle, low, length, size], 0)

    def right(self):
        row = self.row
        scale = choose(row, (lambda r: r < 3, -8.0), (lambda r: r == 5, 2.0), (lambda r: r < 5, 1.0))
        high, middle, low = [scale * piece for piece in self.pieces]
        zero = jnp.zeros_like(high)

        def stack(test, *others):
            h, m, l = [jnp.where(test, piece, 0.0) for piece in (high, middle, low)]
            return jnp.concatenate([h, m, l, h, m, h, *others], 0).astype(BF16)

        length = self.sided(split(self.length), False)
        size = self.sided(self.size, False)
        return [
            stack(row < 3, length, zero),
            stack(row == 3, zero, zero),
            stack(row == 4, zero, zero),
            stack(row == 5, zero, size),
        ]

    def moments(self):
        high, middle, low = self.pieces
        upper = choose(
            self.row,
            (lambda r: r < 3, high),
            (lambda r: r == 3, 1.0),
            (lambda r: r < 7, pltpu.roll(middle, 4, 0)),
        )
        return jnp.concatenate([upper, jnp.where(self.row < 3, low, 0.0)], 0).astype(BF16)


def cut(array, tile):
    return array[:, tile * TILE : (tile + 1) * TILE]


def pair_force(length, coulomb, lennard, contact):
    inverse = lax.rsqrt(length)
    inverse_sq = inverse * inverse
    screened = coulomb * jnp.exp(-(length * inverse)) * inverse
    ratio = contact * inverse_sq
    cubed = ratio * ratio * ratio
    depth = lennard * cubed
    less = cubed - 1.0
    slope = screened * inverse + inverse_sq * (screened + 6.0 * (depth * (cubed + less)))
    switch = jnp.maximum(REACH - length, 0.0)
    return switch * (switch * slope + 4.0 * (screened + depth * less))


def halves(force):
    high = force.astype(BF16)
    return high, (force - high.astype(F32)).astype(BF16)


def dot(a, b):
    return jnp.dot(a, b, preferred_element_type=F32)


def dot_rows(a, b):
    return lax.dot_general(a, b, (((1,), (1,)), ((), ())), preferred_element_type=F32)


def resolve(acc, rows):
    both = acc[0:8, :] + acc[8:16, :]
    turned = both + pltpu.roll(both, 4, 0)
    return (SCALE * (rows * both[3:4, :] - turned))[0:3, :]


def pair_blocks(lefts, rights, own, scratch):
    left, left_x, left_acc, right, right_x, right_acc, parts_a, parts_b, force_a, force_b = scratch
    tiles = lefts[0].rows.shape[1] // TILE

    start = jnp.int32(0)
    left_start = []
    for box in lefts:
        rows, dots = box.left(), box.moments()
        for tile in range(tiles):
            left[start + tile] = cut(rows, tile).T.astype(BF16)
            left_x[start + tile] = cut(dots, tile)
        left_start.append(start)
        start = start + box.live
    n_left = start
    first_own, first_above = left_start[1], left_start[2]

    start = jnp.int32(0)
    right_start = []
    for box in rights:
        features, dots = box.right(), box.moments()
        for tile in range(tiles):
            for number, feature in enumerate(features):
                right[start + tile, number] = cut(feature, tile)
            right_x[start + tile] = cut(dots, tile)
        right_start.append(start)
        start = start + box.live
    n_plate = start
    n_own = jnp.int32(0)
    if own is not None:
        n_own = own.live
        features, dots = own.right(), own.moments()
        for tile in range(tiles):

            @pl.when(tile < n_own)
            def _():
                spot = n_plate + n_own - 1 - tile
                for number, feature in enumerate(features):
                    right[spot, number] = cut(feature, tile)
                right_x[spot] = cut(dots, tile)

    empty = n_plate + n_own
    right[empty, 0] = cut(features[0], 0)
    for number in range(1, 4):
        right[empty, number] = jnp.zeros(right.shape[2:], BF16)
    right_x[empty] = cut(dots, 0)
    right_acc[...] = jnp.zeros(right_acc.shape, F32)

    def extent(t):
        if own is None:
            return n_plate
        own_part = jnp.where(t < first_above, n_own - 1 - (t - first_own), n_own)
        return n_plate + jnp.where(t < first_own, 0, own_part)

    def following(block):
        t, p = block
        step = 2 * p + 2 < extent(t)
        return jnp.where(step, t, jnp.minimum(t + 1, n_left)), jnp.where(step, p + 1, 0)

    def place(block):
        t, p = block
        inside = t < n_left
        one = jnp.where(inside, 2 * p, empty)
        two = jnp.where(inside & (2 * p + 1 < extent(t)), 2 * p + 1, empty)
        return jnp.where(inside, t, 0), one, two

    def spread(spots, parts):
        t, one, two = spots
        mine = left[t]
        for number in range(4):
            theirs = jnp.concatenate([right[one, number], right[two, number]], 1)
            parts[number] = dot(mine, theirs)

    def work(parts, split_force):
        high, low = halves(pair_force(*[parts[number] for number in range(4)]))
        split_force[0] = high
        split_force[1] = low

    def gather(spots, split_force):
        t, one, two = spots
        high, low = split_force[0], split_force[1]
        theirs_x = jnp.concatenate([right_x[one], right_x[two]], 1)
        mine_x = left_x[t]
        left_acc[t] = left_acc[t] + (dot_rows(theirs_x, high) + dot_rows(theirs_x, low))
        back = dot(mine_x, high) + dot(mine_x, low)
        right_acc[one] = right_acc[one] + back[:, :TILE]
        right_acc[two] = right_acc[two] + back[:, TILE:]

    def two_blocks(_, carry):
        block, before = carry
        spots = place(block)
        block = following(block)
        middle = place(block)
        block = following(block)
        spread(middle, parts_b)
        work(parts_a, force_a)
        gather(before, force_b)
        spread(place(block), parts_a)
        work(parts_b, force_b)
        gather(spots, force_a)
        return block, middle

    def pairs_of(count):
        return (count + 1) // 2

    if own is None:
        blocks = n_left * pairs_of(n_plate)
    else:
        blocks = first_own * pairs_of(n_plate) + (n_left - first_above) * pairs_of(n_plate + n_own)
        for tile in range(tiles):
            blocks = blocks + jnp.where(tile < n_own, pairs_of(n_plate + tile), 0)
    left_acc[...] = jnp.zeros(left_acc.shape, F32)
    force_b[...] = jnp.zeros(force_b.shape, BF16)
    zero = jnp.int32(0)
    first = (zero, zero)
    spread(place(first), parts_a)
    _, last = lax.fori_loop(0, pairs_of(blocks), two_blocks, (first, (zero, empty, empty)))
    gather(last, force_b)

    if own is not None:
        for tile in range(tiles):
            t = first_own + tile
            spot = jnp.maximum(n_plate + n_own - 1 - tile, 0)
            mine = left[t]
            force = pair_force(*[dot(mine, right[spot, number]) for number in range(4)])
            row = lax.broadcasted_iota(jnp.int32, force.shape, 0)
            col = lax.broadcasted_iota(jnp.int32, force.shape, 1)
            high, low = halves(jnp.where((row != col) & (tile < n_own), force, 0.0))
            theirs_x = right_x[spot]
            left_acc[t] = left_acc[t] + dot_rows(theirs_x, high) + dot_rows(theirs_x, low)

    def force(box, acc, tile):
        return jnp.where(tile < box.live, resolve(acc, cut(box.rows, tile)), 0.0)

    def left_force(number, tile):
        acc = left_acc[left_start[number] + tile]
        if own is not None and number == 1:
            acc = acc + right_acc[jnp.maximum(n_plate + n_own - 1 - tile, 0)]
        return force(lefts[number], acc, tile)

    def right_force(number, tile):
        return force(rights[number], right_acc[right_start[number] + tile], tile)

    return left_force, right_force


TOWER = ((0, -1, 0), (0, 0, 0), (0, 1, 0))
ROW = ((-1, 0, 1), (0, 0, 1), (1, 0, 1))


def lane(tile):
    return slice(tile * TILE, (tile + 1) * TILE)


def row_kernel(below, own, above, *refs):
    rights, out_row, outs, scratch = refs[:3], refs[3], refs[4:7], refs[7:]
    lefts = [Box(ref, shift) for ref, shift in zip((below, own, above), TOWER)]
    boxes = [Box(ref, shift) for ref, shift in zip(rights, ROW)]
    left_force, right_force = pair_blocks(lefts, boxes, None, scratch)
    for tile in range(own.shape[1] // TILE):
        for number in range(3):
            out_row[3 * number : 3 * number + 3, lane(tile)] = right_force(number, tile)
            outs[number][:, lane(tile)] = left_force(number, tile)


def rest_kernel(below, own, above, beside, add_below, add_own, add_above, *refs):
    out_beside, out_own, out_towers, scratch = refs[0], refs[1], refs[2:-10], refs[-10:]
    lefts = [Box(ref, shift) for ref, shift in zip((below, own, above), TOWER)]
    left_force, right_force = pair_blocks(lefts, [Box(beside, (1, 0, 0))], lefts[1], scratch)
    for tile in range(own.shape[1] // TILE):
        out_beside[:, lane(tile)] = right_force(0, tile)
        out_own[:, lane(tile)] = left_force(1, tile) + add_own[:, lane(tile)]
        low = left_force(0, tile) + add_below[:, lane(tile)]
        high = left_force(2, tile) + add_above[:, lane(tile)]
        if len(out_towers) == 1:
            out_towers[0][:, lane(tile)] = low + high
        else:
            out_towers[0][:, lane(tile)] = low
            out_towers[1][:, lane(tile)] = high


def merge_kernel(row, beside, own, to_low, to_high, total):
    to_low[...] = row[0:3, :]
    to_high[...] = row[6:9, :] + beside[...]
    total[...] = row[3:6, :] + own[...]


def add_up(parts):
    force = parts[0][...]
    for ref in parts[1:]:
        force = force + ref[...]
    return force


def middle_kernel(record, half, *refs):
    force = add_up(refs[:-2])
    new_record, new_half = refs[-2:]
    velocity = half[...] + HALF_STEP * force
    velocity = velocity + HALF_STEP * force
    new_half[...] = velocity
    new_record[3:8, :] = record[3:8, :]
    new_record[0:3, :] = record[0:3, :] + TIME_STEP * velocity


def last_kernel(record, half, *refs):
    force = add_up(refs[:-3])
    places, velocity, pushing = refs[-3:]
    final = half[...] + HALF_STEP * force
    for axis in range(3):
        places[axis, 0, 0] = record[axis : axis + 1, :]
        velocity[axis, 0, 0] = final[axis : axis + 1, :]
        pushing[axis, 0, 0] = force[axis : axis + 1, :]


VMEM = pltpu.VMEM
SMEM = pltpu.SMEM


def shape(*dims):
    return jax.ShapeDtypeStruct(dims, F32)


def whole(space=VMEM):
    return pl.BlockSpec(memory_space=space)


def call(kernel, outs, args, boxes=0, scalars=0):
    scratch, cost = [], None
    spaces = [SMEM] * scalars + [VMEM] * (len(args) - scalars)
    if boxes:
        slots = args[0].shape[1]
        tiles = slots // TILE
        right = boxes * tiles + 1
        scratch = [
            VMEM((3 * tiles, TILE, 64), BF16),
            VMEM((3 * tiles, 16, TILE), BF16),
            VMEM((3 * tiles, 16, TILE), F32),
            VMEM((right, 4, 64, TILE), BF16),
            VMEM((right, 16, TILE), BF16),
            VMEM((right, 16, TILE), F32),
            VMEM((4, TILE, 2 * TILE), F32),
            VMEM((4, TILE, 2 * TILE), F32),
            VMEM((2, TILE, 2 * TILE), BF16),
            VMEM((2, TILE, 2 * TILE), BF16),
        ]
        pairs = 3 * boxes * slots * slots
        cost = pl.CostEstimate(
            flops=50 * pairs, bytes_accessed=14 * 32 * slots, transcendentals=2 * pairs
        )
    return pl.pallas_call(
        kernel,
        out_shape=outs,
        in_specs=[whole(space) for space in spaces],
        out_specs=[whole()] * len(outs),
        scratch_shapes=scratch,
        compiler_params=pltpu.CompilerParams(vmem_limit_bytes=32 * 1024 * 1024),
        cost_estimate=cost,
    )(*args)


class Ring:
    def __init__(self, name, size):
        self.name, self.size = name, size

    def bring(self, value, offset):
        pairs = [((i + offset) % self.size, i) for i in range(self.size)]
        return lax.ppermute(value, self.name, pairs)

    def give(self, value, offset):
        return self.bring(value, -offset)


def step_forces(record, gx, gy, gz):
    slots = record.shape[1]
    one = shape(3, slots)
    up = gz.bring(record, 1)
    above = gy.bring(record, 1)
    below = above if gy.size == 2 else gy.bring(record, -1)
    beside = gx.bring(record, 1)
    row = (gx.bring(up, -1), up, gx.bring(up, 1))
    tower = (below, record, above)
    out_row, *adds = call(row_kernel, [shape(9, slots), one, one, one], (*tower, *row), 3)
    row_back = gz.give(out_row, 1)
    towers = 1 if gy.size == 2 else 2
    out_beside, out_own, *outs = call(
        rest_kernel, [one] * (2 + towers), (*tower, beside, *adds), 2
    )
    back = [gy.give(out, offset) for out, offset in zip(outs, (-1, 1))]
    to_low, to_high, own = call(merge_kernel, [one] * 3, (row_back, out_beside, out_own))
    return [own, gx.give(to_low, -1), gx.give(to_high, 1), *back]


def on_device(axes, positions, velocities, forces, charges, types, counts, epsilon, sigma):
    slots = positions.shape[-1]
    rings = [Ring(name, size) for name, size in zip(("gx", "gy", "gz"), axes)]
    args = (counts, epsilon, sigma, positions, velocities, forces, charges, types)
    record, half = call(start_kernel, [shape(8, slots), shape(3, slots)], args, scalars=3)
    for step in range(STEPS):
        parts = step_forces(record, *rings)
        if step < STEPS - 1:
            outs = [shape(8, slots), shape(3, slots)]
            record, half = call(middle_kernel, outs, (record, half, *parts))
        else:
            outs = call(last_kernel, [shape(*positions.shape)] * 3, (record, half, *parts))
    return tuple(outs)


def solution(mesh):
    boxes = P(None, "gx", "gy", "gz", None)
    slot = P("gx", "gy", "gz", None)
    in_specs = (boxes, boxes, boxes, slot, slot, P("gx", "gy", "gz"), P(), P())
    axes = tuple(mesh.shape[name] for name in ("gx", "gy", "gz"))
    return jax.shard_map(
        functools.partial(on_device, axes),
        mesh=mesh,
        in_specs=in_specs,
        out_specs=(boxes, boxes, boxes),
        check_vma=False,
    )
```

```python
import functools

import jax
import jax.numpy as jnp
from jax import lax
from jax.experimental import pallas as pl
from jax.experimental.pallas import tpu as pltpu
from jax.sharding import PartitionSpec as P

TILE = 128
STEPS = 2

COULOMB = 0.02
SOFTEN = 0.0225
CUTOFF = 0.81
TIME_STEP = 0.05
HALF_STEP = 0.025
REACH = 4.0 * (CUTOFF + SOFTEN)
LOG2_E = 1.4426950408889634
DEPTH = 64
SCALE = 1.0 / (4.0 * CUTOFF * CUTOFF)

F32 = jnp.float32
BF16 = jnp.bfloat16


def start_kernel(count, epsilon, sigma, pos, vel, frc, charge, kinds, record, half):
    live_tiles = count[0, 0, 0]
    slots = pos.shape[4]
    live = lax.broadcasted_iota(jnp.int32, (1, slots), 1) < live_tiles * TILE
    kind = kinds[0, 0]
    depth = jnp.zeros((1, slots), F32)
    size = jnp.zeros((1, slots), F32)
    for k in range(epsilon.shape[0]):
        same = kind == k
        depth = jnp.where(same, epsilon[k], depth)
        size = jnp.where(same, sigma[k], size)
    places = []
    for axis in range(3):
        velocity = vel[axis, 0, 0] + HALF_STEP * frc[axis, 0, 0]
        places.append(pos[axis, 0, 0] + TIME_STEP * velocity)
        half[axis : axis + 1, :] = velocity
    record[...] = jnp.concatenate(
        [
            *places,
            jnp.where(live, (2.0 * COULOMB) ** 0.5 * charge[0, 0], 0.0),
            jnp.where(live, 2.0 * jnp.sqrt(depth), 0.0),
            size,
            jnp.full((1, slots), live_tiles.astype(F32)),
            jnp.zeros((1, slots), F32),
        ],
        0,
    )


def split(value):
    high = value.astype(BF16).astype(F32)
    rest = value - high
    middle = rest.astype(BF16).astype(F32)
    return high, middle, rest - middle


def choose(row, *cases):
    value = 0.0
    for test, case in reversed(cases):
        value = jnp.where(test(row), case, value)
    return value


class Box:
    def __init__(self, record, shift):
        rows = record[...]
        row = lax.broadcasted_iota(jnp.int32, rows.shape, 0)
        self.row = row
        moved = [rows + (value - 0.5) if value != 0.5 else rows for value in shift]
        self.rows = choose(
            row,
            (lambda r: r == 0, moved[0]),
            (lambda r: r == 1, moved[1]),
            (lambda r: r == 2, moved[2]),
            (lambda r: r < 6, rows),
        )
        self.live = jnp.max(record[6:7, 0:TILE]).astype(jnp.int32)
        self.pieces = split(self.rows)
        square = self.rows * self.rows
        length = jnp.sum(jnp.where(row < 3, square, 0.0), axis=0, keepdims=True)
        self.length = jnp.broadcast_to(4.0 * length, rows.shape)
        size = jnp.sum(jnp.where(row == 5, square, 0.0), axis=0, keepdims=True)
        self.size = split(jnp.broadcast_to(size, rows.shape))

    def sided(self, pieces, first):
        start = 0 if first else 3
        return choose(
            self.row,
            (lambda r: r == start, pieces[0]),
            (lambda r: r == start + 1, pieces[1]),
            (lambda r: r == start + 2, pieces[2]),
            (lambda r: r < 6, 1.0),
        )

    def left(self):
        high, middle, low = self.pieces
        length = self.sided(split(self.length + 4.0 * SOFTEN), True)
        size = self.sided(self.size, True)
        return jnp.concatenate([high, high, high, middle, middle, low, length, size], 0)

    def right(self):
        row = self.row
        scale = choose(row, (lambda r: r < 3, -8.0), (lambda r: r == 5, 2.0), (lambda r: r < 5, 1.0))
        high, middle, low = [scale * piece for piece in self.pieces]
        zero = jnp.zeros_like(high)

        def stack(test, *others):
            h, m, l = [jnp.where(test, piece, 0.0) for piece in (high, middle, low)]
            return jnp.concatenate([h, m, l, h, m, h, *others], 0).astype(BF16)

        length = self.sided(split(self.length), False)
        size = self.sided(self.size, False)
        return [
            stack(row < 3, length, zero),
            stack(row == 3, zero, zero),
            stack(row == 4, zero, zero),
            stack(row == 5, zero, size),
        ]

    def moments(self):
        high, middle, low = self.pieces
        upper = choose(
            self.row,
            (lambda r: r < 3, high),
            (lambda r: r == 3, 1.0),
            (lambda r: r < 7, pltpu.roll(middle, 4, 0)),
        )
        return jnp.concatenate([upper, jnp.where(self.row < 3, low, 0.0)], 0).astype(BF16)


def cut(array, tile):
    return array[:, tile * TILE : (tile + 1) * TILE]


def pair_force(length, coulomb, lennard, contact):
    inverse = lax.rsqrt(length)
    inverse_sq = inverse * inverse
    screened = coulomb * jnp.exp2(length * (inverse * -LOG2_E)) * inverse
    ratio = contact * inverse_sq
    cubed = ratio * ratio * ratio
    depth = lennard * cubed
    less = cubed - 1.0
    slope = screened * inverse + inverse_sq * (screened + 6.0 * (depth * (cubed + less)))
    switch = jnp.maximum(REACH - length, 0.0)
    return switch * (switch * slope + 4.0 * (screened + depth * less))


def halves(force):
    high = force.astype(BF16)
    return high, (force - high.astype(F32)).astype(BF16)


def dot(a, b):
    return jnp.dot(a, b, preferred_element_type=F32)


def dot_rows(a, b):
    return lax.dot_general(a, b, (((1,), (1,)), ((), ())), preferred_element_type=F32)


def resolve(acc, rows):
    both = acc[0:8, :] + acc[8:16, :]
    turned = both + pltpu.roll(both, 4, 0)
    return (SCALE * (rows * both[3:4, :] - turned))[0:3, :]


def pack_left(lefts, left, left_x):
    start = jnp.int32(0)
    for box in lefts:
        rows, dots = box.left(), box.moments()
        for tile in range(dots.shape[1] // TILE):
            left[start + tile] = cut(rows, tile).T.astype(BF16)
            left_x[start + tile] = cut(dots, tile)
        start = start + box.live


def pack_right(rights, own, right, right_x):
    start = jnp.int32(0)
    for box in rights:
        features, dots = box.right(), box.moments()
        tiles = dots.shape[1] // TILE
        for tile in range(tiles):
            for number, feature in enumerate(features):
                right[start + tile, number] = cut(feature, tile)
            right_x[start + tile] = cut(dots, tile)
        start = start + box.live
    if own is not None:
        features, dots = own.right(), own.moments()
        first = start
        for tile in range(tiles):

            @pl.when(tile < own.live)
            def _():
                spot = first + own.live - 1 - tile
                for number, feature in enumerate(features):
                    right[spot, number] = cut(feature, tile)
                right_x[spot] = cut(dots, tile)

        start = start + own.live
    right[start, 0] = cut(features[0], 0)
    for number in range(1, 4):
        right[start, number] = jnp.zeros(right.shape[2:], BF16)
    right_x[start] = cut(dots, 0)


def starts(boxes):
    spots = [jnp.int32(0)]
    for box in boxes:
        spots.append(spots[-1] + box.live)
    return spots


def pair_blocks(lefts, rights, own, left, left_x, right, right_x, scratch):
    left_acc, right_acc, parts_a, parts_b, force_a, force_b = scratch
    tiles = lefts[0].rows.shape[1] // TILE
    left_start, right_start = starts(lefts), starts(rights)
    first_own, first_above, n_left = left_start[1:]
    n_plate = right_start[-1]
    n_own = jnp.int32(0) if own is None else own.live
    empty = n_plate + n_own
    right_acc[...] = jnp.zeros(right_acc.shape, F32)

    def extent(t):
        if own is None:
            return n_plate
        own_part = jnp.where(t < first_above, n_own - 1 - (t - first_own), n_own)
        return n_plate + jnp.where(t < first_own, 0, own_part)

    def following(block):
        t, p = block
        step = 2 * p + 2 < extent(t)
        return jnp.where(step, t, jnp.minimum(t + 1, n_left)), jnp.where(step, p + 1, 0)

    def place(block):
        t, p = block
        inside = t < n_left
        one = jnp.where(inside, 2 * p, empty)
        two = jnp.where(inside & (2 * p + 1 < extent(t)), 2 * p + 1, empty)
        return jnp.where(inside, t, 0), one, two

    def spread(spots, parts, number):
        t, one, two = spots
        theirs = jnp.concatenate([right[one, number], right[two, number]], 1)
        parts[number] = dot(left[t], theirs)

    def work(parts, split_force, number):
        rows = slice(number * TILE // 4, (number + 1) * TILE // 4)
        high, low = halves(pair_force(*[parts[kind, rows, :] for kind in range(4)]))
        split_force[0, rows, :] = high
        split_force[1, rows, :] = low

    def gather(spots, split_force, number):
        t, one, two = spots
        half = split_force[number % 2]
        if number < 2:
            theirs_x = jnp.concatenate([right_x[one], right_x[two]], 1)
            left_acc[t] = left_acc[t] + dot_rows(theirs_x, half)
        else:
            back = dot(left_x[t], half)
            right_acc[one] = right_acc[one] + back[:, :TILE]
            right_acc[two] = right_acc[two] + back[:, TILE:]

    def two_blocks(_, carry):
        block, before = carry
        spots = place(block)
        block = following(block)
        middle = place(block)
        block = following(block)
        later = place(block)
        for number in range(4):
            spread(middle, parts_b, number)
            work(parts_a, force_a, number)
            gather(before, force_b, number)
        for number in range(4):
            spread(later, parts_a, number)
            work(parts_b, force_b, number)
            gather(spots, force_a, number)
        return block, middle

    def pairs_of(count):
        return (count + 1) // 2

    if own is None:
        blocks = n_left * pairs_of(n_plate)
    else:
        blocks = first_own * pairs_of(n_plate) + (n_left - first_above) * pairs_of(n_plate + n_own)
        for tile in range(tiles):
            blocks = blocks + jnp.where(tile < n_own, pairs_of(n_plate + tile), 0)
    left_acc[...] = jnp.zeros(left_acc.shape, F32)
    force_b[...] = jnp.zeros(force_b.shape, BF16)
    zero = jnp.int32(0)
    first = (zero, zero)
    for number in range(4):
        spread(place(first), parts_a, number)
    _, last = lax.fori_loop(0, pairs_of(blocks), two_blocks, (first, (zero, empty, empty)))
    for number in range(4):
        gather(last, force_b, number)

    if own is not None:
        for tile in range(tiles):
            t = first_own + tile
            spot = jnp.maximum(n_plate + n_own - 1 - tile, 0)
            mine = left[t]
            force = pair_force(*[dot(mine, right[spot, number]) for number in range(4)])
            row = lax.broadcasted_iota(jnp.int32, force.shape, 0)
            col = lax.broadcasted_iota(jnp.int32, force.shape, 1)
            high, low = halves(jnp.where((row != col) & (tile < n_own), force, 0.0))
            theirs_x = right_x[spot]
            left_acc[t] = left_acc[t] + dot_rows(theirs_x, high) + dot_rows(theirs_x, low)

    def force(box, acc, tile):
        return jnp.where(tile < box.live, resolve(acc, cut(box.rows, tile)), 0.0)

    def left_force(number, tile):
        acc = left_acc[left_start[number] + tile]
        if own is not None and number == 1:
            acc = acc + right_acc[jnp.maximum(n_plate + n_own - 1 - tile, 0)]
        return force(lefts[number], acc, tile)

    def right_force(number, tile):
        return force(rights[number], right_acc[right_start[number] + tile], tile)

    return left_force, right_force


TOWER = ((0, -1, 0), (0, 0, 0), (0, 1, 0))
BESIDE = (1, 0, 0)
ROW = ((-1, 0, 1), (0, 0, 1), (1, 0, 1))


def lane(tile):
    return slice(tile * TILE, (tile + 1) * TILE)


def tower_boxes(below, own, above):
    return [Box(ref, move) for ref, move in zip((below, own, above), TOWER)]


def feature_kernel(below, own, above, beside, left, left_x, right, right_x):
    lefts = tower_boxes(below, own, above)
    pack_left(lefts, left, left_x)
    pack_right([Box(beside, BESIDE)], lefts[1], right, right_x)


def row_kernel(below, own, above, *refs):
    rights, (left, left_x), out_row, outs = refs[:3], refs[3:5], refs[5], refs[6:9]
    (right, right_x), scratch = refs[9:11], refs[11:]
    lefts = tower_boxes(below, own, above)
    boxes = [Box(ref, move) for ref, move in zip(rights, ROW)]
    pack_right(boxes, None, right, right_x)
    left_force, right_force = pair_blocks(
        lefts, boxes, None, left, left_x, right, right_x, scratch
    )
    for tile in range(own.shape[1] // TILE):
        for number in range(3):
            out_row[3 * number : 3 * number + 3, lane(tile)] = right_force(number, tile)
            outs[number][:, lane(tile)] = left_force(number, tile)


def rest_kernel(below, own, above, beside, *refs):
    features, (add_below, add_own, add_above) = refs[:4], refs[4:7]
    out_beside, out_own, out_towers, scratch = refs[7], refs[8], refs[9:-6], refs[-6:]
    lefts = tower_boxes(below, own, above)
    left_force, right_force = pair_blocks(
        lefts, [Box(beside, BESIDE)], lefts[1], *features, scratch
    )
    for tile in range(own.shape[1] // TILE):
        out_beside[:, lane(tile)] = right_force(0, tile)
        out_own[:, lane(tile)] = left_force(1, tile) + add_own[:, lane(tile)]
        low = left_force(0, tile) + add_below[:, lane(tile)]
        high = left_force(2, tile) + add_above[:, lane(tile)]
        if len(out_towers) == 1:
            out_towers[0][:, lane(tile)] = low + high
        else:
            out_towers[0][:, lane(tile)] = low
            out_towers[1][:, lane(tile)] = high


def merge_kernel(row, beside, own, to_low, to_high, total):
    to_low[...] = row[0:3, :]
    to_high[...] = row[6:9, :] + beside[...]
    total[...] = row[3:6, :] + own[...]


def add_up(parts):
    force = parts[0][...]
    for ref in parts[1:]:
        force = force + ref[...]
    return force


def middle_kernel(record, half, *refs):
    force = add_up(refs[:-2])
    new_record, new_half = refs[-2:]
    velocity = half[...] + HALF_STEP * force
    velocity = velocity + HALF_STEP * force
    new_half[...] = velocity
    new_record[3:8, :] = record[3:8, :]
    new_record[0:3, :] = record[0:3, :] + TIME_STEP * velocity


def last_kernel(record, half, *refs):
    force = add_up(refs[:-3])
    places, velocity, pushing = refs[-3:]
    final = half[...] + HALF_STEP * force
    for axis in range(3):
        places[axis, 0, 0] = record[axis : axis + 1, :]
        velocity[axis, 0, 0] = final[axis : axis + 1, :]
        pushing[axis, 0, 0] = force[axis : axis + 1, :]


VMEM = pltpu.VMEM
SMEM = pltpu.SMEM
LIMIT = 32 * 1024 * 1024


def shape(*dims):
    return jax.ShapeDtypeStruct(dims, F32)


def whole(space=VMEM):
    return pl.BlockSpec(memory_space=space)


def call(kernel, outs, args, pairs=0, scratch=()):
    cost = pl.CostEstimate(
        flops=50 * pairs, bytes_accessed=14 * 32 * args[0].shape[1], transcendentals=2 * pairs
    )
    return pl.pallas_call(
        kernel,
        out_shape=outs,
        in_specs=[whole()] * len(args),
        out_specs=[whole()] * len(outs),
        scratch_shapes=list(scratch),
        compiler_params=pltpu.CompilerParams(vmem_limit_bytes=LIMIT),
        cost_estimate=cost,
    )(*args)


class Ring:
    def __init__(self, name, size):
        self.name, self.size = name, size

    def bring(self, value, offset):
        pairs = [((i + offset) % self.size, i) for i in range(self.size)]
        return lax.ppermute(value, self.name, pairs)

    def give(self, value, offset):
        return self.bring(value, -offset)


def step_forces(record, gx, gy, gz):
    slots = record.shape[1]
    one = shape(3, slots)
    up = gz.bring(record, 1)
    above = gy.bring(record, 1)
    below = above if gy.size == 2 else gy.bring(record, -1)
    beside = gx.bring(record, 1)
    row = (gx.bring(up, -1), up, gx.bring(up, 1))
    tower = (below, record, above)
    tiles = slots // TILE

    def kept(*dims):
        return jax.ShapeDtypeStruct(dims, BF16)

    def sides(boxes):
        count = boxes * tiles + 1
        return kept(count, 4, DEPTH, TILE), kept(count, 16, TILE)

    def scratch(boxes):
        return (
            VMEM((3 * tiles, 16, TILE), F32),
            VMEM((boxes * tiles + 1, 16, TILE), F32),
            VMEM((4, TILE, 2 * TILE), F32),
            VMEM((4, TILE, 2 * TILE), F32),
            VMEM((2, TILE, 2 * TILE), BF16),
            VMEM((2, TILE, 2 * TILE), BF16),
        )

    outs = [kept(3 * tiles, TILE, DEPTH), kept(3 * tiles, 16, TILE), *sides(2)]
    left, left_x, *rest = call(feature_kernel, outs, (*tower, beside), pairs=slots * slots)
    out_row, *adds = call(
        row_kernel,
        [shape(9, slots), one, one, one],
        (*tower, *row, left, left_x),
        pairs=9 * slots * slots,
        scratch=[VMEM(side.shape, side.dtype) for side in sides(3)] + [*scratch(3)],
    )
    row_back = gz.give(out_row, 1)
    towers = 1 if gy.size == 2 else 2
    out_beside, out_own, *outs = call(
        rest_kernel,
        [one] * (2 + towers),
        (*tower, beside, left, left_x, *rest, *adds),
        pairs=5 * slots * slots,
        scratch=scratch(2),
    )
    back = [gy.give(out, offset) for out, offset in zip(outs, (-1, 1))]
    to_low, to_high, own = call(merge_kernel, [one] * 3, (row_back, out_beside, out_own))
    return [own, gx.give(to_low, -1), gx.give(to_high, 1), *back]


def on_device(axes, positions, velocities, forces, charges, types, counts, epsilon, sigma):
    slots = positions.shape[-1]
    rings = [Ring(name, size) for name, size in zip(("gx", "gy", "gz"), axes)]
    record, half = pl.pallas_call(
        start_kernel,
        out_shape=[shape(8, slots), shape(3, slots)],
        in_specs=[whole(SMEM)] * 3 + [whole()] * 5,
        out_specs=[whole()] * 2,
    )(counts, epsilon, sigma, positions, velocities, forces, charges, types)
    for step in range(STEPS):
        parts = step_forces(record, *rings)
        if step < STEPS - 1:
            outs = [shape(8, slots), shape(3, slots)]
            record, half = call(middle_kernel, outs, (record, half, *parts))
        else:
            outs = call(last_kernel, [shape(*positions.shape)] * 3, (record, half, *parts))
    return tuple(outs)


def solution(mesh):
    boxes = P(None, "gx", "gy", "gz", None)
    slot = P("gx", "gy", "gz", None)
    in_specs = (boxes, boxes, boxes, slot, slot, P("gx", "gy", "gz"), P(), P())
    axes = tuple(mesh.shape[name] for name in ("gx", "gy", "gz"))
    return jax.shard_map(
        functools.partial(on_device, axes),
        mesh=mesh,
        in_specs=in_specs,
        out_specs=(boxes, boxes, boxes),
        check_vma=False,
    )
```

```python
import functools

import jax
import jax.numpy as jnp
from jax import lax
from jax.experimental import pallas as pl
from jax.experimental.pallas import tpu as pltpu
from jax.sharding import PartitionSpec as P

TILE = 128
STEPS = 2

COULOMB = 0.02
SOFTEN = 0.0225
CUTOFF = 0.81
TIME_STEP = 0.05
HALF_STEP = 0.025
REACH = 4.0 * (CUTOFF + SOFTEN)
LOG2_E = 1.4426950408889634
DEPTH = 64
SCALE = 1.0 / (4.0 * CUTOFF * CUTOFF)

F32 = jnp.float32
BF16 = jnp.bfloat16


def start_kernel(count, epsilon, sigma, pos, vel, frc, charge, kinds, record, half):
    live_tiles = count[0, 0, 0]
    slots = pos.shape[4]
    live = lax.broadcasted_iota(jnp.int32, (1, slots), 1) < live_tiles * TILE
    kind = kinds[0, 0]
    depth = jnp.zeros((1, slots), F32)
    size = jnp.zeros((1, slots), F32)
    for k in range(epsilon.shape[0]):
        same = kind == k
        depth = jnp.where(same, epsilon[k], depth)
        size = jnp.where(same, sigma[k], size)
    places = []
    for axis in range(3):
        velocity = vel[axis, 0, 0] + HALF_STEP * frc[axis, 0, 0]
        places.append(pos[axis, 0, 0] + TIME_STEP * velocity)
        half[axis : axis + 1, :] = velocity
    record[...] = jnp.concatenate(
        [
            *places,
            jnp.where(live, (2.0 * COULOMB) ** 0.5 * charge[0, 0], 0.0),
            jnp.where(live, 4.0 * jnp.sqrt(depth), 0.0),
            size,
            jnp.full((1, slots), live_tiles.astype(F32)),
            jnp.zeros((1, slots), F32),
        ],
        0,
    )


def split(value):
    high = value.astype(BF16).astype(F32)
    rest = value - high
    middle = rest.astype(BF16).astype(F32)
    return high, middle, rest - middle


def choose(row, *cases):
    value = 0.0
    for test, case in reversed(cases):
        value = jnp.where(test(row), case, value)
    return value


class Box:
    def __init__(self, record, shift):
        rows = record[...]
        row = lax.broadcasted_iota(jnp.int32, rows.shape, 0)
        self.row = row
        moved = [rows + (value - 0.5) if value != 0.5 else rows for value in shift]
        self.rows = choose(
            row,
            (lambda r: r == 0, moved[0]),
            (lambda r: r == 1, moved[1]),
            (lambda r: r == 2, moved[2]),
            (lambda r: r < 6, rows),
        )
        self.live = jnp.max(record[6:7, 0:TILE]).astype(jnp.int32)
        self.pieces = split(self.rows)
        square = self.rows * self.rows
        length = jnp.sum(jnp.where(row < 3, square, 0.0), axis=0, keepdims=True)
        self.length = jnp.broadcast_to(4.0 * length, rows.shape)
        size = jnp.sum(jnp.where(row == 5, square, 0.0), axis=0, keepdims=True)
        self.size = split(jnp.broadcast_to(size, rows.shape))

    def sided(self, pieces, first):
        start = 0 if first else 3
        return choose(
            self.row,
            (lambda r: r == start, pieces[0]),
            (lambda r: r == start + 1, pieces[1]),
            (lambda r: r == start + 2, pieces[2]),
            (lambda r: r < 6, 1.0),
        )

    def left(self):
        high, middle, low = self.pieces
        length = self.sided(split(self.length + 4.0 * SOFTEN), True)
        size = self.sided(self.size, True)
        return jnp.concatenate([high, high, high, middle, middle, low, length, size], 0)

    def right(self):
        row = self.row
        scale = choose(row, (lambda r: r < 3, -8.0), (lambda r: r == 5, 2.0), (lambda r: r < 5, 1.0))
        high, middle, low = [scale * piece for piece in self.pieces]
        zero = jnp.zeros_like(high)

        def stack(test, *others):
            h, m, l = [jnp.where(test, piece, 0.0) for piece in (high, middle, low)]
            return jnp.concatenate([h, m, l, h, m, h, *others], 0).astype(BF16)

        length = self.sided(split(self.length), False)
        size = self.sided(self.size, False)
        return [
            stack(row < 3, length, zero),
            stack(row == 3, zero, zero),
            stack(row == 4, zero, zero),
            stack(row == 5, zero, size),
        ]

    def moments(self):
        high, middle, low = self.pieces
        upper = choose(
            self.row,
            (lambda r: r < 3, high),
            (lambda r: r == 3, 1.0),
            (lambda r: r < 7, pltpu.roll(middle, 4, 0)),
        )
        return jnp.concatenate([upper, jnp.where(self.row < 3, low, 0.0)], 0).astype(BF16)


def cut(array, tile):
    return array[:, tile * TILE : (tile + 1) * TILE]


def pair_force(length, coulomb, lennard, contact):
    inverse = lax.rsqrt(length)
    inverse_sq = inverse * inverse
    screened = coulomb * (jnp.exp2(length * (inverse * -LOG2_E)) * inverse)
    ratio = contact * inverse_sq
    cubed = ratio * ratio * ratio
    less = cubed - 1.0
    switch = jnp.maximum(REACH - length, 0.0)
    near = switch * inverse
    nearer = switch * inverse_sq
    charged = screened * (near + nearer + 4.0)
    touching = (lennard * cubed) * (less + (1.5 * nearer) * (cubed + less))
    return switch * (charged + touching)


def halves(force):
    high = force.astype(BF16)
    return high, (force - high.astype(F32)).astype(BF16)


def dot(a, b):
    return jnp.dot(a, b, preferred_element_type=F32)


def dot_rows(a, b):
    return lax.dot_general(a, b, (((1,), (1,)), ((), ())), preferred_element_type=F32)


def resolve(acc, rows):
    both = acc[0:8, :] + acc[8:16, :]
    turned = both + pltpu.roll(both, 4, 0)
    return (SCALE * (rows * both[3:4, :] - turned))[0:3, :]


def pack_left(lefts, left, left_x):
    start = jnp.int32(0)
    for box in lefts:
        rows, dots = box.left(), box.moments()
        for tile in range(dots.shape[1] // TILE):
            left[start + tile] = cut(rows, tile).T.astype(BF16)
            left_x[start + tile] = cut(dots, tile)
        start = start + box.live


def pack_right(rights, own, right, right_x):
    start = jnp.int32(0)
    for box in rights:
        features, dots = box.right(), box.moments()
        tiles = dots.shape[1] // TILE
        for tile in range(tiles):
            for number, feature in enumerate(features):
                right[start + tile, number] = cut(feature, tile)
            right_x[start + tile] = cut(dots, tile)
        start = start + box.live
    if own is not None:
        features, dots = own.right(), own.moments()
        first = start
        for tile in range(tiles):

            @pl.when(tile < own.live)
            def _():
                spot = first + own.live - 1 - tile
                for number, feature in enumerate(features):
                    right[spot, number] = cut(feature, tile)
                right_x[spot] = cut(dots, tile)

        start = start + own.live
    right[start, 0] = cut(features[0], 0)
    for number in range(1, 4):
        right[start, number] = jnp.zeros(right.shape[2:], BF16)
    right_x[start] = cut(dots, 0)


def starts(boxes):
    spots = [jnp.int32(0)]
    for box in boxes:
        spots.append(spots[-1] + box.live)
    return spots


def pair_blocks(lefts, rights, own, left, left_x, right, right_x, scratch):
    left_acc, right_acc, parts_a, parts_b, force_a, force_b = scratch
    tiles = lefts[0].rows.shape[1] // TILE
    left_start, right_start = starts(lefts), starts(rights)
    first_own, first_above, n_left = left_start[1:]
    n_plate = right_start[-1]
    n_own = jnp.int32(0) if own is None else own.live
    empty = n_plate + n_own
    right_acc[...] = jnp.zeros(right_acc.shape, F32)

    def extent(t):
        if own is None:
            return n_plate
        own_part = jnp.where(t < first_above, n_own - 1 - (t - first_own), n_own)
        return n_plate + jnp.where(t < first_own, 0, own_part)

    def following(block):
        t, p = block
        step = 2 * p + 2 < extent(t)
        return jnp.where(step, t, jnp.minimum(t + 1, n_left)), jnp.where(step, p + 1, 0)

    def place(block):
        t, p = block
        inside = t < n_left
        one = jnp.where(inside, 2 * p, empty)
        two = jnp.where(inside & (2 * p + 1 < extent(t)), 2 * p + 1, empty)
        return jnp.where(inside, t, 0), one, two

    def spread(spots, parts, number):
        t, one, two = spots
        theirs = jnp.concatenate([right[one, number], right[two, number]], 1)
        parts[number] = dot(left[t], theirs)

    def work(parts, split_force, number):
        rows = slice(number * TILE // 4, (number + 1) * TILE // 4)
        high, low = halves(pair_force(*[parts[kind, rows, :] for kind in range(4)]))
        split_force[0, rows, :] = high
        split_force[1, rows, :] = low

    def gather_left(spots, split_force):
        t, one, two = spots
        theirs_x = [right_x[one], right_x[two]]
        theirs_x = jnp.concatenate([*theirs_x, *theirs_x], 1)
        force = jnp.concatenate([split_force[0], split_force[1]], 1)
        left_acc[t] = left_acc[t] + dot_rows(theirs_x, force)

    def gather_right(spots, split_force):
        t, one, two = spots
        mine_x = jnp.concatenate([left_x[t], left_x[t]], 1)
        back = dot(mine_x, split_force[...].reshape(2 * TILE, 2 * TILE))
        right_acc[one] = right_acc[one] + back[:, :TILE]
        right_acc[two] = right_acc[two] + back[:, TILE:]

    def two_blocks(_, carry):
        block, before = carry
        spots = place(block)
        block = following(block)
        middle = place(block)
        block = following(block)
        later = place(block)
        for now, into, held, out, past, back in (
            (middle, parts_b, parts_a, force_a, before, force_b),
            (later, parts_a, parts_b, force_b, spots, force_a),
        ):
            for number in range(4):
                spread(now, into, number)
                work(held, out, number)
                if number == 0:
                    gather_left(past, back)
                if number == 2:
                    gather_right(past, back)
        return block, middle

    def pairs_of(count):
        return (count + 1) // 2

    if own is None:
        blocks = n_left * pairs_of(n_plate)
    else:
        blocks = first_own * pairs_of(n_plate) + (n_left - first_above) * pairs_of(n_plate + n_own)
        for tile in range(tiles):
            blocks = blocks + jnp.where(tile < n_own, pairs_of(n_plate + tile), 0)
    left_acc[...] = jnp.zeros(left_acc.shape, F32)
    force_b[...] = jnp.zeros(force_b.shape, BF16)
    zero = jnp.int32(0)
    first = (zero, zero)
    for number in range(4):
        spread(place(first), parts_a, number)
    _, last = lax.fori_loop(0, pairs_of(blocks), two_blocks, (first, (zero, empty, empty)))
    gather_left(last, force_b)
    gather_right(last, force_b)

    if own is not None:
        for tile in range(tiles):
            t = first_own + tile
            spot = jnp.maximum(n_plate + n_own - 1 - tile, 0)
            mine = left[t]
            force = pair_force(*[dot(mine, right[spot, number]) for number in range(4)])
            row = lax.broadcasted_iota(jnp.int32, force.shape, 0)
            col = lax.broadcasted_iota(jnp.int32, force.shape, 1)
            high, low = halves(jnp.where((row != col) & (tile < n_own), force, 0.0))
            theirs_x = right_x[spot]
            left_acc[t] = left_acc[t] + dot_rows(theirs_x, high) + dot_rows(theirs_x, low)

    def force(box, acc, tile):
        return jnp.where(tile < box.live, resolve(acc, cut(box.rows, tile)), 0.0)

    def left_force(number, tile):
        acc = left_acc[left_start[number] + tile]
        if own is not None and number == 1:
            acc = acc + right_acc[jnp.maximum(n_plate + n_own - 1 - tile, 0)]
        return force(lefts[number], acc, tile)

    def right_force(number, tile):
        return force(rights[number], right_acc[right_start[number] + tile], tile)

    return left_force, right_force


TOWER = ((0, -1, 0), (0, 0, 0), (0, 1, 0))
BESIDE = (1, 0, 0)
ROW = ((-1, 0, 1), (0, 0, 1), (1, 0, 1))


def lane(tile):
    return slice(tile * TILE, (tile + 1) * TILE)


def tower_boxes(below, own, above):
    return [Box(ref, move) for ref, move in zip((below, own, above), TOWER)]


def feature_kernel(below, own, above, beside, left, left_x, right, right_x):
    lefts = tower_boxes(below, own, above)
    pack_left(lefts, left, left_x)
    pack_right([Box(beside, BESIDE)], lefts[1], right, right_x)


def row_kernel(below, own, above, *refs):
    rights, (left, left_x), out_row, outs = refs[:3], refs[3:5], refs[5], refs[6:9]
    (right, right_x), scratch = refs[9:11], refs[11:]
    lefts = tower_boxes(below, own, above)
    boxes = [Box(ref, move) for ref, move in zip(rights, ROW)]
    pack_right(boxes, None, right, right_x)
    left_force, right_force = pair_blocks(
        lefts, boxes, None, left, left_x, right, right_x, scratch
    )
    for tile in range(own.shape[1] // TILE):
        for number in range(3):
            out_row[3 * number : 3 * number + 3, lane(tile)] = right_force(number, tile)
            outs[number][:, lane(tile)] = left_force(number, tile)


def rest_kernel(below, own, above, beside, *refs):
    features, (add_below, add_own, add_above) = refs[:4], refs[4:7]
    out_beside, out_own, out_towers, scratch = refs[7], refs[8], refs[9:-6], refs[-6:]
    lefts = tower_boxes(below, own, above)
    left_force, right_force = pair_blocks(
        lefts, [Box(beside, BESIDE)], lefts[1], *features, scratch
    )
    for tile in range(own.shape[1] // TILE):
        out_beside[:, lane(tile)] = right_force(0, tile)
        out_own[:, lane(tile)] = left_force(1, tile) + add_own[:, lane(tile)]
        low = left_force(0, tile) + add_below[:, lane(tile)]
        high = left_force(2, tile) + add_above[:, lane(tile)]
        if len(out_towers) == 1:
            out_towers[0][:, lane(tile)] = low + high
        else:
            out_towers[0][:, lane(tile)] = low
            out_towers[1][:, lane(tile)] = high


def merge_kernel(row, beside, own, to_low, to_high, total):
    to_low[...] = row[0:3, :]
    to_high[...] = row[6:9, :] + beside[...]
    total[...] = row[3:6, :] + own[...]


def add_up(parts):
    force = parts[0][...]
    for ref in parts[1:]:
        force = force + ref[...]
    return force


def middle_kernel(record, half, *refs):
    force = add_up(refs[:-2])
    new_record, new_half = refs[-2:]
    velocity = half[...] + HALF_STEP * force
    velocity = velocity + HALF_STEP * force
    new_half[...] = velocity
    new_record[3:8, :] = record[3:8, :]
    new_record[0:3, :] = record[0:3, :] + TIME_STEP * velocity


def last_kernel(record, half, *refs):
    force = add_up(refs[:-3])
    places, velocity, pushing = refs[-3:]
    final = half[...] + HALF_STEP * force
    for axis in range(3):
        places[axis, 0, 0] = record[axis : axis + 1, :]
        velocity[axis, 0, 0] = final[axis : axis + 1, :]
        pushing[axis, 0, 0] = force[axis : axis + 1, :]


VMEM = pltpu.VMEM
SMEM = pltpu.SMEM
LIMIT = 32 * 1024 * 1024


def shape(*dims):
    return jax.ShapeDtypeStruct(dims, F32)


def whole(space=VMEM):
    return pl.BlockSpec(memory_space=space)


def call(kernel, outs, args, pairs=0, scratch=()):
    cost = pl.CostEstimate(
        flops=50 * pairs, bytes_accessed=14 * 32 * args[0].shape[1], transcendentals=2 * pairs
    )
    return pl.pallas_call(
        kernel,
        out_shape=outs,
        in_specs=[whole()] * len(args),
        out_specs=[whole()] * len(outs),
        scratch_shapes=list(scratch),
        compiler_params=pltpu.CompilerParams(vmem_limit_bytes=LIMIT),
        cost_estimate=cost,
    )(*args)


class Ring:
    def __init__(self, name, size):
        self.name, self.size = name, size

    def bring(self, value, offset):
        pairs = [((i + offset) % self.size, i) for i in range(self.size)]
        return lax.ppermute(value, self.name, pairs)

    def give(self, value, offset):
        return self.bring(value, -offset)


def step_forces(record, gx, gy, gz):
    slots = record.shape[1]
    one = shape(3, slots)
    up = gz.bring(record, 1)
    above = gy.bring(record, 1)
    below = above if gy.size == 2 else gy.bring(record, -1)
    beside = gx.bring(record, 1)
    row = (gx.bring(up, -1), up, gx.bring(up, 1))
    tower = (below, record, above)
    tiles = slots // TILE

    def kept(*dims):
        return jax.ShapeDtypeStruct(dims, BF16)

    def sides(boxes):
        count = boxes * tiles + 1
        return kept(count, 4, DEPTH, TILE), kept(count, 16, TILE)

    def scratch(boxes):
        return (
            VMEM((3 * tiles, 16, TILE), F32),
            VMEM((boxes * tiles + 1, 16, TILE), F32),
            VMEM((4, TILE, 2 * TILE), F32),
            VMEM((4, TILE, 2 * TILE), F32),
            VMEM((2, TILE, 2 * TILE), BF16),
            VMEM((2, TILE, 2 * TILE), BF16),
        )

    outs = [kept(3 * tiles, TILE, DEPTH), kept(3 * tiles, 16, TILE), *sides(2)]
    left, left_x, *rest = call(feature_kernel, outs, (*tower, beside), pairs=slots * slots)
    out_row, *adds = call(
        row_kernel,
        [shape(9, slots), one, one, one],
        (*tower, *row, left, left_x),
        pairs=9 * slots * slots,
        scratch=[VMEM(side.shape, side.dtype) for side in sides(3)] + [*scratch(3)],
    )
    row_back = gz.give(out_row, 1)
    towers = 1 if gy.size == 2 else 2
    out_beside, out_own, *outs = call(
        rest_kernel,
        [one] * (2 + towers),
        (*tower, beside, left, left_x, *rest, *adds),
        pairs=5 * slots * slots,
        scratch=scratch(2),
    )
    back = [gy.give(out, offset) for out, offset in zip(outs, (-1, 1))]
    to_low, to_high, own = call(merge_kernel, [one] * 3, (row_back, out_beside, out_own))
    return [own, gx.give(to_low, -1), gx.give(to_high, 1), *back]


def on_device(axes, positions, velocities, forces, charges, types, counts, epsilon, sigma):
    slots = positions.shape[-1]
    rings = [Ring(name, size) for name, size in zip(("gx", "gy", "gz"), axes)]
    record, half = pl.pallas_call(
        start_kernel,
        out_shape=[shape(8, slots), shape(3, slots)],
        in_specs=[whole(SMEM)] * 3 + [whole()] * 5,
        out_specs=[whole()] * 2,
    )(counts, epsilon, sigma, positions, velocities, forces, charges, types)
    for step in range(STEPS):
        parts = step_forces(record, *rings)
        if step < STEPS - 1:
            outs = [shape(8, slots), shape(3, slots)]
            record, half = call(middle_kernel, outs, (record, half, *parts))
        else:
            outs = call(last_kernel, [shape(*positions.shape)] * 3, (record, half, *parts))
    return tuple(outs)


def solution(mesh):
    boxes = P(None, "gx", "gy", "gz", None)
    slot = P("gx", "gy", "gz", None)
    in_specs = (boxes, boxes, boxes, slot, slot, P("gx", "gy", "gz"), P(), P())
    axes = tuple(mesh.shape[name] for name in ("gx", "gy", "gz"))
    return jax.shard_map(
        functools.partial(on_device, axes),
        mesh=mesh,
        in_specs=in_specs,
        out_specs=(boxes, boxes, boxes),
        check_vma=False,
    )
```

```python
import functools

import jax
import jax.numpy as jnp
from jax import lax
from jax.experimental import pallas as pl
from jax.experimental.pallas import tpu as pltpu
from jax.sharding import PartitionSpec as P

TILE = 128
STEPS = 2

COULOMB = 0.02
SOFTEN = 0.0225
CUTOFF = 0.81
TIME_STEP = 0.05
HALF_STEP = 0.025
REACH = 4.0 * (CUTOFF + SOFTEN)
LOG2_E = 1.4426950408889634
DEPTH = 32
SCALE = 1.0 / (4.0 * CUTOFF * CUTOFF)

F32 = jnp.float32
BF16 = jnp.bfloat16


def start_kernel(count, epsilon, sigma, pos, vel, frc, charge, kinds, record, half):
    live_tiles = count[0, 0, 0]
    slots = pos.shape[4]
    live = lax.broadcasted_iota(jnp.int32, (1, slots), 1) < live_tiles * TILE
    kind = kinds[0, 0]
    depth = jnp.zeros((1, slots), F32)
    size = jnp.zeros((1, slots), F32)
    for k in range(epsilon.shape[0]):
        same = kind == k
        depth = jnp.where(same, epsilon[k], depth)
        size = jnp.where(same, sigma[k], size)
    places = []
    for axis in range(3):
        velocity = vel[axis, 0, 0] + HALF_STEP * frc[axis, 0, 0]
        places.append(pos[axis, 0, 0] + TIME_STEP * velocity)
        half[axis : axis + 1, :] = velocity
    record[...] = jnp.concatenate(
        [
            *places,
            jnp.where(live, (2.0 * COULOMB) ** 0.5 * charge[0, 0], 0.0),
            jnp.where(live, 4.0 * jnp.sqrt(depth), 0.0),
            size,
            jnp.full((1, slots), live_tiles.astype(F32)),
            jnp.zeros((1, slots), F32),
        ],
        0,
    )


def split(value):
    high = value.astype(BF16).astype(F32)
    rest = value - high
    middle = rest.astype(BF16).astype(F32)
    return high, middle, rest - middle


def choose(row, *cases):
    value = 0.0
    for test, case in reversed(cases):
        value = jnp.where(test(row), case, value)
    return value


class Box:
    def __init__(self, record, shift):
        rows = record[...]
        row = lax.broadcasted_iota(jnp.int32, rows.shape, 0)
        self.row = row
        moved = [rows + (value - 0.5) if value != 0.5 else rows for value in shift]
        self.rows = choose(
            row,
            (lambda r: r == 0, moved[0]),
            (lambda r: r == 1, moved[1]),
            (lambda r: r == 2, moved[2]),
            (lambda r: r < 6, rows),
        )
        self.live = jnp.max(record[6:7, 0:TILE]).astype(jnp.int32)
        self.pieces = split(self.rows)
        square = jnp.where(row < 3, self.rows * self.rows, 0.0)
        length = jnp.sum(square, axis=0, keepdims=True)
        self.length = jnp.broadcast_to(4.0 * length, rows.shape)

    def sided(self, pieces, first):
        start = 0 if first else 3
        return choose(
            self.row,
            (lambda r: r == start, pieces[0]),
            (lambda r: r == start + 1, pieces[1]),
            (lambda r: r == start + 2, pieces[2]),
            (lambda r: r < 6, 1.0),
        )

    def pair(self, first, second):
        return choose(
            self.row, (lambda r: r < 3, first), (lambda r: r < 6, pltpu.roll(second, 3, 0))
        )

    def left(self):
        high, middle, low = self.pieces
        length = self.sided(split(self.length + 4.0 * SOFTEN), True)
        pairs = [self.pair(high, high), self.pair(high, middle), self.pair(middle, low)]
        return jnp.concatenate([*pairs, length], 0)

    def right(self):
        high, middle, low = [-8.0 * piece for piece in self.pieces]
        length = self.sided(split(self.length), False)
        pairs = [self.pair(high, middle), self.pair(low, high), self.pair(middle, high)]
        return jnp.concatenate([*pairs, length], 0).astype(BF16)

    def moments(self):
        high, middle, low = self.pieces
        upper = choose(
            self.row,
            (lambda r: r < 3, high),
            (lambda r: r == 3, 1.0),
            (lambda r: r < 7, pltpu.roll(middle, 4, 0)),
        )
        return jnp.concatenate([upper, jnp.where(self.row < 3, low, 0.0)], 0).astype(BF16)


def cut(array, tile):
    return array[:, tile * TILE : (tile + 1) * TILE]


def pair_force(length, mine, theirs):
    inverse = lax.rsqrt(length)
    inverse_sq = inverse * inverse
    screened = (mine[0] * theirs[0]) * (jnp.exp2(length * (inverse * -LOG2_E)) * inverse)
    root = (mine[2] + theirs[2]) * inverse
    ratio = root * root
    cubed = ratio * ratio * ratio
    less = cubed - 1.0
    switch = jnp.maximum(REACH - length, 0.0)
    near = switch * inverse
    nearer = switch * inverse_sq
    charged = screened * (near + nearer + 4.0)
    touching = (mine[1] * theirs[1] * cubed) * (less + (1.5 * nearer) * (cubed + less))
    return switch * (charged + touching)


def halves(force):
    high = force.astype(BF16)
    return high, (force - high.astype(F32)).astype(BF16)


def dot(a, b):
    return jnp.dot(a, b, preferred_element_type=F32)


def dot_rows(a, b):
    return lax.dot_general(a, b, (((1,), (1,)), ((), ())), preferred_element_type=F32)


def resolve(acc, rows):
    both = acc[0:8, :] + acc[8:16, :]
    turned = both + pltpu.roll(both, 4, 0)
    return (SCALE * (rows * both[3:4, :] - turned))[0:3, :]


def pack_left(lefts, left, left_x, left_traits):
    start = jnp.int32(0)
    for box in lefts:
        rows, dots = jnp.concatenate([box.left(), box.rows], 0), box.moments()
        for tile in range(dots.shape[1] // TILE):
            columns = cut(rows, tile).T
            left[start + tile] = columns[:, :DEPTH].astype(BF16)
            left_x[start + tile] = cut(dots, tile)
            for number in range(3):
                column = columns[:, DEPTH + 3 + number : DEPTH + 4 + number]
                left_traits[start + tile, number] = jnp.broadcast_to(column, (TILE, TILE))
        start = start + box.live


def pack_right(rights, own, right, right_x, right_traits):
    def put(spot, box, features, dots, tile):
        right[spot] = cut(features, tile)
        right_x[spot] = cut(dots, tile)
        right_traits[spot] = cut(box.rows, tile)

    start = jnp.int32(0)
    for box in rights:
        features, dots = box.right(), box.moments()
        tiles = dots.shape[1] // TILE
        for tile in range(tiles):
            put(start + tile, box, features, dots, tile)
        start = start + box.live
    if own is not None:
        box, features, dots = own, own.right(), own.moments()
        first = start
        for tile in range(tiles):

            @pl.when(tile < own.live)
            def _():
                put(first + own.live - 1 - tile, own, features, dots, tile)

        start = start + own.live
    put(start, box, features, dots, 0)
    right_traits[start] = jnp.zeros(right_traits.shape[1:], F32)


def starts(boxes):
    spots = [jnp.int32(0)]
    for box in boxes:
        spots.append(spots[-1] + box.live)
    return spots


def pair_blocks(lefts, rights, own, left_side, right_side, scratch):
    left, left_x, left_traits = left_side
    right, right_x, right_traits = right_side
    left_acc, right_acc, parts_a, parts_b, force_a, force_b = scratch
    tiles = lefts[0].rows.shape[1] // TILE
    left_start, right_start = starts(lefts), starts(rights)
    first_own, first_above, n_left = left_start[1:]
    n_plate = right_start[-1]
    n_own = jnp.int32(0) if own is None else own.live
    empty = n_plate + n_own
    right_acc[...] = jnp.zeros(right_acc.shape, F32)

    def extent(t):
        if own is None:
            return n_plate
        own_part = jnp.where(t < first_above, n_own - 1 - (t - first_own), n_own)
        return n_plate + jnp.where(t < first_own, 0, own_part)

    def following(block):
        t, p = block
        step = 2 * p + 2 < extent(t)
        return jnp.where(step, t, jnp.minimum(t + 1, n_left)), jnp.where(step, p + 1, 0)

    def place(block):
        t, p = block
        inside = t < n_left
        one = jnp.where(inside, 2 * p, empty)
        two = jnp.where(inside & (2 * p + 1 < extent(t)), 2 * p + 1, empty)
        return jnp.where(inside, t, 0), one, two

    def spread(spots, parts):
        t, one, two = spots
        parts[...] = dot(left[t], jnp.concatenate([right[one], right[two]], 1))

    def work(spots, parts, split_force, number):
        t, one, two = spots
        rows = slice(number * TILE // 4, (number + 1) * TILE // 4)
        mine = [left_traits[t, trait, rows, :] for trait in range(3)]
        for lanes, spot in ((slice(0, TILE), one), (slice(TILE, 2 * TILE), two)):
            theirs = [right_traits[spot, 3 + trait : 4 + trait, :] for trait in range(3)]
            high, low = halves(pair_force(parts[rows, lanes], mine, theirs))
            split_force[0, rows, lanes] = high
            split_force[1, rows, lanes] = low

    def gather_left(spots, split_force):
        t, one, two = spots
        theirs_x = [right_x[one], right_x[two]]
        theirs_x = jnp.concatenate([*theirs_x, *theirs_x], 1)
        force = jnp.concatenate([split_force[0], split_force[1]], 1)
        left_acc[t] = left_acc[t] + dot_rows(theirs_x, force)

    def gather_right(spots, split_force):
        t, one, two = spots
        mine_x = jnp.concatenate([left_x[t], left_x[t]], 1)
        back = dot(mine_x, split_force[...].reshape(2 * TILE, 2 * TILE))
        right_acc[one] = right_acc[one] + back[:, :TILE]
        right_acc[two] = right_acc[two] + back[:, TILE:]

    def two_blocks(_, carry):
        block, before = carry
        spots = place(block)
        block = following(block)
        middle = place(block)
        block = following(block)
        later = place(block)
        for now, into, held, parts, out, past, back in (
            (middle, parts_b, spots, parts_a, force_a, before, force_b),
            (later, parts_a, middle, parts_b, force_b, spots, force_a),
        ):
            spread(now, into)
            for number in range(4):
                work(held, parts, out, number)
                if number == 0:
                    gather_left(past, back)
                if number == 2:
                    gather_right(past, back)
        return block, middle

    def pairs_of(count):
        return (count + 1) // 2

    if own is None:
        blocks = n_left * pairs_of(n_plate)
    else:
        blocks = first_own * pairs_of(n_plate) + (n_left - first_above) * pairs_of(n_plate + n_own)
        for tile in range(tiles):
            blocks = blocks + jnp.where(tile < n_own, pairs_of(n_plate + tile), 0)
    left_acc[...] = jnp.zeros(left_acc.shape, F32)
    force_b[...] = jnp.zeros(force_b.shape, BF16)
    zero = jnp.int32(0)
    first = (zero, zero)
    spread(place(first), parts_a)
    _, last = lax.fori_loop(0, pairs_of(blocks), two_blocks, (first, (zero, empty, empty)))
    gather_left(last, force_b)
    gather_right(last, force_b)

    if own is not None:
        for tile in range(tiles):
            t = first_own + tile
            spot = jnp.maximum(n_plate + n_own - 1 - tile, 0)
            mine = left[t]
            columns = [left_traits[t, trait] for trait in range(3)]
            theirs = [right_traits[spot, 3 + trait : 4 + trait, :] for trait in range(3)]
            force = pair_force(dot(mine, right[spot]), columns, theirs)
            row = lax.broadcasted_iota(jnp.int32, force.shape, 0)
            col = lax.broadcasted_iota(jnp.int32, force.shape, 1)
            high, low = halves(jnp.where((row != col) & (tile < n_own), force, 0.0))
            theirs_x = right_x[spot]
            left_acc[t] = left_acc[t] + dot_rows(theirs_x, high) + dot_rows(theirs_x, low)

    def force(box, acc, tile):
        return jnp.where(tile < box.live, resolve(acc, cut(box.rows, tile)), 0.0)

    def left_force(number, tile):
        acc = left_acc[left_start[number] + tile]
        if own is not None and number == 1:
            acc = acc + right_acc[jnp.maximum(n_plate + n_own - 1 - tile, 0)]
        return force(lefts[number], acc, tile)

    def right_force(number, tile):
        return force(rights[number], right_acc[right_start[number] + tile], tile)

    return left_force, right_force


TOWER = ((0, -1, 0), (0, 0, 0), (0, 1, 0))
BESIDE = (1, 0, 0)
ROW = ((-1, 0, 1), (0, 0, 1), (1, 0, 1))


def lane(tile):
    return slice(tile * TILE, (tile + 1) * TILE)


def tower_boxes(below, own, above):
    return [Box(ref, move) for ref, move in zip((below, own, above), TOWER)]


def feature_kernel(below, own, above, beside, *sides):
    lefts = tower_boxes(below, own, above)
    pack_left(lefts, *sides[:3])
    pack_right([Box(beside, BESIDE)], lefts[1], *sides[3:])


def row_kernel(below, own, above, *refs):
    rights, left_side, out_row, outs = refs[:3], refs[3:6], refs[6], refs[7:10]
    right_side, scratch = refs[10:13], refs[13:]
    lefts = tower_boxes(below, own, above)
    boxes = [Box(ref, move) for ref, move in zip(rights, ROW)]
    pack_right(boxes, None, *right_side)
    left_force, right_force = pair_blocks(lefts, boxes, None, left_side, right_side, scratch)
    for tile in range(own.shape[1] // TILE):
        for number in range(3):
            out_row[3 * number : 3 * number + 3, lane(tile)] = right_force(number, tile)
            outs[number][:, lane(tile)] = left_force(number, tile)


def rest_kernel(below, own, above, beside, *refs):
    left_side, right_side, (add_below, add_own, add_above) = refs[:3], refs[3:6], refs[6:9]
    out_beside, out_own, out_towers, scratch = refs[9], refs[10], refs[11:-6], refs[-6:]
    lefts = tower_boxes(below, own, above)
    left_force, right_force = pair_blocks(
        lefts, [Box(beside, BESIDE)], lefts[1], left_side, right_side, scratch
    )
    for tile in range(own.shape[1] // TILE):
        out_beside[:, lane(tile)] = right_force(0, tile)
        out_own[:, lane(tile)] = left_force(1, tile) + add_own[:, lane(tile)]
        low = left_force(0, tile) + add_below[:, lane(tile)]
        high = left_force(2, tile) + add_above[:, lane(tile)]
        if len(out_towers) == 1:
            out_towers[0][:, lane(tile)] = low + high
        else:
            out_towers[0][:, lane(tile)] = low
            out_towers[1][:, lane(tile)] = high


def merge_kernel(row, beside, own, to_low, to_high, total):
    to_low[...] = row[0:3, :]
    to_high[...] = row[6:9, :] + beside[...]
    total[...] = row[3:6, :] + own[...]


def add_up(parts):
    force = parts[0][...]
    for ref in parts[1:]:
        force = force + ref[...]
    return force


def middle_kernel(record, half, *refs):
    force = add_up(refs[:-2])
    new_record, new_half = refs[-2:]
    velocity = half[...] + HALF_STEP * force
    velocity = velocity + HALF_STEP * force
    new_half[...] = velocity
    new_record[3:8, :] = record[3:8, :]
    new_record[0:3, :] = record[0:3, :] + TIME_STEP * velocity


def last_kernel(record, half, *refs):
    force = add_up(refs[:-3])
    places, velocity, pushing = refs[-3:]
    final = half[...] + HALF_STEP * force
    for axis in range(3):
        places[axis, 0, 0] = record[axis : axis + 1, :]
        velocity[axis, 0, 0] = final[axis : axis + 1, :]
        pushing[axis, 0, 0] = force[axis : axis + 1, :]


VMEM = pltpu.VMEM
SMEM = pltpu.SMEM
LIMIT = 32 * 1024 * 1024


def shape(*dims):
    return jax.ShapeDtypeStruct(dims, F32)


def whole(space=VMEM):
    return pl.BlockSpec(memory_space=space)


def call(kernel, outs, args, pairs=0, scratch=()):
    cost = pl.CostEstimate(
        flops=50 * pairs, bytes_accessed=14 * 32 * args[0].shape[1], transcendentals=2 * pairs
    )
    return pl.pallas_call(
        kernel,
        out_shape=outs,
        in_specs=[whole()] * len(args),
        out_specs=[whole()] * len(outs),
        scratch_shapes=list(scratch),
        compiler_params=pltpu.CompilerParams(vmem_limit_bytes=LIMIT),
        cost_estimate=cost,
    )(*args)


class Ring:
    def __init__(self, name, size):
        self.name, self.size = name, size

    def bring(self, value, offset):
        pairs = [((i + offset) % self.size, i) for i in range(self.size)]
        return lax.ppermute(value, self.name, pairs)

    def give(self, value, offset):
        return self.bring(value, -offset)


def step_forces(record, gx, gy, gz):
    slots = record.shape[1]
    one = shape(3, slots)
    up = gz.bring(record, 1)
    above = gy.bring(record, 1)
    below = above if gy.size == 2 else gy.bring(record, -1)
    beside = gx.bring(record, 1)
    row = (gx.bring(up, -1), up, gx.bring(up, 1))
    tower = (below, record, above)
    tiles = slots // TILE

    def kept(*dims):
        return jax.ShapeDtypeStruct(dims, BF16)

    def sides(boxes):
        count = boxes * tiles + 1
        return kept(count, DEPTH, TILE), kept(count, 16, TILE), shape(count, 8, TILE)

    def scratch(boxes):
        return (
            VMEM((3 * tiles, 16, TILE), F32),
            VMEM((boxes * tiles + 1, 16, TILE), F32),
            VMEM((TILE, 2 * TILE), F32),
            VMEM((TILE, 2 * TILE), F32),
            VMEM((2, TILE, 2 * TILE), BF16),
            VMEM((2, TILE, 2 * TILE), BF16),
        )

    outs = [kept(3 * tiles, TILE, DEPTH), kept(3 * tiles, 16, TILE)]
    outs += [shape(3 * tiles, 3, TILE, TILE), *sides(2)]
    features = call(feature_kernel, outs, (*tower, beside), pairs=slots * slots)
    out_row, *adds = call(
        row_kernel,
        [shape(9, slots), one, one, one],
        (*tower, *row, *features[:3]),
        pairs=9 * slots * slots,
        scratch=[VMEM(side.shape, side.dtype) for side in sides(3)] + [*scratch(3)],
    )
    row_back = gz.give(out_row, 1)
    towers = 1 if gy.size == 2 else 2
    out_beside, out_own, *outs = call(
        rest_kernel,
        [one] * (2 + towers),
        (*tower, beside, *features, *adds),
        pairs=5 * slots * slots,
        scratch=scratch(2),
    )
    back = [gy.give(out, offset) for out, offset in zip(outs, (-1, 1))]
    to_low, to_high, own = call(merge_kernel, [one] * 3, (row_back, out_beside, out_own))
    return [own, gx.give(to_low, -1), gx.give(to_high, 1), *back]


def on_device(axes, positions, velocities, forces, charges, types, counts, epsilon, sigma):
    slots = positions.shape[-1]
    rings = [Ring(name, size) for name, size in zip(("gx", "gy", "gz"), axes)]
    record, half = pl.pallas_call(
        start_kernel,
        out_shape=[shape(8, slots), shape(3, slots)],
        in_specs=[whole(SMEM)] * 3 + [whole()] * 5,
        out_specs=[whole()] * 2,
    )(counts, epsilon, sigma, positions, velocities, forces, charges, types)
    for step in range(STEPS):
        parts = step_forces(record, *rings)
        if step < STEPS - 1:
            outs = [shape(8, slots), shape(3, slots)]
            record, half = call(middle_kernel, outs, (record, half, *parts))
        else:
            outs = call(last_kernel, [shape(*positions.shape)] * 3, (record, half, *parts))
    return tuple(outs)


def solution(mesh):
    boxes = P(None, "gx", "gy", "gz", None)
    slot = P("gx", "gy", "gz", None)
    in_specs = (boxes, boxes, boxes, slot, slot, P("gx", "gy", "gz"), P(), P())
    axes = tuple(mesh.shape[name] for name in ("gx", "gy", "gz"))
    return jax.shard_map(
        functools.partial(on_device, axes),
        mesh=mesh,
        in_specs=in_specs,
        out_specs=(boxes, boxes, boxes),
        check_vma=False,
    )
```

```python
import functools

import jax
import jax.numpy as jnp
from jax import lax
from jax.experimental import pallas as pl
from jax.experimental.pallas import tpu as pltpu
from jax.sharding import PartitionSpec as P

TILE = 128
STEPS = 2

COULOMB = 0.02
SOFTEN = 0.0225
CUTOFF = 0.81
TIME_STEP = 0.05
HALF_STEP = 0.025
REACH = 4.0 * (CUTOFF + SOFTEN)
LOG2_E = 1.4426950408889634
DEPTH = 32
SCALE = 1.0 / (4.0 * CUTOFF * CUTOFF)

F32 = jnp.float32
BF16 = jnp.bfloat16


def start_kernel(count, epsilon, sigma, pos, vel, frc, charge, kinds, record, half):
    live_tiles = count[0, 0, 0]
    slots = pos.shape[4]
    live = lax.broadcasted_iota(jnp.int32, (1, slots), 1) < live_tiles * TILE
    kind = kinds[0, 0]
    depth = jnp.zeros((1, slots), F32)
    size = jnp.zeros((1, slots), F32)
    for k in range(epsilon.shape[0]):
        same = kind == k
        depth = jnp.where(same, epsilon[k], depth)
        size = jnp.where(same, sigma[k], size)
    places = []
    for axis in range(3):
        velocity = vel[axis, 0, 0] + HALF_STEP * frc[axis, 0, 0]
        places.append(pos[axis, 0, 0] + TIME_STEP * velocity)
        half[axis : axis + 1, :] = velocity
    record[...] = jnp.concatenate(
        [
            *places,
            jnp.where(live, (2.0 * COULOMB) ** 0.5 * charge[0, 0], 0.0),
            jnp.where(live, 4.0 * jnp.sqrt(depth), 0.0),
            size,
            jnp.full((1, slots), live_tiles.astype(F32)),
            jnp.zeros((1, slots), F32),
        ],
        0,
    )


def split(value):
    high = value.astype(BF16).astype(F32)
    rest = value - high
    middle = rest.astype(BF16).astype(F32)
    return high, middle, rest - middle


def choose(row, *cases):
    value = 0.0
    for test, case in reversed(cases):
        value = jnp.where(test(row), case, value)
    return value


class Box:
    def __init__(self, record, shift):
        rows = record[...]
        row = lax.broadcasted_iota(jnp.int32, rows.shape, 0)
        self.row = row
        moved = [rows + (value - 0.5) if value != 0.5 else rows for value in shift]
        self.rows = choose(
            row,
            (lambda r: r == 0, moved[0]),
            (lambda r: r == 1, moved[1]),
            (lambda r: r == 2, moved[2]),
            (lambda r: r < 6, rows),
        )
        self.live = jnp.max(record[6:7, 0:TILE]).astype(jnp.int32)
        self.pieces = split(self.rows)
        square = jnp.where(row < 3, self.rows * self.rows, 0.0)
        length = jnp.sum(square, axis=0, keepdims=True)
        self.length = jnp.broadcast_to(4.0 * length, rows.shape)

    def sided(self, pieces, first):
        start = 0 if first else 3
        return choose(
            self.row,
            (lambda r: r == start, pieces[0]),
            (lambda r: r == start + 1, pieces[1]),
            (lambda r: r == start + 2, pieces[2]),
            (lambda r: r < 6, 1.0),
        )

    def pair(self, first, second):
        return choose(
            self.row, (lambda r: r < 3, first), (lambda r: r < 6, pltpu.roll(second, 3, 0))
        )

    def left(self):
        high, middle, low = self.pieces
        length = self.sided(split(self.length + 4.0 * SOFTEN), True)
        pairs = [self.pair(high, high), self.pair(high, middle), self.pair(middle, low)]
        return jnp.concatenate([*pairs, length], 0)

    def right(self):
        high, middle, low = [-8.0 * piece for piece in self.pieces]
        length = self.sided(split(self.length), False)
        pairs = [self.pair(high, middle), self.pair(low, high), self.pair(middle, high)]
        return jnp.concatenate([*pairs, length], 0).astype(BF16)

    def moments(self):
        high, middle, low = self.pieces
        upper = choose(
            self.row,
            (lambda r: r < 3, high),
            (lambda r: r == 3, 1.0),
            (lambda r: r < 7, pltpu.roll(middle, 4, 0)),
        )
        return jnp.concatenate([upper, jnp.where(self.row < 3, low, 0.0)], 0).astype(BF16)


def cut(array, tile):
    return array[:, tile * TILE : (tile + 1) * TILE]


def pair_force(length, mine, theirs):
    inverse = lax.rsqrt(length)
    inverse_sq = inverse * inverse
    screened = (mine[0] * theirs[0]) * (jnp.exp2(length * (inverse * -LOG2_E)) * inverse)
    root = (mine[2] + theirs[2]) * inverse
    ratio = root * root
    cubed = ratio * ratio * ratio
    less = cubed - 1.0
    switch = jnp.maximum(REACH - length, 0.0)
    near = switch * inverse
    nearer = switch * inverse_sq
    charged = screened * (near + nearer + 4.0)
    touching = (mine[1] * theirs[1] * cubed) * (less + (1.5 * nearer) * (cubed + less))
    return switch * (charged + touching)


def halves(force):
    high = force.astype(BF16)
    return high, (force - high.astype(F32)).astype(BF16)


def dot(a, b):
    return jnp.dot(a, b, preferred_element_type=F32)


def dot_rows(a, b):
    return lax.dot_general(a, b, (((1,), (1,)), ((), ())), preferred_element_type=F32)


def resolve(acc, rows):
    both = acc[0:8, :] + acc[8:16, :]
    turned = both + pltpu.roll(both, 4, 0)
    return (SCALE * (rows * both[3:4, :] - turned))[0:3, :]


def pack_left(lefts, left, left_x, left_traits):
    start = jnp.int32(0)
    for box in lefts:
        rows, dots = jnp.concatenate([box.left(), box.rows], 0), box.moments()
        for tile in range(dots.shape[1] // TILE):
            columns = cut(rows, tile).T
            left[start + tile] = columns[:, :DEPTH].astype(BF16)
            left_x[start + tile] = cut(dots, tile)
            for number in range(3):
                column = columns[:, DEPTH + 3 + number : DEPTH + 4 + number]
                left_traits[start + tile, number] = jnp.broadcast_to(column, (TILE, TILE))
        start = start + box.live


def pack_right(rights, own, right, right_x, right_traits):
    def put(spot, box, features, dots, tile):
        right[spot] = cut(features, tile)
        right_x[spot] = cut(dots, tile)
        right_traits[spot] = cut(box.rows, tile)

    start = jnp.int32(0)
    for box in rights:
        features, dots = box.right(), box.moments()
        tiles = dots.shape[1] // TILE
        for tile in range(tiles):
            put(start + tile, box, features, dots, tile)
        start = start + box.live
    if own is not None:
        box, features, dots = own, own.right(), own.moments()
        first = start
        for tile in range(tiles):

            @pl.when(tile < own.live)
            def _():
                put(first + own.live - 1 - tile, own, features, dots, tile)

        start = start + own.live
    put(start, box, features, dots, 0)
    right_traits[start] = jnp.zeros(right_traits.shape[1:], F32)


def starts(boxes):
    spots = [jnp.int32(0)]
    for box in boxes:
        spots.append(spots[-1] + box.live)
    return spots


def pair_blocks(lefts, rights, own, left_side, right_side, scratch):
    left, left_x, left_traits = left_side
    right, right_x, right_traits = right_side
    left_acc, right_acc, parts_a, parts_b, force_a, force_b = scratch
    tiles = lefts[0].rows.shape[1] // TILE
    left_start, right_start = starts(lefts), starts(rights)
    first_own, first_above, n_left = left_start[1:]
    n_plate = right_start[-1]
    n_own = jnp.int32(0) if own is None else own.live
    empty = n_plate + n_own
    right_acc[...] = jnp.zeros(right_acc.shape, F32)

    def extent(t):
        if own is None:
            return n_plate
        own_part = jnp.where(t < first_above, n_own - 1 - (t - first_own), n_own)
        return n_plate + jnp.where(t < first_own, 0, own_part)

    def following(block):
        t, p = block
        step = 2 * p + 2 < extent(t)
        return jnp.where(step, t, jnp.minimum(t + 1, n_left)), jnp.where(step, p + 1, 0)

    def place(block):
        t, p = block
        inside = t < n_left
        one = jnp.where(inside, 2 * p, empty)
        two = jnp.where(inside & (2 * p + 1 < extent(t)), 2 * p + 1, empty)
        return jnp.where(inside, t, 0), one, two

    def spread(spots):
        t, one, two = spots
        return dot(left[t], jnp.concatenate([right[one], right[two]], 1))

    def work(spots, parts):
        t, one, two = spots
        mine = [left_traits[t, trait] for trait in range(3)]
        forces = []
        for lanes, spot in ((slice(0, TILE), one), (slice(TILE, 2 * TILE), two)):
            theirs = [right_traits[spot, 3 + trait : 4 + trait, :] for trait in range(3)]
            forces.append(halves(pair_force(parts[:, lanes], mine, theirs)))
        return forces

    def hold(split_force, forces):
        for side, (high, low) in enumerate(forces):
            split_force[0, :, side * TILE : (side + 1) * TILE] = high
            split_force[1, :, side * TILE : (side + 1) * TILE] = low

    def gather(spots, split_force):
        t, one, two = spots
        theirs_x = [right_x[one], right_x[two]]
        theirs_x = jnp.concatenate([*theirs_x, *theirs_x], 1)
        mine_x = jnp.concatenate([left_x[t], left_x[t]], 1)
        force = jnp.concatenate([split_force[0], split_force[1]], 1)
        back = dot(mine_x, split_force[...].reshape(2 * TILE, 2 * TILE))
        return dot_rows(theirs_x, force), back

    def collect(spots, sums):
        t, one, two = spots
        forward, back = sums
        left_acc[t] = left_acc[t] + forward
        right_acc[one] = right_acc[one] + back[:, :TILE]
        right_acc[two] = right_acc[two] + back[:, TILE:]

    def two_blocks(_, carry):
        block, before = carry
        spots = place(block)
        block = following(block)
        middle = place(block)
        block = following(block)
        later = place(block)
        for now, into, held, parts, out, past, back in (
            (middle, parts_b, spots, parts_a, force_a, before, force_b),
            (later, parts_a, middle, parts_b, force_b, spots, force_a),
        ):
            lengths = spread(now)
            sums = gather(past, back)
            forces = work(held, parts)
            into[...] = lengths
            hold(out, forces)
            collect(past, sums)
        return block, middle

    def pairs_of(count):
        return (count + 1) // 2

    if own is None:
        blocks = n_left * pairs_of(n_plate)
    else:
        blocks = first_own * pairs_of(n_plate) + (n_left - first_above) * pairs_of(n_plate + n_own)
        for tile in range(tiles):
            blocks = blocks + jnp.where(tile < n_own, pairs_of(n_plate + tile), 0)
    left_acc[...] = jnp.zeros(left_acc.shape, F32)
    force_b[...] = jnp.zeros(force_b.shape, BF16)
    zero = jnp.int32(0)
    first = (zero, zero)
    parts_a[...] = spread(place(first))
    _, last = lax.fori_loop(0, pairs_of(blocks), two_blocks, (first, (zero, empty, empty)))
    collect(last, gather(last, force_b))

    if own is not None:
        for tile in range(tiles):
            t = first_own + tile
            spot = jnp.maximum(n_plate + n_own - 1 - tile, 0)
            mine = left[t]
            columns = [left_traits[t, trait] for trait in range(3)]
            theirs = [right_traits[spot, 3 + trait : 4 + trait, :] for trait in range(3)]
            force = pair_force(dot(mine, right[spot]), columns, theirs)
            row = lax.broadcasted_iota(jnp.int32, force.shape, 0)
            col = lax.broadcasted_iota(jnp.int32, force.shape, 1)
            high, low = halves(jnp.where((row != col) & (tile < n_own), force, 0.0))
            theirs_x = right_x[spot]
            left_acc[t] = left_acc[t] + dot_rows(theirs_x, high) + dot_rows(theirs_x, low)

    def force(box, acc, tile):
        return jnp.where(tile < box.live, resolve(acc, cut(box.rows, tile)), 0.0)

    def left_force(number, tile):
        acc = left_acc[left_start[number] + tile]
        if own is not None and number == 1:
            acc = acc + right_acc[jnp.maximum(n_plate + n_own - 1 - tile, 0)]
        return force(lefts[number], acc, tile)

    def right_force(number, tile):
        return force(rights[number], right_acc[right_start[number] + tile], tile)

    return left_force, right_force


TOWER = ((0, -1, 0), (0, 0, 0), (0, 1, 0))
BESIDE = (1, 0, 0)
ROW = ((-1, 0, 1), (0, 0, 1), (1, 0, 1))


def lane(tile):
    return slice(tile * TILE, (tile + 1) * TILE)


def tower_boxes(below, own, above):
    return [Box(ref, move) for ref, move in zip((below, own, above), TOWER)]


def feature_kernel(below, own, above, beside, *sides):
    lefts = tower_boxes(below, own, above)
    pack_left(lefts, *sides[:3])
    pack_right([Box(beside, BESIDE)], lefts[1], *sides[3:])


def row_kernel(below, own, above, *refs):
    rights, left_side, out_row, outs = refs[:3], refs[3:6], refs[6], refs[7:10]
    right_side, scratch = refs[10:13], refs[13:]
    lefts = tower_boxes(below, own, above)
    boxes = [Box(ref, move) for ref, move in zip(rights, ROW)]
    pack_right(boxes, None, *right_side)
    left_force, right_force = pair_blocks(lefts, boxes, None, left_side, right_side, scratch)
    for tile in range(own.shape[1] // TILE):
        for number in range(3):
            out_row[3 * number : 3 * number + 3, lane(tile)] = right_force(number, tile)
            outs[number][:, lane(tile)] = left_force(number, tile)


def rest_kernel(below, own, above, beside, *refs):
    left_side, right_side, (add_below, add_own, add_above) = refs[:3], refs[3:6], refs[6:9]
    out_beside, out_own, out_towers, scratch = refs[9], refs[10], refs[11:-6], refs[-6:]
    lefts = tower_boxes(below, own, above)
    left_force, right_force = pair_blocks(
        lefts, [Box(beside, BESIDE)], lefts[1], left_side, right_side, scratch
    )
    for tile in range(own.shape[1] // TILE):
        out_beside[:, lane(tile)] = right_force(0, tile)
        out_own[:, lane(tile)] = left_force(1, tile) + add_own[:, lane(tile)]
        low = left_force(0, tile) + add_below[:, lane(tile)]
        high = left_force(2, tile) + add_above[:, lane(tile)]
        if len(out_towers) == 1:
            out_towers[0][:, lane(tile)] = low + high
        else:
            out_towers[0][:, lane(tile)] = low
            out_towers[1][:, lane(tile)] = high


def merge_kernel(row, beside, own, to_low, to_high, total):
    to_low[...] = row[0:3, :]
    to_high[...] = row[6:9, :] + beside[...]
    total[...] = row[3:6, :] + own[...]


def add_up(parts):
    force = parts[0][...]
    for ref in parts[1:]:
        force = force + ref[...]
    return force


def middle_kernel(record, half, *refs):
    force = add_up(refs[:-2])
    new_record, new_half = refs[-2:]
    velocity = half[...] + HALF_STEP * force
    velocity = velocity + HALF_STEP * force
    new_half[...] = velocity
    new_record[3:8, :] = record[3:8, :]
    new_record[0:3, :] = record[0:3, :] + TIME_STEP * velocity


def last_kernel(record, half, *refs):
    force = add_up(refs[:-3])
    places, velocity, pushing = refs[-3:]
    final = half[...] + HALF_STEP * force
    for axis in range(3):
        places[axis, 0, 0] = record[axis : axis + 1, :]
        velocity[axis, 0, 0] = final[axis : axis + 1, :]
        pushing[axis, 0, 0] = force[axis : axis + 1, :]


VMEM = pltpu.VMEM
SMEM = pltpu.SMEM
LIMIT = 32 * 1024 * 1024


def shape(*dims):
    return jax.ShapeDtypeStruct(dims, F32)


def whole(space=VMEM):
    return pl.BlockSpec(memory_space=space)


def call(kernel, outs, args, pairs=0, scratch=()):
    cost = pl.CostEstimate(
        flops=50 * pairs, bytes_accessed=14 * 32 * args[0].shape[1], transcendentals=2 * pairs
    )
    return pl.pallas_call(
        kernel,
        out_shape=outs,
        in_specs=[whole()] * len(args),
        out_specs=[whole()] * len(outs),
        scratch_shapes=list(scratch),
        compiler_params=pltpu.CompilerParams(vmem_limit_bytes=LIMIT),
        cost_estimate=cost,
    )(*args)


class Ring:
    def __init__(self, name, size):
        self.name, self.size = name, size

    def bring(self, value, offset):
        pairs = [((i + offset) % self.size, i) for i in range(self.size)]
        return lax.ppermute(value, self.name, pairs)

    def give(self, value, offset):
        return self.bring(value, -offset)


def step_forces(record, gx, gy, gz):
    slots = record.shape[1]
    one = shape(3, slots)
    up = gz.bring(record, 1)
    above = gy.bring(record, 1)
    below = above if gy.size == 2 else gy.bring(record, -1)
    beside = gx.bring(record, 1)
    row = (gx.bring(up, -1), up, gx.bring(up, 1))
    tower = (below, record, above)
    tiles = slots // TILE

    def kept(*dims):
        return jax.ShapeDtypeStruct(dims, BF16)

    def sides(boxes):
        count = boxes * tiles + 1
        return kept(count, DEPTH, TILE), kept(count, 16, TILE), shape(count, 8, TILE)

    def scratch(boxes):
        return (
            VMEM((3 * tiles, 16, TILE), F32),
            VMEM((boxes * tiles + 1, 16, TILE), F32),
            VMEM((TILE, 2 * TILE), F32),
            VMEM((TILE, 2 * TILE), F32),
            VMEM((2, TILE, 2 * TILE), BF16),
            VMEM((2, TILE, 2 * TILE), BF16),
        )

    outs = [kept(3 * tiles, TILE, DEPTH), kept(3 * tiles, 16, TILE)]
    outs += [shape(3 * tiles, 3, TILE, TILE), *sides(2)]
    features = call(feature_kernel, outs, (*tower, beside), pairs=slots * slots)
    out_row, *adds = call(
        row_kernel,
        [shape(9, slots), one, one, one],
        (*tower, *row, *features[:3]),
        pairs=9 * slots * slots,
        scratch=[VMEM(side.shape, side.dtype) for side in sides(3)] + [*scratch(3)],
    )
    row_back = gz.give(out_row, 1)
    towers = 1 if gy.size == 2 else 2
    out_beside, out_own, *outs = call(
        rest_kernel,
        [one] * (2 + towers),
        (*tower, beside, *features, *adds),
        pairs=5 * slots * slots,
        scratch=scratch(2),
    )
    back = [gy.give(out, offset) for out, offset in zip(outs, (-1, 1))]
    to_low, to_high, own = call(merge_kernel, [one] * 3, (row_back, out_beside, out_own))
    return [own, gx.give(to_low, -1), gx.give(to_high, 1), *back]


def on_device(axes, positions, velocities, forces, charges, types, counts, epsilon, sigma):
    slots = positions.shape[-1]
    rings = [Ring(name, size) for name, size in zip(("gx", "gy", "gz"), axes)]
    record, half = pl.pallas_call(
        start_kernel,
        out_shape=[shape(8, slots), shape(3, slots)],
        in_specs=[whole(SMEM)] * 3 + [whole()] * 5,
        out_specs=[whole()] * 2,
    )(counts, epsilon, sigma, positions, velocities, forces, charges, types)
    for step in range(STEPS):
        parts = step_forces(record, *rings)
        if step < STEPS - 1:
            outs = [shape(8, slots), shape(3, slots)]
            record, half = call(middle_kernel, outs, (record, half, *parts))
        else:
            outs = call(last_kernel, [shape(*positions.shape)] * 3, (record, half, *parts))
    return tuple(outs)


def solution(mesh):
    boxes = P(None, "gx", "gy", "gz", None)
    slot = P("gx", "gy", "gz", None)
    in_specs = (boxes, boxes, boxes, slot, slot, P("gx", "gy", "gz"), P(), P())
    axes = tuple(mesh.shape[name] for name in ("gx", "gy", "gz"))
    return jax.shard_map(
        functools.partial(on_device, axes),
        mesh=mesh,
        in_specs=in_specs,
        out_specs=(boxes, boxes, boxes),
        check_vma=False,
    )
```

```python
import functools

import jax
import jax.numpy as jnp
from jax import lax
from jax.experimental import pallas as pl
from jax.experimental.pallas import tpu as pltpu
from jax.sharding import PartitionSpec as P

TILE = 128
STEPS = 2

COULOMB = 0.02
SOFTEN = 0.0225
CUTOFF = 0.81
TIME_STEP = 0.05
HALF_STEP = 0.025
REACH = 4.0 * (CUTOFF + SOFTEN)
LOG2_E = 1.4426950408889634
DEPTH = 32
SCALE = 1.0 / (4.0 * CUTOFF * CUTOFF)

F32 = jnp.float32
BF16 = jnp.bfloat16


def start_kernel(count, epsilon, sigma, pos, vel, frc, charge, kinds, record, half):
    live_tiles = count[0, 0, 0]
    slots = pos.shape[4]
    live = lax.broadcasted_iota(jnp.int32, (1, slots), 1) < live_tiles * TILE
    kind = kinds[0, 0]
    depth = jnp.zeros((1, slots), F32)
    size = jnp.zeros((1, slots), F32)
    for k in range(epsilon.shape[0]):
        same = kind == k
        depth = jnp.where(same, epsilon[k], depth)
        size = jnp.where(same, sigma[k], size)
    places = []
    for axis in range(3):
        velocity = vel[axis, 0, 0] + HALF_STEP * frc[axis, 0, 0]
        places.append(pos[axis, 0, 0] + TIME_STEP * velocity)
        half[axis : axis + 1, :] = velocity
    record[...] = jnp.concatenate(
        [
            *places,
            jnp.where(live, (2.0 * COULOMB) ** 0.5 * charge[0, 0], 0.0),
            jnp.where(live, 4.0 * jnp.sqrt(depth), 0.0),
            size,
            jnp.full((1, slots), live_tiles.astype(F32)),
            jnp.zeros((1, slots), F32),
        ],
        0,
    )


def split(value):
    high = value.astype(BF16).astype(F32)
    rest = value - high
    middle = rest.astype(BF16).astype(F32)
    return high, middle, rest - middle


def choose(row, *cases):
    value = 0.0
    for test, case in reversed(cases):
        value = jnp.where(test(row), case, value)
    return value


class Box:
    def __init__(self, record, shift):
        rows = record[...]
        row = lax.broadcasted_iota(jnp.int32, rows.shape, 0)
        self.row = row
        moved = [rows + (value - 0.5) if value != 0.5 else rows for value in shift]
        self.rows = choose(
            row,
            (lambda r: r == 0, moved[0]),
            (lambda r: r == 1, moved[1]),
            (lambda r: r == 2, moved[2]),
            (lambda r: r < 6, rows),
        )
        self.live = jnp.max(record[6:7, 0:TILE]).astype(jnp.int32)
        self.pieces = split(self.rows)
        square = jnp.where(row < 3, self.rows * self.rows, 0.0)
        length = jnp.sum(square, axis=0, keepdims=True)
        self.length = jnp.broadcast_to(4.0 * length, rows.shape)

    def sided(self, pieces, first):
        start = 0 if first else 3
        return choose(
            self.row,
            (lambda r: r == start, pieces[0]),
            (lambda r: r == start + 1, pieces[1]),
            (lambda r: r == start + 2, pieces[2]),
            (lambda r: r < 6, 1.0),
        )

    def pair(self, first, second):
        return choose(
            self.row, (lambda r: r < 3, first), (lambda r: r < 6, pltpu.roll(second, 3, 0))
        )

    def left(self):
        high, middle, low = self.pieces
        length = self.sided(split(self.length + 4.0 * SOFTEN), True)
        pairs = [self.pair(high, high), self.pair(high, middle), self.pair(middle, low)]
        return jnp.concatenate([*pairs, length], 0)

    def right(self):
        high, middle, low = [-8.0 * piece for piece in self.pieces]
        length = self.sided(split(self.length), False)
        pairs = [self.pair(high, middle), self.pair(low, high), self.pair(middle, high)]
        return jnp.concatenate([*pairs, length], 0).astype(BF16)

    def moments(self):
        high, middle, low = self.pieces
        upper = choose(
            self.row,
            (lambda r: r < 3, high),
            (lambda r: r == 3, 1.0),
            (lambda r: r < 7, pltpu.roll(middle, 4, 0)),
        )
        return jnp.concatenate([upper, jnp.where(self.row < 3, low, 0.0)], 0)


def cut(array, tile):
    return array[:, tile * TILE : (tile + 1) * TILE]


def pair_force(length, mine, theirs):
    inverse = lax.rsqrt(length)
    inverse_sq = inverse * inverse
    screened = (mine[0] * theirs[0]) * (jnp.exp2(length * (inverse * -LOG2_E)) * inverse)
    root = (mine[2] + theirs[2]) * inverse
    ratio = root * root
    cubed = ratio * ratio * ratio
    less = cubed - 1.0
    switch = jnp.maximum(REACH - length, 0.0)
    near = switch * inverse
    nearer = switch * inverse_sq
    charged = screened * (near + nearer + 4.0)
    touching = (mine[1] * theirs[1] * cubed) * (less + (1.5 * nearer) * (cubed + less))
    return switch * (charged + touching)


def halves(force):
    high = force.astype(BF16)
    return high, (force - high.astype(F32)).astype(BF16)


def dot(a, b):
    return jnp.dot(a, b, preferred_element_type=F32)


def resolve(acc, rows):
    both = acc[0:8, :] + acc[8:16, :]
    turned = both + pltpu.roll(both, 4, 0)
    return (SCALE * (rows * both[3:4, :] - turned))[0:3, :]


def pack_left(lefts, left, left_x, left_traits):
    start = jnp.int32(0)
    for box in lefts:
        rows, dots = jnp.concatenate([box.left(), box.rows], 0), box.moments()
        for tile in range(dots.shape[1] // TILE):
            columns = cut(rows, tile).T
            left[start + tile] = columns[:, :DEPTH].astype(BF16)
            left_x[start + tile] = cut(dots, tile).astype(BF16)
            for number in range(3):
                column = columns[:, DEPTH + 3 + number : DEPTH + 4 + number]
                left_traits[start + tile, number] = jnp.broadcast_to(column, (TILE, TILE))
        start = start + box.live


def pack_right(rights, own, right, right_x, right_traits):
    def put(spot, box, features, dots, tile):
        right[spot] = cut(features, tile)
        right_x[spot] = cut(dots, tile).T.astype(BF16)
        right_traits[spot] = cut(box.rows, tile)

    start = jnp.int32(0)
    for box in rights:
        features, dots = box.right(), box.moments()
        tiles = dots.shape[1] // TILE
        for tile in range(tiles):
            put(start + tile, box, features, dots, tile)
        start = start + box.live
    if own is not None:
        box, features, dots = own, own.right(), own.moments()
        first = start
        for tile in range(tiles):

            @pl.when(tile < own.live)
            def _():
                put(first + own.live - 1 - tile, own, features, dots, tile)

        start = start + own.live
    put(start, box, features, dots, 0)
    right_traits[start] = jnp.zeros(right_traits.shape[1:], F32)


def starts(boxes):
    spots = [jnp.int32(0)]
    for box in boxes:
        spots.append(spots[-1] + box.live)
    return spots


def pair_blocks(lefts, rights, own, left_side, right_side, scratch):
    left, left_x, left_traits = left_side
    right, right_x, right_traits = right_side
    left_acc, right_acc, parts_a, parts_b, force_a, force_b = scratch
    tiles = lefts[0].rows.shape[1] // TILE
    left_start, right_start = starts(lefts), starts(rights)
    first_own, first_above, n_left = left_start[1:]
    n_plate = right_start[-1]
    n_own = jnp.int32(0) if own is None else own.live
    empty = n_plate + n_own
    right_acc[...] = jnp.zeros(right_acc.shape, F32)

    def extent(t):
        if own is None:
            return n_plate
        own_part = jnp.where(t < first_above, n_own - 1 - (t - first_own), n_own)
        return n_plate + jnp.where(t < first_own, 0, own_part)

    def following(block):
        t, p = block
        step = 2 * p + 2 < extent(t)
        return jnp.where(step, t, jnp.minimum(t + 1, n_left)), jnp.where(step, p + 1, 0)

    def place(block):
        t, p = block
        inside = t < n_left
        one = jnp.where(inside, 2 * p, empty)
        two = jnp.where(inside & (2 * p + 1 < extent(t)), 2 * p + 1, empty)
        return jnp.where(inside, t, 0), one, two

    def spread(spots):
        t, one, two = spots
        return dot(left[t], jnp.concatenate([right[one], right[two]], 1))

    def work(spots, parts):
        t, one, two = spots
        mine = [left_traits[t, trait] for trait in range(3)]
        forces = []
        for lanes, spot in ((slice(0, TILE), one), (slice(TILE, 2 * TILE), two)):
            theirs = [right_traits[spot, 3 + trait : 4 + trait, :] for trait in range(3)]
            forces.append(halves(pair_force(parts[:, lanes], mine, theirs)))
        return forces

    def hold(split_force, forces):
        for side, (high, low) in enumerate(forces):
            split_force[0, :, side * TILE : (side + 1) * TILE] = high
            split_force[1, :, side * TILE : (side + 1) * TILE] = low

    def gather(spots, split_force):
        t, one, two = spots
        theirs_x = [right_x[one], right_x[two]]
        theirs_x = jnp.concatenate([*theirs_x, *theirs_x], 0)
        mine_x = jnp.concatenate([left_x[t], left_x[t]], 1)
        force = jnp.concatenate([split_force[0], split_force[1]], 1)
        back = dot(mine_x, split_force[...].reshape(2 * TILE, 2 * TILE))
        return dot(force, theirs_x), back

    def collect(spots, sums):
        t, one, two = spots
        forward, back = sums
        left_acc[t] = left_acc[t] + forward
        right_acc[one] = right_acc[one] + back[:, :TILE]
        right_acc[two] = right_acc[two] + back[:, TILE:]

    def two_blocks(_, carry):
        block, before = carry
        spots = place(block)
        block = following(block)
        middle = place(block)
        block = following(block)
        later = place(block)
        for now, into, held, parts, out, past, back in (
            (middle, parts_b, spots, parts_a, force_a, before, force_b),
            (later, parts_a, middle, parts_b, force_b, spots, force_a),
        ):
            lengths = spread(now)
            sums = gather(past, back)
            forces = work(held, parts)
            into[...] = lengths
            hold(out, forces)
            collect(past, sums)
        return block, middle

    def pairs_of(count):
        return (count + 1) // 2

    if own is None:
        blocks = n_left * pairs_of(n_plate)
    else:
        blocks = first_own * pairs_of(n_plate) + (n_left - first_above) * pairs_of(n_plate + n_own)
        for tile in range(tiles):
            blocks = blocks + jnp.where(tile < n_own, pairs_of(n_plate + tile), 0)
    left_acc[...] = jnp.zeros(left_acc.shape, F32)
    force_b[...] = jnp.zeros(force_b.shape, BF16)
    zero = jnp.int32(0)
    first = (zero, zero)
    parts_a[...] = spread(place(first))
    _, last = lax.fori_loop(0, pairs_of(blocks), two_blocks, (first, (zero, empty, empty)))
    collect(last, gather(last, force_b))

    if own is not None:
        for tile in range(tiles):
            t = first_own + tile
            spot = jnp.maximum(n_plate + n_own - 1 - tile, 0)
            mine = left[t]
            columns = [left_traits[t, trait] for trait in range(3)]
            theirs = [right_traits[spot, 3 + trait : 4 + trait, :] for trait in range(3)]
            force = pair_force(dot(mine, right[spot]), columns, theirs)
            row = lax.broadcasted_iota(jnp.int32, force.shape, 0)
            col = lax.broadcasted_iota(jnp.int32, force.shape, 1)
            high, low = halves(jnp.where((row != col) & (tile < n_own), force, 0.0))
            theirs_x = right_x[spot]
            left_acc[t] = left_acc[t] + dot(high, theirs_x) + dot(low, theirs_x)

    def force(box, acc, tile):
        return jnp.where(tile < box.live, resolve(acc, cut(box.rows, tile)), 0.0)

    def left_force(number, tile):
        acc = left_acc[left_start[number] + tile].T
        if own is not None and number == 1:
            acc = acc + right_acc[jnp.maximum(n_plate + n_own - 1 - tile, 0)]
        return force(lefts[number], acc, tile)

    def right_force(number, tile):
        return force(rights[number], right_acc[right_start[number] + tile], tile)

    return left_force, right_force


TOWER = ((0, -1, 0), (0, 0, 0), (0, 1, 0))
BESIDE = (1, 0, 0)
ROW = ((-1, 0, 1), (0, 0, 1), (1, 0, 1))


def lane(tile):
    return slice(tile * TILE, (tile + 1) * TILE)


def tower_boxes(below, own, above):
    return [Box(ref, move) for ref, move in zip((below, own, above), TOWER)]


def feature_kernel(below, own, above, beside, *sides):
    lefts = tower_boxes(below, own, above)
    pack_left(lefts, *sides[:3])
    pack_right([Box(beside, BESIDE)], lefts[1], *sides[3:])


def row_kernel(below, own, above, *refs):
    rights, left_side, out_row, outs = refs[:3], refs[3:6], refs[6], refs[7:10]
    right_side, scratch = refs[10:13], refs[13:]
    lefts = tower_boxes(below, own, above)
    boxes = [Box(ref, move) for ref, move in zip(rights, ROW)]
    pack_right(boxes, None, *right_side)
    left_force, right_force = pair_blocks(lefts, boxes, None, left_side, right_side, scratch)
    for tile in range(own.shape[1] // TILE):
        for number in range(3):
            out_row[3 * number : 3 * number + 3, lane(tile)] = right_force(number, tile)
            outs[number][:, lane(tile)] = left_force(number, tile)


def rest_kernel(below, own, above, beside, *refs):
    left_side, right_side, (add_below, add_own, add_above) = refs[:3], refs[3:6], refs[6:9]
    out_beside, out_own, out_towers, scratch = refs[9], refs[10], refs[11:-6], refs[-6:]
    lefts = tower_boxes(below, own, above)
    left_force, right_force = pair_blocks(
        lefts, [Box(beside, BESIDE)], lefts[1], left_side, right_side, scratch
    )
    for tile in range(own.shape[1] // TILE):
        out_beside[:, lane(tile)] = right_force(0, tile)
        out_own[:, lane(tile)] = left_force(1, tile) + add_own[:, lane(tile)]
        low = left_force(0, tile) + add_below[:, lane(tile)]
        high = left_force(2, tile) + add_above[:, lane(tile)]
        if len(out_towers) == 1:
            out_towers[0][:, lane(tile)] = low + high
        else:
            out_towers[0][:, lane(tile)] = low
            out_towers[1][:, lane(tile)] = high


def merge_kernel(row, beside, own, to_low, to_high, total):
    to_low[...] = row[0:3, :]
    to_high[...] = row[6:9, :] + beside[...]
    total[...] = row[3:6, :] + own[...]


def add_up(parts):
    force = parts[0][...]
    for ref in parts[1:]:
        force = force + ref[...]
    return force


def middle_kernel(record, half, *refs):
    force = add_up(refs[:-2])
    new_record, new_half = refs[-2:]
    velocity = half[...] + HALF_STEP * force
    velocity = velocity + HALF_STEP * force
    new_half[...] = velocity
    new_record[3:8, :] = record[3:8, :]
    new_record[0:3, :] = record[0:3, :] + TIME_STEP * velocity


def last_kernel(record, half, *refs):
    force = add_up(refs[:-3])
    places, velocity, pushing = refs[-3:]
    final = half[...] + HALF_STEP * force
    for axis in range(3):
        places[axis, 0, 0] = record[axis : axis + 1, :]
        velocity[axis, 0, 0] = final[axis : axis + 1, :]
        pushing[axis, 0, 0] = force[axis : axis + 1, :]


VMEM = pltpu.VMEM
SMEM = pltpu.SMEM
LIMIT = 32 * 1024 * 1024


def shape(*dims):
    return jax.ShapeDtypeStruct(dims, F32)


def whole(space=VMEM):
    return pl.BlockSpec(memory_space=space)


def call(kernel, outs, args, pairs=0, scratch=()):
    cost = pl.CostEstimate(
        flops=50 * pairs, bytes_accessed=14 * 32 * args[0].shape[1], transcendentals=2 * pairs
    )
    return pl.pallas_call(
        kernel,
        out_shape=outs,
        in_specs=[whole()] * len(args),
        out_specs=[whole()] * len(outs),
        scratch_shapes=list(scratch),
        compiler_params=pltpu.CompilerParams(vmem_limit_bytes=LIMIT),
        cost_estimate=cost,
    )(*args)


class Ring:
    def __init__(self, name, size):
        self.name, self.size = name, size

    def bring(self, value, offset):
        pairs = [((i + offset) % self.size, i) for i in range(self.size)]
        return lax.ppermute(value, self.name, pairs)

    def give(self, value, offset):
        return self.bring(value, -offset)


def step_forces(record, gx, gy, gz):
    slots = record.shape[1]
    one = shape(3, slots)
    up = gz.bring(record, 1)
    above = gy.bring(record, 1)
    below = above if gy.size == 2 else gy.bring(record, -1)
    beside = gx.bring(record, 1)
    row = (gx.bring(up, -1), up, gx.bring(up, 1))
    tower = (below, record, above)
    tiles = slots // TILE

    def kept(*dims):
        return jax.ShapeDtypeStruct(dims, BF16)

    def sides(boxes):
        count = boxes * tiles + 1
        return kept(count, DEPTH, TILE), kept(count, TILE, 16), shape(count, 8, TILE)

    def scratch(boxes):
        return (
            VMEM((3 * tiles, TILE, 16), F32),
            VMEM((boxes * tiles + 1, 16, TILE), F32),
            VMEM((TILE, 2 * TILE), F32),
            VMEM((TILE, 2 * TILE), F32),
            VMEM((2, TILE, 2 * TILE), BF16),
            VMEM((2, TILE, 2 * TILE), BF16),
        )

    outs = [kept(3 * tiles, TILE, DEPTH), kept(3 * tiles, 16, TILE)]
    outs += [shape(3 * tiles, 3, TILE, TILE), *sides(2)]
    features = call(feature_kernel, outs, (*tower, beside), pairs=slots * slots)
    out_row, *adds = call(
        row_kernel,
        [shape(9, slots), one, one, one],
        (*tower, *row, *features[:3]),
        pairs=9 * slots * slots,
        scratch=[VMEM(side.shape, side.dtype) for side in sides(3)] + [*scratch(3)],
    )
    row_back = gz.give(out_row, 1)
    towers = 1 if gy.size == 2 else 2
    out_beside, out_own, *outs = call(
        rest_kernel,
        [one] * (2 + towers),
        (*tower, beside, *features, *adds),
        pairs=5 * slots * slots,
        scratch=scratch(2),
    )
    back = [gy.give(out, offset) for out, offset in zip(outs, (-1, 1))]
    to_low, to_high, own = call(merge_kernel, [one] * 3, (row_back, out_beside, out_own))
    return [own, gx.give(to_low, -1), gx.give(to_high, 1), *back]


def on_device(axes, positions, velocities, forces, charges, types, counts, epsilon, sigma):
    slots = positions.shape[-1]
    rings = [Ring(name, size) for name, size in zip(("gx", "gy", "gz"), axes)]
    record, half = pl.pallas_call(
        start_kernel,
        out_shape=[shape(8, slots), shape(3, slots)],
        in_specs=[whole(SMEM)] * 3 + [whole()] * 5,
        out_specs=[whole()] * 2,
    )(counts, epsilon, sigma, positions, velocities, forces, charges, types)
    for step in range(STEPS):
        parts = step_forces(record, *rings)
        if step < STEPS - 1:
            outs = [shape(8, slots), shape(3, slots)]
            record, half = call(middle_kernel, outs, (record, half, *parts))
        else:
            outs = call(last_kernel, [shape(*positions.shape)] * 3, (record, half, *parts))
    return tuple(outs)


def solution(mesh):
    boxes = P(None, "gx", "gy", "gz", None)
    slot = P("gx", "gy", "gz", None)
    in_specs = (boxes, boxes, boxes, slot, slot, P("gx", "gy", "gz"), P(), P())
    axes = tuple(mesh.shape[name] for name in ("gx", "gy", "gz"))
    return jax.shard_map(
        functools.partial(on_device, axes),
        mesh=mesh,
        in_specs=in_specs,
        out_specs=(boxes, boxes, boxes),
        check_vma=False,
    )
```

```python
import functools

import jax
import jax.numpy as jnp
from jax import lax
from jax.experimental import pallas as pl
from jax.experimental.pallas import tpu as pltpu
from jax.sharding import PartitionSpec as P

TILE = 128
STEPS = 2

COULOMB = 0.02
SOFTEN = 0.0225
CUTOFF = 0.81
TIME_STEP = 0.05
HALF_STEP = 0.025
REACH = 4.0 * (CUTOFF + SOFTEN)
LOG2_E = 1.4426950408889634
DEPTH = 32
UNROLL = 4
SCALE = 1.0 / (4.0 * CUTOFF * CUTOFF)

F32 = jnp.float32
BF16 = jnp.bfloat16


def start_kernel(count, epsilon, sigma, pos, vel, frc, charge, kinds, record, half):
    live_tiles = count[0, 0, 0]
    slots = pos.shape[4]
    live = lax.broadcasted_iota(jnp.int32, (1, slots), 1) < live_tiles * TILE
    kind = kinds[0, 0]
    depth = jnp.zeros((1, slots), F32)
    size = jnp.zeros((1, slots), F32)
    for k in range(epsilon.shape[0]):
        same = kind == k
        depth = jnp.where(same, epsilon[k], depth)
        size = jnp.where(same, sigma[k], size)
    places = []
    for axis in range(3):
        velocity = vel[axis, 0, 0] + HALF_STEP * frc[axis, 0, 0]
        places.append(pos[axis, 0, 0] + TIME_STEP * velocity)
        half[axis : axis + 1, :] = velocity
    record[...] = jnp.concatenate(
        [
            *places,
            jnp.where(live, (2.0 * COULOMB) ** 0.5 * charge[0, 0], 0.0),
            jnp.where(live, 4.0 * jnp.sqrt(depth), 0.0),
            size,
            jnp.full((1, slots), live_tiles.astype(F32)),
            jnp.zeros((1, slots), F32),
        ],
        0,
    )


def split(value):
    high = value.astype(BF16).astype(F32)
    rest = value - high
    middle = rest.astype(BF16).astype(F32)
    return high, middle, rest - middle


def choose(row, *cases):
    value = 0.0
    for test, case in reversed(cases):
        value = jnp.where(test(row), case, value)
    return value


class Box:
    def __init__(self, record, shift):
        rows = record[...]
        row = lax.broadcasted_iota(jnp.int32, rows.shape, 0)
        self.row = row
        moved = [rows + (value - 0.5) if value != 0.5 else rows for value in shift]
        self.rows = choose(
            row,
            (lambda r: r == 0, moved[0]),
            (lambda r: r == 1, moved[1]),
            (lambda r: r == 2, moved[2]),
            (lambda r: r < 6, rows),
        )
        self.live = jnp.max(record[6:7, 0:TILE]).astype(jnp.int32)
        self.pieces = split(self.rows)
        square = jnp.where(row < 3, self.rows * self.rows, 0.0)
        length = jnp.sum(square, axis=0, keepdims=True)
        self.length = jnp.broadcast_to(4.0 * length, rows.shape)

    def sided(self, pieces, first):
        start = 0 if first else 3
        return choose(
            self.row,
            (lambda r: r == start, pieces[0]),
            (lambda r: r == start + 1, pieces[1]),
            (lambda r: r == start + 2, pieces[2]),
            (lambda r: r < 6, 1.0),
        )

    def pair(self, first, second):
        return choose(
            self.row, (lambda r: r < 3, first), (lambda r: r < 6, pltpu.roll(second, 3, 0))
        )

    def left(self):
        high, middle, low = self.pieces
        length = self.sided(split(self.length + 4.0 * SOFTEN), True)
        pairs = [self.pair(high, high), self.pair(high, middle), self.pair(middle, low)]
        return jnp.concatenate([*pairs, length], 0)

    def right(self):
        high, middle, low = [-8.0 * piece for piece in self.pieces]
        length = self.sided(split(self.length), False)
        pairs = [self.pair(high, middle), self.pair(low, high), self.pair(middle, high)]
        return jnp.concatenate([*pairs, length], 0).astype(BF16)

    def moments(self):
        high, middle, low = self.pieces
        upper = choose(
            self.row,
            (lambda r: r < 3, high),
            (lambda r: r == 3, 1.0),
            (lambda r: r < 7, pltpu.roll(middle, 4, 0)),
        )
        return jnp.concatenate([upper, jnp.where(self.row < 3, low, 0.0)], 0).astype(BF16)


def cut(array, tile):
    return array[:, tile * TILE : (tile + 1) * TILE]


def pair_force(length, mine, theirs):
    inverse = lax.rsqrt(length)
    inverse_sq = inverse * inverse
    screened = (mine[0] * theirs[0]) * (jnp.exp2(length * (inverse * -LOG2_E)) * inverse)
    root = (mine[2] + theirs[2]) * inverse
    ratio = root * root
    cubed = ratio * ratio * ratio
    less = cubed - 1.0
    switch = jnp.maximum(REACH - length, 0.0)
    near = switch * inverse
    nearer = switch * inverse_sq
    charged = screened * (near + nearer + 4.0)
    touching = (mine[1] * theirs[1] * cubed) * (less + (1.5 * nearer) * (cubed + less))
    return switch * (charged + touching)


def halves(force):
    high = force.astype(BF16)
    return high, (force - high.astype(F32)).astype(BF16)


def dot(a, b):
    return jnp.dot(a, b, preferred_element_type=F32)


def dot_rows(a, b):
    return lax.dot_general(a, b, (((1,), (1,)), ((), ())), preferred_element_type=F32)


def resolve(acc, rows):
    both = acc[0:8, :] + acc[8:16, :]
    turned = both + pltpu.roll(both, 4, 0)
    return (SCALE * (rows * both[3:4, :] - turned))[0:3, :]


def pack_left(lefts, left, left_x, left_traits):
    start = jnp.int32(0)
    for box in lefts:
        rows, dots = jnp.concatenate([box.left(), box.rows], 0), box.moments()
        for tile in range(dots.shape[1] // TILE):
            columns = cut(rows, tile).T
            left[start + tile] = columns[:, :DEPTH].astype(BF16)
            left_x[start + tile] = cut(dots, tile)
            for number in range(3):
                column = columns[:, DEPTH + 3 + number : DEPTH + 4 + number]
                left_traits[start + tile, number] = jnp.broadcast_to(column, (TILE, TILE))
        start = start + box.live


def pack_right(rights, own, right, right_x, right_traits):
    def put(spot, box, features, dots, tile):
        right[spot] = cut(features, tile)
        right_x[spot] = cut(dots, tile)
        right_traits[spot] = cut(box.rows, tile)

    start = jnp.int32(0)
    for box in rights:
        features, dots = box.right(), box.moments()
        tiles = dots.shape[1] // TILE
        for tile in range(tiles):
            put(start + tile, box, features, dots, tile)
        start = start + box.live
    if own is not None:
        box, features, dots = own, own.right(), own.moments()
        first = start
        for tile in range(tiles):

            @pl.when(tile < own.live)
            def _():
                put(first + own.live - 1 - tile, own, features, dots, tile)

        start = start + own.live
    put(start, box, features, dots, 0)
    right_traits[start] = jnp.zeros(right_traits.shape[1:], F32)


def starts(boxes):
    spots = [jnp.int32(0)]
    for box in boxes:
        spots.append(spots[-1] + box.live)
    return spots


def pair_blocks(lefts, rights, own, left_side, right_side, scratch):
    left, left_x, left_traits = left_side
    right, right_x, right_traits = right_side
    left_acc, right_acc, parts_a, parts_b, force_a, force_b = scratch
    tiles = lefts[0].rows.shape[1] // TILE
    left_start, right_start = starts(lefts), starts(rights)
    first_own, first_above, n_left = left_start[1:]
    n_plate = right_start[-1]
    n_own = jnp.int32(0) if own is None else own.live
    empty = n_plate + n_own
    right_acc[...] = jnp.zeros(right_acc.shape, F32)

    def extent(t):
        if own is None:
            return n_plate
        own_part = jnp.where(t < first_above, n_own - 1 - (t - first_own), n_own)
        return n_plate + jnp.where(t < first_own, 0, own_part)

    def following(block):
        t, p = block
        step = 2 * p + 2 < extent(t)
        return jnp.where(step, t, jnp.minimum(t + 1, n_left)), jnp.where(step, p + 1, 0)

    def place(block):
        t, p = block
        inside = t < n_left
        one = jnp.where(inside, 2 * p, empty)
        two = jnp.where(inside & (2 * p + 1 < extent(t)), 2 * p + 1, empty)
        return jnp.where(inside, t, 0), one, two

    def spread(spots):
        t, one, two = spots
        return dot(left[t], jnp.concatenate([right[one], right[two]], 1))

    def work(spots, parts):
        t, one, two = spots
        mine = [left_traits[t, trait] for trait in range(3)]
        forces = []
        for lanes, spot in ((slice(0, TILE), one), (slice(TILE, 2 * TILE), two)):
            theirs = [right_traits[spot, 3 + trait : 4 + trait, :] for trait in range(3)]
            forces.append(halves(pair_force(parts[:, lanes], mine, theirs)))
        return forces

    def hold(split_force, forces):
        for side, (high, low) in enumerate(forces):
            split_force[0, :, side * TILE : (side + 1) * TILE] = high
            split_force[1, :, side * TILE : (side + 1) * TILE] = low

    def gather(spots, split_force):
        t, one, two = spots
        theirs_x = [right_x[one], right_x[two]]
        theirs_x = jnp.concatenate([*theirs_x, *theirs_x], 1)
        mine_x = jnp.concatenate([left_x[t], left_x[t]], 1)
        force = jnp.concatenate([split_force[0], split_force[1]], 1)
        back = dot(mine_x, split_force[...].reshape(2 * TILE, 2 * TILE))
        return dot_rows(theirs_x, force), back

    def collect(spots, sums):
        t, one, two = spots
        forward, back = sums
        left_acc[t] = left_acc[t] + forward
        right_acc[one] = right_acc[one] + back[:, :TILE]
        right_acc[two] = right_acc[two] + back[:, TILE:]

    def some_blocks(_, carry):
        block, before = carry
        spots = [before]
        for _ in range(UNROLL + 1):
            spots.append(place(block))
            ahead, block = block, following(block)
        stores = ((parts_a, force_a), (parts_b, force_b))
        for number in range(UNROLL):
            past, held, now = spots[number : number + 3]
            (parts, out), (into, back) = stores[number % 2], stores[1 - number % 2]
            lengths = spread(now)
            sums = gather(past, back)
            forces = work(held, parts)
            into[...] = lengths
            hold(out, forces)
            collect(past, sums)
        return ahead, spots[UNROLL]

    def pairs_of(count):
        return (count + 1) // 2

    if own is None:
        blocks = n_left * pairs_of(n_plate)
    else:
        blocks = first_own * pairs_of(n_plate) + (n_left - first_above) * pairs_of(n_plate + n_own)
        for tile in range(tiles):
            blocks = blocks + jnp.where(tile < n_own, pairs_of(n_plate + tile), 0)
    left_acc[...] = jnp.zeros(left_acc.shape, F32)
    force_b[...] = jnp.zeros(force_b.shape, BF16)
    zero = jnp.int32(0)
    first = (zero, zero)
    parts_a[...] = spread(place(first))
    _, last = lax.fori_loop(
        0, (blocks + UNROLL - 1) // UNROLL, some_blocks, (first, (zero, empty, empty))
    )
    collect(last, gather(last, force_b))

    if own is not None:
        for tile in range(tiles):
            t = first_own + tile
            spot = jnp.maximum(n_plate + n_own - 1 - tile, 0)
            mine = left[t]
            columns = [left_traits[t, trait] for trait in range(3)]
            theirs = [right_traits[spot, 3 + trait : 4 + trait, :] for trait in range(3)]
            force = pair_force(dot(mine, right[spot]), columns, theirs)
            row = lax.broadcasted_iota(jnp.int32, force.shape, 0)
            col = lax.broadcasted_iota(jnp.int32, force.shape, 1)
            high, low = halves(jnp.where((row != col) & (tile < n_own), force, 0.0))
            theirs_x = right_x[spot]
            left_acc[t] = left_acc[t] + dot_rows(theirs_x, high) + dot_rows(theirs_x, low)

    def force(box, acc, tile):
        return jnp.where(tile < box.live, resolve(acc, cut(box.rows, tile)), 0.0)

    def left_force(number, tile):
        acc = left_acc[left_start[number] + tile]
        if own is not None and number == 1:
            acc = acc + right_acc[jnp.maximum(n_plate + n_own - 1 - tile, 0)]
        return force(lefts[number], acc, tile)

    def right_force(number, tile):
        return force(rights[number], right_acc[right_start[number] + tile], tile)

    return left_force, right_force


TOWER = ((0, -1, 0), (0, 0, 0), (0, 1, 0))
BESIDE = (1, 0, 0)
ROW = ((-1, 0, 1), (0, 0, 1), (1, 0, 1))


def lane(tile):
    return slice(tile * TILE, (tile + 1) * TILE)


def tower_boxes(below, own, above):
    return [Box(ref, move) for ref, move in zip((below, own, above), TOWER)]


def feature_kernel(below, own, above, beside, *sides):
    lefts = tower_boxes(below, own, above)
    pack_left(lefts, *sides[:3])
    pack_right([Box(beside, BESIDE)], lefts[1], *sides[3:])


def row_kernel(below, own, above, *refs):
    rights, left_side, out_row, outs = refs[:3], refs[3:6], refs[6], refs[7:10]
    right_side, scratch = refs[10:13], refs[13:]
    lefts = tower_boxes(below, own, above)
    boxes = [Box(ref, move) for ref, move in zip(rights, ROW)]
    pack_right(boxes, None, *right_side)
    left_force, right_force = pair_blocks(lefts, boxes, None, left_side, right_side, scratch)
    for tile in range(own.shape[1] // TILE):
        for number in range(3):
            out_row[3 * number : 3 * number + 3, lane(tile)] = right_force(number, tile)
            outs[number][:, lane(tile)] = left_force(number, tile)


def rest_kernel(below, own, above, beside, *refs):
    left_side, right_side, (add_below, add_own, add_above) = refs[:3], refs[3:6], refs[6:9]
    out_beside, out_own, out_towers, scratch = refs[9], refs[10], refs[11:-6], refs[-6:]
    lefts = tower_boxes(below, own, above)
    left_force, right_force = pair_blocks(
        lefts, [Box(beside, BESIDE)], lefts[1], left_side, right_side, scratch
    )
    for tile in range(own.shape[1] // TILE):
        out_beside[:, lane(tile)] = right_force(0, tile)
        out_own[:, lane(tile)] = left_force(1, tile) + add_own[:, lane(tile)]
        low = left_force(0, tile) + add_below[:, lane(tile)]
        high = left_force(2, tile) + add_above[:, lane(tile)]
        if len(out_towers) == 1:
            out_towers[0][:, lane(tile)] = low + high
        else:
            out_towers[0][:, lane(tile)] = low
            out_towers[1][:, lane(tile)] = high


def merge_kernel(row, beside, own, to_low, to_high, total):
    to_low[...] = row[0:3, :]
    to_high[...] = row[6:9, :] + beside[...]
    total[...] = row[3:6, :] + own[...]


def add_up(parts):
    force = parts[0][...]
    for ref in parts[1:]:
        force = force + ref[...]
    return force


def middle_kernel(record, half, *refs):
    force = add_up(refs[:-2])
    new_record, new_half = refs[-2:]
    velocity = half[...] + HALF_STEP * force
    velocity = velocity + HALF_STEP * force
    new_half[...] = velocity
    new_record[3:8, :] = record[3:8, :]
    new_record[0:3, :] = record[0:3, :] + TIME_STEP * velocity


def last_kernel(record, half, *refs):
    force = add_up(refs[:-3])
    places, velocity, pushing = refs[-3:]
    final = half[...] + HALF_STEP * force
    for axis in range(3):
        places[axis, 0, 0] = record[axis : axis + 1, :]
        velocity[axis, 0, 0] = final[axis : axis + 1, :]
        pushing[axis, 0, 0] = force[axis : axis + 1, :]


VMEM = pltpu.VMEM
SMEM = pltpu.SMEM
LIMIT = 32 * 1024 * 1024


def shape(*dims):
    return jax.ShapeDtypeStruct(dims, F32)


def whole(space=VMEM):
    return pl.BlockSpec(memory_space=space)


def call(kernel, outs, args, pairs=0, scratch=()):
    cost = pl.CostEstimate(
        flops=50 * pairs, bytes_accessed=14 * 32 * args[0].shape[1], transcendentals=2 * pairs
    )
    return pl.pallas_call(
        kernel,
        out_shape=outs,
        in_specs=[whole()] * len(args),
        out_specs=[whole()] * len(outs),
        scratch_shapes=list(scratch),
        compiler_params=pltpu.CompilerParams(vmem_limit_bytes=LIMIT),
        cost_estimate=cost,
    )(*args)


class Ring:
    def __init__(self, name, size):
        self.name, self.size = name, size

    def bring(self, value, offset):
        pairs = [((i + offset) % self.size, i) for i in range(self.size)]
        return lax.ppermute(value, self.name, pairs)

    def give(self, value, offset):
        return self.bring(value, -offset)


def step_forces(record, gx, gy, gz):
    slots = record.shape[1]
    one = shape(3, slots)
    up = gz.bring(record, 1)
    above = gy.bring(record, 1)
    below = above if gy.size == 2 else gy.bring(record, -1)
    beside = gx.bring(record, 1)
    row = (gx.bring(up, -1), up, gx.bring(up, 1))
    tower = (below, record, above)
    tiles = slots // TILE

    def kept(*dims):
        return jax.ShapeDtypeStruct(dims, BF16)

    def sides(boxes):
        count = boxes * tiles + 1
        return kept(count, DEPTH, TILE), kept(count, 16, TILE), shape(count, 8, TILE)

    def scratch(boxes):
        return (
            VMEM((3 * tiles, 16, TILE), F32),
            VMEM((boxes * tiles + 1, 16, TILE), F32),
            VMEM((TILE, 2 * TILE), F32),
            VMEM((TILE, 2 * TILE), F32),
            VMEM((2, TILE, 2 * TILE), BF16),
            VMEM((2, TILE, 2 * TILE), BF16),
        )

    outs = [kept(3 * tiles, TILE, DEPTH), kept(3 * tiles, 16, TILE)]
    outs += [shape(3 * tiles, 3, TILE, TILE), *sides(2)]
    features = call(feature_kernel, outs, (*tower, beside), pairs=slots * slots)
    out_row, *adds = call(
        row_kernel,
        [shape(9, slots), one, one, one],
        (*tower, *row, *features[:3]),
        pairs=9 * slots * slots,
        scratch=[VMEM(side.shape, side.dtype) for side in sides(3)] + [*scratch(3)],
    )
    row_back = gz.give(out_row, 1)
    towers = 1 if gy.size == 2 else 2
    out_beside, out_own, *outs = call(
        rest_kernel,
        [one] * (2 + towers),
        (*tower, beside, *features, *adds),
        pairs=5 * slots * slots,
        scratch=scratch(2),
    )
    back = [gy.give(out, offset) for out, offset in zip(outs, (-1, 1))]
    to_low, to_high, own = call(merge_kernel, [one] * 3, (row_back, out_beside, out_own))
    return [own, gx.give(to_low, -1), gx.give(to_high, 1), *back]


def on_device(axes, positions, velocities, forces, charges, types, counts, epsilon, sigma):
    slots = positions.shape[-1]
    rings = [Ring(name, size) for name, size in zip(("gx", "gy", "gz"), axes)]
    record, half = pl.pallas_call(
        start_kernel,
        out_shape=[shape(8, slots), shape(3, slots)],
        in_specs=[whole(SMEM)] * 3 + [whole()] * 5,
        out_specs=[whole()] * 2,
    )(counts, epsilon, sigma, positions, velocities, forces, charges, types)
    for step in range(STEPS):
        parts = step_forces(record, *rings)
        if step < STEPS - 1:
            outs = [shape(8, slots), shape(3, slots)]
            record, half = call(middle_kernel, outs, (record, half, *parts))
        else:
            outs = call(last_kernel, [shape(*positions.shape)] * 3, (record, half, *parts))
    return tuple(outs)


def solution(mesh):
    boxes = P(None, "gx", "gy", "gz", None)
    slot = P("gx", "gy", "gz", None)
    in_specs = (boxes, boxes, boxes, slot, slot, P("gx", "gy", "gz"), P(), P())
    axes = tuple(mesh.shape[name] for name in ("gx", "gy", "gz"))
    return jax.shard_map(
        functools.partial(on_device, axes),
        mesh=mesh,
        in_specs=in_specs,
        out_specs=(boxes, boxes, boxes),
        check_vma=False,
    )
```

```python
import functools

import jax
import jax.numpy as jnp
from jax import lax
from jax.experimental import pallas as pl
from jax.experimental.pallas import tpu as pltpu
from jax.sharding import PartitionSpec as P

TILE = 128
STEPS = 2

COULOMB = 0.02
SOFTEN = 0.0225
CUTOFF = 0.81
TIME_STEP = 0.05
HALF_STEP = 0.025
REACH = 4.0 * (CUTOFF + SOFTEN)
LOG2_E = 1.4426950408889634
DEPTH = 32
UNROLL = 4
FAR = 2.0**20
SCALE = 1.0 / (4.0 * CUTOFF * CUTOFF)

F32 = jnp.float32
BF16 = jnp.bfloat16


def start_kernel(count, epsilon, sigma, pos, vel, frc, charge, kinds, record, half):
    live_tiles = count[0, 0, 0]
    slots = pos.shape[4]
    live = lax.broadcasted_iota(jnp.int32, (1, slots), 1) < live_tiles * TILE
    kind = kinds[0, 0]
    depth = jnp.zeros((1, slots), F32)
    size = jnp.zeros((1, slots), F32)
    for k in range(epsilon.shape[0]):
        same = kind == k
        depth = jnp.where(same, epsilon[k], depth)
        size = jnp.where(same, sigma[k], size)
    places = []
    for axis in range(3):
        velocity = vel[axis, 0, 0] + HALF_STEP * frc[axis, 0, 0]
        places.append(pos[axis, 0, 0] + TIME_STEP * velocity)
        half[axis : axis + 1, :] = velocity
    record[...] = jnp.concatenate(
        [
            *places,
            jnp.where(live, (2.0 * COULOMB) ** 0.5 * charge[0, 0], 0.0),
            jnp.where(live, 4.0 * jnp.sqrt(depth), 0.0),
            size,
            jnp.full((1, slots), live_tiles.astype(F32)),
            jnp.zeros((1, slots), F32),
        ],
        0,
    )


def split(value):
    high = value.astype(BF16).astype(F32)
    rest = value - high
    middle = rest.astype(BF16).astype(F32)
    return high, middle, rest - middle


def choose(row, *cases):
    value = 0.0
    for test, case in reversed(cases):
        value = jnp.where(test(row), case, value)
    return value


class Box:
    def __init__(self, record, shift):
        rows = record[...]
        row = lax.broadcasted_iota(jnp.int32, rows.shape, 0)
        self.row = row
        moved = [rows + (value - 0.5) if value != 0.5 else rows for value in shift]
        self.rows = choose(
            row,
            (lambda r: r == 0, moved[0]),
            (lambda r: r == 1, moved[1]),
            (lambda r: r == 2, moved[2]),
            (lambda r: r < 6, rows),
        )
        self.live = jnp.max(record[6:7, 0:TILE]).astype(jnp.int32)
        self.pieces = split(self.rows)
        square = jnp.where(row < 3, self.rows * self.rows, 0.0)
        length = jnp.sum(square, axis=0, keepdims=True)
        self.length = jnp.broadcast_to(4.0 * length, rows.shape)

    def sided(self, pieces, first, mark):
        start = 0 if first else 3
        return choose(
            self.row,
            (lambda r: r == start, pieces[0]),
            (lambda r: r == start + 1, pieces[1]),
            (lambda r: r == start + 2, pieces[2]),
            (lambda r: r < 6, 1.0),
            (lambda r: r == 6, mark),
        )

    def pair(self, first, second):
        return choose(
            self.row, (lambda r: r < 3, first), (lambda r: r < 6, pltpu.roll(second, 3, 0))
        )

    def left(self, offset=0.0, mark=0.0):
        high, middle, low = self.pieces
        length = self.sided(split(self.length + (4.0 * SOFTEN + offset)), True, mark)
        pairs = [self.pair(high, high), self.pair(high, middle), self.pair(middle, low)]
        return jnp.concatenate([*pairs, length], 0)

    def right(self, mark=0.0):
        high, middle, low = [-8.0 * piece for piece in self.pieces]
        length = self.sided(split(self.length), False, mark)
        pairs = [self.pair(high, middle), self.pair(low, high), self.pair(middle, high)]
        return jnp.concatenate([*pairs, length], 0).astype(BF16)

    def moments(self, mark=0.0):
        high, middle, low = self.pieces
        upper = choose(
            self.row,
            (lambda r: r < 3, high),
            (lambda r: r == 3, 1.0),
            (lambda r: r < 7, pltpu.roll(middle, 4, 0)),
            (lambda r: r == 7, mark),
        )
        return jnp.concatenate([upper, jnp.where(self.row < 3, low, 0.0)], 0).astype(BF16)


def cut(array, tile):
    return array[:, tile * TILE : (tile + 1) * TILE]


def pair_force(length, mine, theirs):
    inverse = lax.rsqrt(length)
    inverse_sq = inverse * inverse
    screened = (mine[0] * theirs[0]) * (jnp.exp2(length * (inverse * -LOG2_E)) * inverse)
    root = (mine[2] + theirs[2]) * inverse
    ratio = root * root
    cubed = ratio * ratio * ratio
    less = cubed - 1.0
    switch = jnp.maximum(REACH - length, 0.0)
    near = switch * inverse
    nearer = switch * inverse_sq
    charged = screened * (near + nearer + 4.0)
    touching = (mine[1] * theirs[1] * cubed) * (less + (1.5 * nearer) * (cubed + less))
    return switch * (charged + touching)


def halves(force):
    high = force.astype(BF16)
    return high, (force - high.astype(F32)).astype(BF16)


def dot(a, b):
    return jnp.dot(a, b, preferred_element_type=F32)


def dot_rows(a, b):
    return lax.dot_general(a, b, (((1,), (1,)), ((), ())), preferred_element_type=F32)


def resolve(acc, rows, lift=None):
    both = acc[0:8, :] + acc[8:16, :]
    turned = both + pltpu.roll(both, 4, 0)
    force = rows * both[3:4, :] - turned
    if lift is not None:
        row = lax.broadcasted_iota(jnp.int32, force.shape, 0)
        force = force + jnp.where(row == 1, lift, 0.0)
    return (SCALE * force)[0:3, :]


def tower_boxes(tower, folded):
    below, own, above = tower
    if folded:
        return [Box(own, (0, 0, 0)), Box(above, (0, 0, 0))]
    return [Box(ref, (0, move, 0)) for ref, move in zip(tower, (-1, 0, 1))]


def tower_features(tower, boxes, folded):
    if not folded:
        return [[box.left()] for box in boxes]
    lower, upper = [Box(tower[2], (0, move, 0)) for move in (-1, 1)]
    own = [boxes[0].left(), boxes[0].left(offset=FAR)]
    return [own, [lower.left(mark=1.0), upper.left()]]


def pack_left(boxes, features, left, left_x, left_traits):
    start = jnp.int32(0)
    for number, (box, images) in enumerate(zip(boxes, features)):
        rows = jnp.concatenate([*images, box.rows], 0)
        dots = box.moments(mark=1.0 if len(images) == 2 and number == 1 else 0.0)
        traits = DEPTH * len(images) + 3
        for tile in range(dots.shape[1] // TILE):
            columns = cut(rows, tile).T
            for image in range(len(images)):
                part = columns[:, image * DEPTH : (image + 1) * DEPTH]
                left[start + tile, image * TILE : (image + 1) * TILE, :] = part.astype(BF16)
            left_x[start + tile] = cut(dots, tile)
            for trait in range(3):
                column = columns[:, traits + trait : traits + trait + 1]
                left_traits[start + tile, trait] = jnp.broadcast_to(column, (TILE, TILE))
        start = start + box.live


def pack_right(rights, own, right, right_x, right_traits):
    def put(spot, box, features, dots, tile):
        right[spot] = cut(features, tile)
        right_x[spot] = cut(dots, tile)
        right_traits[spot] = cut(box.rows, tile)

    start = jnp.int32(0)
    for box in rights:
        features, dots = box.right(), box.moments()
        tiles = dots.shape[1] // TILE
        for tile in range(tiles):
            put(start + tile, box, features, dots, tile)
        start = start + box.live
    if own is not None:
        box, features, dots = own, own.right(mark=FAR), own.moments()
        first = start
        for tile in range(tiles):

            @pl.when(tile < own.live)
            def _():
                put(first + own.live - 1 - tile, own, features, dots, tile)

        start = start + own.live
    put(start, box, features, dots, 0)
    right_traits[start] = jnp.zeros(right_traits.shape[1:], F32)


def starts(boxes):
    spots = [jnp.int32(0)]
    for box in boxes:
        spots.append(spots[-1] + box.live)
    return spots


def pair_blocks(lefts, rights, own, left_side, right_side, scratch):
    folded = len(lefts) == 2
    middle = 0 if folded else 1
    left, left_x, left_traits = left_side
    right, right_x, right_traits = right_side
    left_acc, right_acc, left_up, right_up, parts_a, parts_b, force_a, force_b = scratch
    tiles = lefts[0].rows.shape[1] // TILE
    left_start, right_start = starts(lefts), starts(rights)
    first_own, first_above, n_left = left_start[middle], left_start[middle + 1], left_start[-1]
    n_plate = right_start[-1]
    n_own = jnp.int32(0) if own is None else own.live
    empty = n_plate + n_own
    right_acc[...] = jnp.zeros(right_acc.shape, F32)

    def extent(t):
        if own is None:
            return n_plate
        own_part = jnp.where(t < first_above, n_own - 1 - (t - first_own), n_own)
        return n_plate + jnp.where(t < first_own, 0, own_part)

    def following(block):
        t, p = block
        step = 2 * p + 2 < extent(t)
        return jnp.where(step, t, jnp.minimum(t + 1, n_left)), jnp.where(step, p + 1, 0)

    def place(block):
        t, p = block
        inside = t < n_left
        one = jnp.where(inside, 2 * p, empty)
        two = jnp.where(inside & (2 * p + 1 < extent(t)), 2 * p + 1, empty)
        return jnp.where(inside, t, 0), one, two

    def spread(spots):
        t, one, two = spots
        return dot(left[t], jnp.concatenate([right[one], right[two]], 1))

    def work(spots, parts):
        t, one, two = spots
        mine = [left_traits[t, trait] for trait in range(3)]
        forces, uppers = [], []
        for lanes, spot in ((slice(0, TILE), one), (slice(TILE, 2 * TILE), two)):
            theirs = [right_traits[spot, 3 + trait : 4 + trait, :] for trait in range(3)]
            length = parts[0:TILE, lanes]
            if folded:
                upper = parts[TILE : 2 * TILE, lanes]
                force = pair_force(jnp.minimum(length, upper), mine, theirs)
                uppers.append(jnp.where(upper < length, force, 0.0))
            else:
                force = pair_force(length, mine, theirs)
            forces.append(halves(force))
        return forces, uppers

    def raise_up(spots, uppers):
        t, one, two = spots
        left_up[t] = left_up[t] + (uppers[0] + uppers[1])
        for spot, upper in zip((one, two), uppers):
            right_up[spot] = right_up[spot] + jnp.sum(upper.reshape(TILE // 8, 8, TILE), axis=0)

    def hold(split_force, forces):
        for side, (high, low) in enumerate(forces):
            split_force[0, :, side * TILE : (side + 1) * TILE] = high
            split_force[1, :, side * TILE : (side + 1) * TILE] = low

    def gather(spots, split_force):
        t, one, two = spots
        theirs_x = [right_x[one], right_x[two]]
        theirs_x = jnp.concatenate([*theirs_x, *theirs_x], 1)
        mine_x = jnp.concatenate([left_x[t], left_x[t]], 1)
        force = jnp.concatenate([split_force[0], split_force[1]], 1)
        back = dot(mine_x, split_force[...].reshape(2 * TILE, 2 * TILE))
        return dot_rows(theirs_x, force), back

    def collect(spots, sums):
        t, one, two = spots
        forward, back = sums
        left_acc[t] = left_acc[t] + forward
        right_acc[one] = right_acc[one] + back[:, :TILE]
        right_acc[two] = right_acc[two] + back[:, TILE:]

    def some_blocks(_, carry):
        block, before = carry
        spots = [before]
        for _ in range(UNROLL + 1):
            spots.append(place(block))
            ahead, block = block, following(block)
        stores = ((parts_a, force_a), (parts_b, force_b))
        for number in range(UNROLL):
            past, held, now = spots[number : number + 3]
            (parts, out), (into, back) = stores[number % 2], stores[1 - number % 2]
            lengths = spread(now)
            sums = gather(past, back)
            forces, uppers = work(held, parts)
            into[...] = lengths
            hold(out, forces)
            collect(past, sums)
            if folded:
                raise_up(held, uppers)
        return ahead, spots[UNROLL]

    def pairs_of(count):
        return (count + 1) // 2

    if own is None:
        blocks = n_left * pairs_of(n_plate)
    else:
        blocks = first_own * pairs_of(n_plate) + (n_left - first_above) * pairs_of(n_plate + n_own)
        for tile in range(tiles):
            blocks = blocks + jnp.where(tile < n_own, pairs_of(n_plate + tile), 0)
    left_acc[...] = jnp.zeros(left_acc.shape, F32)
    left_up[...] = jnp.zeros(left_up.shape, F32)
    right_up[...] = jnp.zeros(right_up.shape, F32)
    force_b[...] = jnp.zeros(force_b.shape, BF16)
    zero = jnp.int32(0)
    first = (zero, zero)
    parts_a[...] = spread(place(first))
    _, last = lax.fori_loop(
        0, (blocks + UNROLL - 1) // UNROLL, some_blocks, (first, (zero, empty, empty))
    )
    collect(last, gather(last, force_b))

    if own is not None:
        for tile in range(tiles):
            t = first_own + tile
            spot = jnp.maximum(n_plate + n_own - 1 - tile, 0)
            mine = left[t, 0:TILE, :]
            columns = [left_traits[t, trait] for trait in range(3)]
            theirs = [right_traits[spot, 3 + trait : 4 + trait, :] for trait in range(3)]
            force = pair_force(dot(mine, right[spot]), columns, theirs)
            row = lax.broadcasted_iota(jnp.int32, force.shape, 0)
            col = lax.broadcasted_iota(jnp.int32, force.shape, 1)
            high, low = halves(jnp.where((row != col) & (tile < n_own), force, 0.0))
            theirs_x = right_x[spot]
            left_acc[t] = left_acc[t] + dot_rows(theirs_x, high) + dot_rows(theirs_x, low)

    def alive(box, tile, force):
        return jnp.where(tile < box.live, force, 0.0)

    def left_force(number, tile):
        box, spot = lefts[number], left_start[number] + tile
        acc, lift = left_acc[spot], None
        if folded and number == 1:
            raised = jnp.sum(left_up[spot].T, axis=0, keepdims=True)
            lift = 2.0 * raised - acc[3:4, :]
        force = resolve(acc, cut(box.rows, tile), lift)
        if own is not None and number == middle:
            force = force + pushed(box, jnp.maximum(n_plate + n_own - 1 - tile, 0), tile)
        return alive(box, tile, force)

    def pushed(box, spot, tile):
        acc, lift = right_acc[spot], None
        if folded:
            raised = jnp.sum(right_up[spot], axis=0, keepdims=True)
            lift = acc[7:8, :] - 2.0 * raised
        return resolve(acc, cut(box.rows, tile), lift)

    def right_force(number, tile):
        box = rights[number]
        return alive(box, tile, pushed(box, right_start[number] + tile, tile))

    return left_force, right_force


BESIDE = (1, 0, 0)
ROW = ((-1, 0, 1), (0, 0, 1), (1, 0, 1))


def lane(tile):
    return slice(tile * TILE, (tile + 1) * TILE)


def feature_kernel(folded, below, own, above, beside, *sides):
    tower = (below, own, above)
    lefts = tower_boxes(tower, folded)
    pack_left(lefts, tower_features(tower, lefts, folded), *sides[:3])
    pack_right([Box(beside, BESIDE)], lefts[0 if folded else 1], *sides[3:])


def row_kernel(folded, below, own, above, *refs):
    rights, left_side, out_row, refs = refs[:3], refs[3:6], refs[6], refs[7:]
    lefts = tower_boxes((below, own, above), folded)
    outs, refs = refs[: len(lefts)], refs[len(lefts) :]
    right_side, scratch = refs[:3], refs[3:]
    boxes = [Box(ref, move) for ref, move in zip(rights, ROW)]
    pack_right(boxes, None, *right_side)
    left_force, right_force = pair_blocks(lefts, boxes, None, left_side, right_side, scratch)
    for tile in range(own.shape[1] // TILE):
        for number in range(3):
            out_row[3 * number : 3 * number + 3, lane(tile)] = right_force(number, tile)
        for number, out in enumerate(outs):
            out[:, lane(tile)] = left_force(number, tile)


def rest_kernel(folded, below, own, above, beside, *refs):
    left_side, right_side, refs = refs[:3], refs[3:6], refs[6:]
    lefts = tower_boxes((below, own, above), folded)
    adds, refs = refs[: len(lefts)], refs[len(lefts) :]
    out_beside, outs, scratch = refs[0], refs[1 : 1 + len(lefts)], refs[1 + len(lefts) :]
    left_force, right_force = pair_blocks(
        lefts, [Box(beside, BESIDE)], lefts[0 if folded else 1], left_side, right_side, scratch
    )
    for tile in range(own.shape[1] // TILE):
        out_beside[:, lane(tile)] = right_force(0, tile)
        for number, (out, add) in enumerate(zip(outs, adds)):
            out[:, lane(tile)] = left_force(number, tile) + add[:, lane(tile)]


def merge_kernel(row, beside, own, to_low, to_high, total):
    to_low[...] = row[0:3, :]
    to_high[...] = row[6:9, :] + beside[...]
    total[...] = row[3:6, :] + own[...]


def add_up(parts):
    force = parts[0][...]
    for ref in parts[1:]:
        force = force + ref[...]
    return force


def middle_kernel(record, half, *refs):
    force = add_up(refs[:-2])
    new_record, new_half = refs[-2:]
    velocity = half[...] + HALF_STEP * force
    velocity = velocity + HALF_STEP * force
    new_half[...] = velocity
    new_record[3:8, :] = record[3:8, :]
    new_record[0:3, :] = record[0:3, :] + TIME_STEP * velocity


def last_kernel(record, half, *refs):
    force = add_up(refs[:-3])
    places, velocity, pushing = refs[-3:]
    final = half[...] + HALF_STEP * force
    for axis in range(3):
        places[axis, 0, 0] = record[axis : axis + 1, :]
        velocity[axis, 0, 0] = final[axis : axis + 1, :]
        pushing[axis, 0, 0] = force[axis : axis + 1, :]


VMEM = pltpu.VMEM
SMEM = pltpu.SMEM
LIMIT = 32 * 1024 * 1024


def shape(*dims):
    return jax.ShapeDtypeStruct(dims, F32)


def whole(space=VMEM):
    return pl.BlockSpec(memory_space=space)


def call(kernel, outs, args, pairs=0, scratch=()):
    cost = pl.CostEstimate(
        flops=50 * pairs, bytes_accessed=14 * 32 * args[0].shape[1], transcendentals=2 * pairs
    )
    return pl.pallas_call(
        kernel,
        out_shape=outs,
        in_specs=[whole()] * len(args),
        out_specs=[whole()] * len(outs),
        scratch_shapes=list(scratch),
        compiler_params=pltpu.CompilerParams(vmem_limit_bytes=LIMIT),
        cost_estimate=cost,
    )(*args)


class Ring:
    def __init__(self, name, size):
        self.name, self.size = name, size

    def bring(self, value, offset):
        pairs = [((i + offset) % self.size, i) for i in range(self.size)]
        return lax.ppermute(value, self.name, pairs)

    def give(self, value, offset):
        return self.bring(value, -offset)


def step_forces(record, gx, gy, gz):
    slots = record.shape[1]
    one = shape(3, slots)
    up = gz.bring(record, 1)
    above = gy.bring(record, 1)
    below = above if gy.size == 2 else gy.bring(record, -1)
    beside = gx.bring(record, 1)
    row = (gx.bring(up, -1), up, gx.bring(up, 1))
    tower = (below, record, above)
    tiles = slots // TILE
    folded = gy.size == 2
    lefts, images = (2, 2) if folded else (3, 1)

    def kept(*dims):
        return jax.ShapeDtypeStruct(dims, BF16)

    def sides(boxes):
        count = boxes * tiles + 1
        return kept(count, DEPTH, TILE), kept(count, 16, TILE), shape(count, 8, TILE)

    def scratch(boxes):
        return (
            VMEM((lefts * tiles, 16, TILE), F32),
            VMEM((boxes * tiles + 1, 16, TILE), F32),
            VMEM((lefts * tiles if folded else 1, TILE, TILE), F32),
            VMEM((boxes * tiles + 1, 8, TILE), F32),
            VMEM((images * TILE, 2 * TILE), F32),
            VMEM((images * TILE, 2 * TILE), F32),
            VMEM((2, TILE, 2 * TILE), BF16),
            VMEM((2, TILE, 2 * TILE), BF16),
        )

    outs = [kept(lefts * tiles, images * TILE, DEPTH), kept(lefts * tiles, 16, TILE)]
    outs += [shape(lefts * tiles, 3, TILE, TILE), *sides(2)]
    features = call(
        functools.partial(feature_kernel, folded), outs, (*tower, beside), pairs=slots * slots
    )
    out_row, *adds = call(
        functools.partial(row_kernel, folded),
        [shape(9, slots)] + [one] * lefts,
        (*tower, *row, *features[:3]),
        pairs=3 * lefts * slots * slots,
        scratch=[VMEM(side.shape, side.dtype) for side in sides(3)] + [*scratch(3)],
    )
    row_back = gz.give(out_row, 1)
    out_beside, *outs = call(
        functools.partial(rest_kernel, folded),
        [one] * (1 + lefts),
        (*tower, beside, *features, *adds),
        pairs=4 * slots * slots,
        scratch=scratch(2),
    )
    if folded:
        out_own, out_other = outs
        back = [gy.give(out_other, 1)]
    else:
        out_low, out_own, out_high = outs
        back = [gy.give(out_low, -1), gy.give(out_high, 1)]
    to_low, to_high, own = call(merge_kernel, [one] * 3, (row_back, out_beside, out_own))
    return [own, gx.give(to_low, -1), gx.give(to_high, 1), *back]


def on_device(axes, positions, velocities, forces, charges, types, counts, epsilon, sigma):
    slots = positions.shape[-1]
    rings = [Ring(name, size) for name, size in zip(("gx", "gy", "gz"), axes)]
    record, half = pl.pallas_call(
        start_kernel,
        out_shape=[shape(8, slots), shape(3, slots)],
        in_specs=[whole(SMEM)] * 3 + [whole()] * 5,
        out_specs=[whole()] * 2,
    )(counts, epsilon, sigma, positions, velocities, forces, charges, types)
    for step in range(STEPS):
        parts = step_forces(record, *rings)
        if step < STEPS - 1:
            outs = [shape(8, slots), shape(3, slots)]
            record, half = call(middle_kernel, outs, (record, half, *parts))
        else:
            outs = call(last_kernel, [shape(*positions.shape)] * 3, (record, half, *parts))
    return tuple(outs)


def solution(mesh):
    boxes = P(None, "gx", "gy", "gz", None)
    slot = P("gx", "gy", "gz", None)
    in_specs = (boxes, boxes, boxes, slot, slot, P("gx", "gy", "gz"), P(), P())
    axes = tuple(mesh.shape[name] for name in ("gx", "gy", "gz"))
    return jax.shard_map(
        functools.partial(on_device, axes),
        mesh=mesh,
        in_specs=in_specs,
        out_specs=(boxes, boxes, boxes),
        check_vma=False,
    )
```

```python
import functools

import jax
import jax.numpy as jnp
from jax import lax
from jax.experimental import pallas as pl
from jax.experimental.pallas import tpu as pltpu
from jax.sharding import PartitionSpec as P

TILE = 128
STEPS = 2

COULOMB = 0.02
SOFTEN = 0.0225
CUTOFF = 0.81
TIME_STEP = 0.05
HALF_STEP = 0.025
REACH = 4.0 * (CUTOFF + SOFTEN)
LOG2_E = 1.4426950408889634
DEPTH = 32
UNROLL = 4
FAR = 2.0**20
SCALE = 1.0 / (4.0 * CUTOFF * CUTOFF)

F32 = jnp.float32
BF16 = jnp.bfloat16


def start_kernel(count, epsilon, sigma, pos, vel, frc, charge, kinds, record, half):
    live_tiles = count[0, 0, 0]
    slots = pos.shape[4]
    live = lax.broadcasted_iota(jnp.int32, (1, slots), 1) < live_tiles * TILE
    kind = kinds[0, 0]
    depth = jnp.zeros((1, slots), F32)
    size = jnp.zeros((1, slots), F32)
    for k in range(epsilon.shape[0]):
        same = kind == k
        depth = jnp.where(same, epsilon[k], depth)
        size = jnp.where(same, sigma[k], size)
    places = []
    for axis in range(3):
        velocity = vel[axis, 0, 0] + HALF_STEP * frc[axis, 0, 0]
        places.append(pos[axis, 0, 0] + TIME_STEP * velocity)
        half[axis : axis + 1, :] = velocity
    record[...] = jnp.concatenate(
        [
            *places,
            jnp.where(live, (2.0 * COULOMB) ** 0.5 * charge[0, 0], 0.0),
            jnp.where(live, 4.0 * jnp.sqrt(depth), 0.0),
            size,
            jnp.full((1, slots), live_tiles.astype(F32)),
            jnp.zeros((1, slots), F32),
        ],
        0,
    )


def split(value):
    high = value.astype(BF16).astype(F32)
    rest = value - high
    middle = rest.astype(BF16).astype(F32)
    return high, middle, rest - middle


def choose(row, *cases):
    value = 0.0
    for test, case in reversed(cases):
        value = jnp.where(test(row), case, value)
    return value


class Box:
    def __init__(self, record, shift):
        rows = record[...]
        row = lax.broadcasted_iota(jnp.int32, rows.shape, 0)
        self.row = row
        moved = [rows + (value - 0.5) if value != 0.5 else rows for value in shift]
        self.rows = choose(
            row,
            (lambda r: r == 0, moved[0]),
            (lambda r: r == 1, moved[1]),
            (lambda r: r == 2, moved[2]),
            (lambda r: r < 6, rows),
        )
        self.live = jnp.max(record[6:7, 0:TILE]).astype(jnp.int32)
        self.pieces = split(self.rows)
        square = jnp.where(row < 3, self.rows * self.rows, 0.0)
        length = jnp.sum(square, axis=0, keepdims=True)
        self.length = jnp.broadcast_to(4.0 * length, rows.shape)

    def sided(self, pieces, first):
        start = 0 if first else 3
        return choose(
            self.row,
            (lambda r: r == start, pieces[0]),
            (lambda r: r == start + 1, pieces[1]),
            (lambda r: r == start + 2, pieces[2]),
            (lambda r: r < 6, 1.0),
        )

    def pair(self, first, second):
        return choose(
            self.row, (lambda r: r < 3, first), (lambda r: r < 6, pltpu.roll(second, 3, 0))
        )

    def left(self):
        high, middle, low = self.pieces
        length = self.sided(split(self.length + 4.0 * SOFTEN), True)
        pairs = [self.pair(high, high), self.pair(high, middle), self.pair(middle, low)]
        return jnp.concatenate([*pairs, length], 0)

    def right(self):
        high, middle, low = [-8.0 * piece for piece in self.pieces]
        length = self.sided(split(self.length), False)
        pairs = [self.pair(high, middle), self.pair(low, high), self.pair(middle, high)]
        return jnp.concatenate([*pairs, length], 0).astype(BF16)

    def traits(self, slope, start):
        return jnp.where(self.row == 6, slope * self.rows[1:2, :] + start, self.rows)

    def moments(self):
        high, middle, low = self.pieces
        upper = choose(
            self.row,
            (lambda r: r < 3, high),
            (lambda r: r == 3, 1.0),
            (lambda r: r < 7, pltpu.roll(middle, 4, 0)),
        )
        return jnp.concatenate([upper, jnp.where(self.row < 3, low, 0.0)], 0).astype(BF16)


def cut(array, tile):
    return array[:, tile * TILE : (tile + 1) * TILE]


def pair_force(length, mine, theirs):
    inverse = lax.rsqrt(length)
    inverse_sq = inverse * inverse
    screened = (mine[0] * theirs[0]) * (jnp.exp2(length * (inverse * -LOG2_E)) * inverse)
    root = (mine[2] + theirs[2]) * inverse
    ratio = root * root
    cubed = ratio * ratio * ratio
    less = cubed - 1.0
    switch = jnp.maximum(REACH - length, 0.0)
    near = switch * inverse
    nearer = switch * inverse_sq
    charged = screened * (near + nearer + 4.0)
    touching = (mine[1] * theirs[1] * cubed) * (less + (1.5 * nearer) * (cubed + less))
    return switch * (charged + touching)


def halves(force):
    high = force.astype(BF16)
    return high, (force - high.astype(F32)).astype(BF16)


def dot(a, b):
    return jnp.dot(a, b, preferred_element_type=F32)


def dot_rows(a, b):
    return lax.dot_general(a, b, (((1,), (1,)), ((), ())), preferred_element_type=F32)


def resolve(acc, rows, lift=None):
    both = acc[0:8, :] + acc[8:16, :]
    turned = both + pltpu.roll(both, 4, 0)
    force = rows * both[3:4, :] - turned
    if lift is not None:
        row = lax.broadcasted_iota(jnp.int32, force.shape, 0)
        force = force + jnp.where(row == 1, lift, 0.0)
    return (SCALE * force)[0:3, :]


def tower_boxes(tower, folded):
    below, own, above = tower
    if folded:
        return [Box(own, (0, 0, 0)), Box(above, (0, 1, 0))]
    return [Box(ref, (0, move, 0)) for ref, move in zip(tower, (-1, 0, 1))]


def pack_left(boxes, left, left_x, left_traits):
    start = jnp.int32(0)
    for number, box in enumerate(boxes):
        slope = (-16.0, 16.0) if len(boxes) == 2 and number == 1 else (0.0, FAR)
        rows, dots = jnp.concatenate([box.left(), box.traits(*slope)], 0), box.moments()
        for tile in range(dots.shape[1] // TILE):
            columns = cut(rows, tile).T
            left[start + tile] = columns[:, :DEPTH].astype(BF16)
            left_x[start + tile] = cut(dots, tile)
            for trait in range(left_traits.shape[1]):
                column = columns[:, DEPTH + 3 + trait : DEPTH + 4 + trait]
                left_traits[start + tile, trait] = jnp.broadcast_to(column, (TILE, TILE))
        start = start + box.live


def pack_right(rights, own, right, right_x, right_traits):
    def put(spot, traits, features, dots, tile):
        right[spot] = cut(features, tile)
        right_x[spot] = cut(dots, tile)
        right_traits[spot] = cut(traits, tile)

    start = jnp.int32(0)
    for box in rights:
        traits, features, dots = box.traits(16.0, 0.0), box.right(), box.moments()
        tiles = dots.shape[1] // TILE
        for tile in range(tiles):
            put(start + tile, traits, features, dots, tile)
        start = start + box.live
    if own is not None:
        traits, features, dots = own.traits(0.0, FAR), own.right(), own.moments()
        first = start
        for tile in range(tiles):

            @pl.when(tile < own.live)
            def _():
                put(first + own.live - 1 - tile, traits, features, dots, tile)

        start = start + own.live
    put(start, traits, features, dots, 0)
    row = lax.broadcasted_iota(jnp.int32, right_traits.shape[1:], 0)
    right_traits[start] = jnp.where(row == 6, FAR, 0.0)


def starts(boxes):
    spots = [jnp.int32(0)]
    for box in boxes:
        spots.append(spots[-1] + box.live)
    return spots


def pair_blocks(lefts, rights, own, left_side, right_side, scratch):
    folded = len(lefts) == 2
    middle = 0 if folded else 1
    left, left_x, left_traits = left_side
    right, right_x, right_traits = right_side
    left_acc, right_acc, left_low, right_low, parts_a, parts_b, force_a, force_b = scratch
    tiles = lefts[0].rows.shape[1] // TILE
    left_start, right_start = starts(lefts), starts(rights)
    first_own, first_above, n_left = left_start[middle], left_start[middle + 1], left_start[-1]
    n_plate = right_start[-1]
    n_own = jnp.int32(0) if own is None else own.live
    empty = n_plate + n_own
    right_acc[...] = jnp.zeros(right_acc.shape, F32)

    def extent(t):
        if own is None:
            return n_plate
        own_part = jnp.where(t < first_above, n_own - 1 - (t - first_own), n_own)
        return n_plate + jnp.where(t < first_own, 0, own_part)

    def following(block):
        t, p = block
        step = 2 * p + 2 < extent(t)
        return jnp.where(step, t, jnp.minimum(t + 1, n_left)), jnp.where(step, p + 1, 0)

    def place(block):
        t, p = block
        inside = t < n_left
        one = jnp.where(inside, 2 * p, empty)
        two = jnp.where(inside & (2 * p + 1 < extent(t)), 2 * p + 1, empty)
        return jnp.where(inside, t, 0), one, two

    def spread(spots):
        t, one, two = spots
        return dot(left[t], jnp.concatenate([right[one], right[two]], 1))

    def work(spots, parts):
        t, one, two = spots
        count = 4 if folded else 3
        mine = [left_traits[t, trait] for trait in range(count)]
        forces, lowers = [], []
        for lanes, spot in ((slice(0, TILE), one), (slice(TILE, 2 * TILE), two)):
            theirs = [right_traits[spot, 3 + trait : 4 + trait, :] for trait in range(count)]
            length = parts[:, lanes]
            if folded:
                lower = mine[3] + theirs[3]
                force = pair_force(length + jnp.minimum(lower, 0.0), mine, theirs)
                lowers.append(jnp.where(lower < 0.0, force, 0.0))
            else:
                force = pair_force(length, mine, theirs)
            forces.append(halves(force))
        return forces, lowers

    def take_down(spots, lowers):
        t, one, two = spots
        left_low[t] = left_low[t] + (lowers[0] + lowers[1])
        for spot, lower in zip((one, two), lowers):
            right_low[spot] = right_low[spot] + jnp.sum(lower.reshape(TILE // 8, 8, TILE), axis=0)

    def hold(split_force, forces):
        for side, (high, low) in enumerate(forces):
            split_force[0, :, side * TILE : (side + 1) * TILE] = high
            split_force[1, :, side * TILE : (side + 1) * TILE] = low

    def gather(spots, split_force):
        t, one, two = spots
        theirs_x = [right_x[one], right_x[two]]
        theirs_x = jnp.concatenate([*theirs_x, *theirs_x], 1)
        mine_x = jnp.concatenate([left_x[t], left_x[t]], 1)
        force = jnp.concatenate([split_force[0], split_force[1]], 1)
        back = dot(mine_x, split_force[...].reshape(2 * TILE, 2 * TILE))
        return dot_rows(theirs_x, force), back

    def collect(spots, sums):
        t, one, two = spots
        forward, back = sums
        left_acc[t] = left_acc[t] + forward
        right_acc[one] = right_acc[one] + back[:, :TILE]
        right_acc[two] = right_acc[two] + back[:, TILE:]

    def some_blocks(_, carry):
        block, before = carry
        spots = [before]
        for _ in range(UNROLL + 1):
            spots.append(place(block))
            ahead, block = block, following(block)
        stores = ((parts_a, force_a), (parts_b, force_b))
        for number in range(UNROLL):
            past, held, now = spots[number : number + 3]
            (parts, out), (into, back) = stores[number % 2], stores[1 - number % 2]
            lengths = spread(now)
            sums = gather(past, back)
            forces, lowers = work(held, parts)
            into[...] = lengths
            hold(out, forces)
            collect(past, sums)
            if folded:
                take_down(held, lowers)
        return ahead, spots[UNROLL]

    def pairs_of(count):
        return (count + 1) // 2

    if own is None:
        blocks = n_left * pairs_of(n_plate)
    else:
        blocks = first_own * pairs_of(n_plate) + (n_left - first_above) * pairs_of(n_plate + n_own)
        for tile in range(tiles):
            blocks = blocks + jnp.where(tile < n_own, pairs_of(n_plate + tile), 0)
    left_acc[...] = jnp.zeros(left_acc.shape, F32)
    left_low[...] = jnp.zeros(left_low.shape, F32)
    right_low[...] = jnp.zeros(right_low.shape, F32)
    force_b[...] = jnp.zeros(force_b.shape, BF16)
    zero = jnp.int32(0)
    first = (zero, zero)
    parts_a[...] = spread(place(first))
    _, last = lax.fori_loop(
        0, (blocks + UNROLL - 1) // UNROLL, some_blocks, (first, (zero, empty, empty))
    )
    collect(last, gather(last, force_b))

    if own is not None:
        for tile in range(tiles):
            t = first_own + tile
            spot = jnp.maximum(n_plate + n_own - 1 - tile, 0)
            mine = left[t]
            columns = [left_traits[t, trait] for trait in range(3)]
            theirs = [right_traits[spot, 3 + trait : 4 + trait, :] for trait in range(3)]
            force = pair_force(dot(mine, right[spot]), columns, theirs)
            row = lax.broadcasted_iota(jnp.int32, force.shape, 0)
            col = lax.broadcasted_iota(jnp.int32, force.shape, 1)
            high, low = halves(jnp.where((row != col) & (tile < n_own), force, 0.0))
            theirs_x = right_x[spot]
            left_acc[t] = left_acc[t] + dot_rows(theirs_x, high) + dot_rows(theirs_x, low)

    def alive(box, tile, force):
        return jnp.where(tile < box.live, force, 0.0)

    def left_force(number, tile):
        box, spot = lefts[number], left_start[number] + tile
        acc, lift = left_acc[spot], None
        if folded and number == 1:
            lift = -2.0 * jnp.sum(left_low[spot].T, axis=0, keepdims=True)
        force = resolve(acc, cut(box.rows, tile), lift)
        if own is not None and number == middle:
            force = force + pushed(box, jnp.maximum(n_plate + n_own - 1 - tile, 0), tile)
        return alive(box, tile, force)

    def pushed(box, spot, tile):
        acc, lift = right_acc[spot], None
        if folded:
            lift = 2.0 * jnp.sum(right_low[spot], axis=0, keepdims=True)
        return resolve(acc, cut(box.rows, tile), lift)

    def right_force(number, tile):
        box = rights[number]
        return alive(box, tile, pushed(box, right_start[number] + tile, tile))

    return left_force, right_force


BESIDE = (1, 0, 0)
ROW = ((-1, 0, 1), (0, 0, 1), (1, 0, 1))


def lane(tile):
    return slice(tile * TILE, (tile + 1) * TILE)


def feature_kernel(folded, below, own, above, beside, *sides):
    lefts = tower_boxes((below, own, above), folded)
    pack_left(lefts, *sides[:3])
    pack_right([Box(beside, BESIDE)], lefts[0 if folded else 1], *sides[3:])


def row_kernel(folded, below, own, above, *refs):
    rights, left_side, out_row, refs = refs[:3], refs[3:6], refs[6], refs[7:]
    lefts = tower_boxes((below, own, above), folded)
    outs, refs = refs[: len(lefts)], refs[len(lefts) :]
    right_side, scratch = refs[:3], refs[3:]
    boxes = [Box(ref, move) for ref, move in zip(rights, ROW)]
    pack_right(boxes, None, *right_side)
    left_force, right_force = pair_blocks(lefts, boxes, None, left_side, right_side, scratch)
    for tile in range(own.shape[1] // TILE):
        for number in range(3):
            out_row[3 * number : 3 * number + 3, lane(tile)] = right_force(number, tile)
        for number, out in enumerate(outs):
            out[:, lane(tile)] = left_force(number, tile)


def rest_kernel(folded, below, own, above, beside, *refs):
    left_side, right_side, refs = refs[:3], refs[3:6], refs[6:]
    lefts = tower_boxes((below, own, above), folded)
    adds, refs = refs[: len(lefts)], refs[len(lefts) :]
    out_beside, outs, scratch = refs[0], refs[1 : 1 + len(lefts)], refs[1 + len(lefts) :]
    left_force, right_force = pair_blocks(
        lefts, [Box(beside, BESIDE)], lefts[0 if folded else 1], left_side, right_side, scratch
    )
    for tile in range(own.shape[1] // TILE):
        out_beside[:, lane(tile)] = right_force(0, tile)
        for number, (out, add) in enumerate(zip(outs, adds)):
            out[:, lane(tile)] = left_force(number, tile) + add[:, lane(tile)]


def merge_kernel(row, beside, own, to_low, to_high, total):
    to_low[...] = row[0:3, :]
    to_high[...] = row[6:9, :] + beside[...]
    total[...] = row[3:6, :] + own[...]


def add_up(parts):
    force = parts[0][...]
    for ref in parts[1:]:
        force = force + ref[...]
    return force


def middle_kernel(record, half, *refs):
    force = add_up(refs[:-2])
    new_record, new_half = refs[-2:]
    velocity = half[...] + HALF_STEP * force
    velocity = velocity + HALF_STEP * force
    new_half[...] = velocity
    new_record[3:8, :] = record[3:8, :]
    new_record[0:3, :] = record[0:3, :] + TIME_STEP * velocity


def last_kernel(record, half, *refs):
    force = add_up(refs[:-3])
    places, velocity, pushing = refs[-3:]
    final = half[...] + HALF_STEP * force
    for axis in range(3):
        places[axis, 0, 0] = record[axis : axis + 1, :]
        velocity[axis, 0, 0] = final[axis : axis + 1, :]
        pushing[axis, 0, 0] = force[axis : axis + 1, :]


VMEM = pltpu.VMEM
SMEM = pltpu.SMEM
LIMIT = 32 * 1024 * 1024


def shape(*dims):
    return jax.ShapeDtypeStruct(dims, F32)


def whole(space=VMEM):
    return pl.BlockSpec(memory_space=space)


def call(kernel, outs, args, pairs=0, scratch=()):
    cost = pl.CostEstimate(
        flops=50 * pairs, bytes_accessed=14 * 32 * args[0].shape[1], transcendentals=2 * pairs
    )
    return pl.pallas_call(
        kernel,
        out_shape=outs,
        in_specs=[whole()] * len(args),
        out_specs=[whole()] * len(outs),
        scratch_shapes=list(scratch),
        compiler_params=pltpu.CompilerParams(vmem_limit_bytes=LIMIT),
        cost_estimate=cost,
    )(*args)


class Ring:
    def __init__(self, name, size):
        self.name, self.size = name, size

    def bring(self, value, offset):
        pairs = [((i + offset) % self.size, i) for i in range(self.size)]
        return lax.ppermute(value, self.name, pairs)

    def give(self, value, offset):
        return self.bring(value, -offset)


def step_forces(record, gx, gy, gz):
    slots = record.shape[1]
    one = shape(3, slots)
    up = gz.bring(record, 1)
    above = gy.bring(record, 1)
    below = above if gy.size == 2 else gy.bring(record, -1)
    beside = gx.bring(record, 1)
    row = (gx.bring(up, -1), up, gx.bring(up, 1))
    tower = (below, record, above)
    tiles = slots // TILE
    folded = gy.size == 2
    lefts, traits = (2, 4) if folded else (3, 3)

    def kept(*dims):
        return jax.ShapeDtypeStruct(dims, BF16)

    def sides(boxes):
        count = boxes * tiles + 1
        return kept(count, DEPTH, TILE), kept(count, 16, TILE), shape(count, 8, TILE)

    def scratch(boxes):
        return (
            VMEM((lefts * tiles, 16, TILE), F32),
            VMEM((boxes * tiles + 1, 16, TILE), F32),
            VMEM((lefts * tiles if folded else 1, TILE, TILE), F32),
            VMEM((boxes * tiles + 1, 8, TILE), F32),
            VMEM((TILE, 2 * TILE), F32),
            VMEM((TILE, 2 * TILE), F32),
            VMEM((2, TILE, 2 * TILE), BF16),
            VMEM((2, TILE, 2 * TILE), BF16),
        )

    outs = [kept(lefts * tiles, TILE, DEPTH), kept(lefts * tiles, 16, TILE)]
    outs += [shape(lefts * tiles, traits, TILE, TILE), *sides(2)]
    features = call(
        functools.partial(feature_kernel, folded), outs, (*tower, beside), pairs=slots * slots
    )
    out_row, *adds = call(
        functools.partial(row_kernel, folded),
        [shape(9, slots)] + [one] * lefts,
        (*tower, *row, *features[:3]),
        pairs=3 * lefts * slots * slots,
        scratch=[VMEM(side.shape, side.dtype) for side in sides(3)] + [*scratch(3)],
    )
    row_back = gz.give(out_row, 1)
    out_beside, *outs = call(
        functools.partial(rest_kernel, folded),
        [one] * (1 + lefts),
        (*tower, beside, *features, *adds),
        pairs=4 * slots * slots,
        scratch=scratch(2),
    )
    if folded:
        out_own, out_other = outs
        back = [gy.give(out_other, 1)]
    else:
        out_low, out_own, out_high = outs
        back = [gy.give(out_low, -1), gy.give(out_high, 1)]
    to_low, to_high, own = call(merge_kernel, [one] * 3, (row_back, out_beside, out_own))
    return [own, gx.give(to_low, -1), gx.give(to_high, 1), *back]


def on_device(axes, positions, velocities, forces, charges, types, counts, epsilon, sigma):
    slots = positions.shape[-1]
    rings = [Ring(name, size) for name, size in zip(("gx", "gy", "gz"), axes)]
    record, half = pl.pallas_call(
        start_kernel,
        out_shape=[shape(8, slots), shape(3, slots)],
        in_specs=[whole(SMEM)] * 3 + [whole()] * 5,
        out_specs=[whole()] * 2,
    )(counts, epsilon, sigma, positions, velocities, forces, charges, types)
    for step in range(STEPS):
        parts = step_forces(record, *rings)
        if step < STEPS - 1:
            outs = [shape(8, slots), shape(3, slots)]
            record, half = call(middle_kernel, outs, (record, half, *parts))
        else:
            outs = call(last_kernel, [shape(*positions.shape)] * 3, (record, half, *parts))
    return tuple(outs)


def solution(mesh):
    boxes = P(None, "gx", "gy", "gz", None)
    slot = P("gx", "gy", "gz", None)
    in_specs = (boxes, boxes, boxes, slot, slot, P("gx", "gy", "gz"), P(), P())
    axes = tuple(mesh.shape[name] for name in ("gx", "gy", "gz"))
    return jax.shard_map(
        functools.partial(on_device, axes),
        mesh=mesh,
        in_specs=in_specs,
        out_specs=(boxes, boxes, boxes),
        check_vma=False,
    )
```

```python
import functools

import jax
import jax.numpy as jnp
from jax import lax
from jax.experimental import pallas as pl
from jax.experimental.pallas import tpu as pltpu
from jax.sharding import PartitionSpec as P

TILE = 128
STEPS = 2

COULOMB = 0.02
SOFTEN = 0.0225
CUTOFF = 0.81
TIME_STEP = 0.05
HALF_STEP = 0.025
REACH = 4.0 * (CUTOFF + SOFTEN)
LOG2_E = 1.4426950408889634
DEPTH = 32
UNROLL = 4
FAR = 2.0**20
SCALE = 1.0 / (4.0 * CUTOFF * CUTOFF)

F32 = jnp.float32
BF16 = jnp.bfloat16


def start_kernel(count, epsilon, sigma, pos, vel, frc, charge, kinds, record, half):
    live_tiles = count[0, 0, 0]
    slots = pos.shape[4]
    live = lax.broadcasted_iota(jnp.int32, (1, slots), 1) < live_tiles * TILE
    kind = kinds[0, 0]
    depth = jnp.zeros((1, slots), F32)
    size = jnp.zeros((1, slots), F32)
    for k in range(epsilon.shape[0]):
        same = kind == k
        depth = jnp.where(same, epsilon[k], depth)
        size = jnp.where(same, sigma[k], size)
    places = []
    for axis in range(3):
        velocity = vel[axis, 0, 0] + HALF_STEP * frc[axis, 0, 0]
        places.append(pos[axis, 0, 0] + TIME_STEP * velocity)
        half[axis : axis + 1, :] = velocity
    record[...] = jnp.concatenate(
        [
            *places,
            jnp.where(live, (2.0 * COULOMB) ** 0.5 * charge[0, 0], 0.0),
            jnp.where(live, 4.0 * jnp.sqrt(depth), 0.0),
            size,
            jnp.full((1, slots), live_tiles.astype(F32)),
            jnp.zeros((1, slots), F32),
        ],
        0,
    )


def split(value):
    high = value.astype(BF16).astype(F32)
    rest = value - high
    middle = rest.astype(BF16).astype(F32)
    return high, middle, rest - middle


def choose(row, *cases):
    value = 0.0
    for test, case in reversed(cases):
        value = jnp.where(test(row), case, value)
    return value


class Box:
    def __init__(self, record, shift):
        rows = record[...]
        row = lax.broadcasted_iota(jnp.int32, rows.shape, 0)
        self.row = row
        moved = [rows + (value - 0.5) if value != 0.5 else rows for value in shift]
        self.rows = choose(
            row,
            (lambda r: r == 0, moved[0]),
            (lambda r: r == 1, moved[1]),
            (lambda r: r == 2, moved[2]),
            (lambda r: r < 6, rows),
        )
        self.live = jnp.max(record[6:7, 0:TILE]).astype(jnp.int32)
        self.pieces = split(self.rows)
        square = jnp.where(row < 3, self.rows * self.rows, 0.0)
        length = jnp.sum(square, axis=0, keepdims=True)
        self.length = jnp.broadcast_to(4.0 * length, rows.shape)

    def sided(self, pieces, first):
        start = 0 if first else 3
        return choose(
            self.row,
            (lambda r: r == start, pieces[0]),
            (lambda r: r == start + 1, pieces[1]),
            (lambda r: r == start + 2, pieces[2]),
            (lambda r: r < 6, 1.0),
        )

    def pair(self, first, second):
        return choose(
            self.row, (lambda r: r < 3, first), (lambda r: r < 6, pltpu.roll(second, 3, 0))
        )

    def left(self):
        high, middle, low = self.pieces
        length = self.sided(split(self.length + 4.0 * SOFTEN), True)
        pairs = [self.pair(high, high), self.pair(high, middle), self.pair(middle, low)]
        return jnp.concatenate([*pairs, length], 0)

    def right(self):
        high, middle, low = [-8.0 * piece for piece in self.pieces]
        length = self.sided(split(self.length), False)
        pairs = [self.pair(high, middle), self.pair(low, high), self.pair(middle, high)]
        return jnp.concatenate([*pairs, length], 0).astype(BF16)

    def traits(self, slope, start):
        return jnp.where(self.row == 6, slope * self.rows[1:2, :] + start, self.rows)

    def moments(self):
        high, middle, low = self.pieces
        upper = choose(
            self.row,
            (lambda r: r < 3, high),
            (lambda r: r == 3, 1.0),
            (lambda r: r < 7, pltpu.roll(middle, 4, 0)),
        )
        return jnp.concatenate([upper, jnp.where(self.row < 3, low, 0.0)], 0).astype(BF16)


def cut(array, tile):
    return array[:, tile * TILE : (tile + 1) * TILE]


def pair_force(length, mine, theirs):
    inverse = lax.rsqrt(length)
    inverse_sq = inverse * inverse
    screened = (mine[0] * theirs[0]) * (jnp.exp2(length * (inverse * -LOG2_E)) * inverse)
    root = (mine[2] + theirs[2]) * inverse
    ratio = root * root
    cubed = ratio * ratio * ratio
    less = cubed - 1.0
    switch = jnp.maximum(REACH - length, 0.0)
    near = switch * inverse
    nearer = switch * inverse_sq
    charged = screened * (near + nearer + 4.0)
    touching = (mine[1] * theirs[1] * cubed) * (less + (1.5 * nearer) * (cubed + less))
    return switch * (charged + touching)


def halves(force):
    high = force.astype(BF16)
    return high, (force - high.astype(F32)).astype(BF16)


def dot(a, b):
    return jnp.dot(a, b, preferred_element_type=F32)


def dot_rows(a, b):
    return lax.dot_general(a, b, (((1,), (1,)), ((), ())), preferred_element_type=F32)


def resolve(acc, rows, lift=None):
    both = acc[0:8, :] + acc[8:16, :]
    turned = both + pltpu.roll(both, 4, 0)
    force = rows * both[3:4, :] - turned
    if lift is not None:
        row = lax.broadcasted_iota(jnp.int32, force.shape, 0)
        force = force + jnp.where(row == 1, lift, 0.0)
    return (SCALE * force)[0:3, :]


def tower_boxes(tower, folded):
    below, own, above = tower
    if folded:
        return [Box(own, (0, 0, 0)), Box(above, (0, 1, 0))]
    return [Box(ref, (0, move, 0)) for ref, move in zip(tower, (-1, 0, 1))]


def pack_left(boxes, left, left_x, left_traits):
    start = jnp.int32(0)
    for number, box in enumerate(boxes):
        slope = (-16.0, 16.0) if len(boxes) == 2 and number == 1 else (0.0, FAR)
        rows, dots = jnp.concatenate([box.left(), box.traits(*slope)], 0), box.moments()
        for tile in range(dots.shape[1] // TILE):
            columns = cut(rows, tile).T
            left[start + tile] = columns[:, :DEPTH].astype(BF16)
            left_x[start + tile] = cut(dots, tile)
            for trait in range(left_traits.shape[1]):
                column = columns[:, DEPTH + 3 + trait : DEPTH + 4 + trait]
                left_traits[start + tile, trait] = jnp.broadcast_to(column, (TILE, TILE))
        start = start + box.live


def pack_right(rights, own, right, right_x, right_traits):
    def put(spot, traits, features, dots, tile):
        right[spot] = cut(features, tile)
        right_x[spot] = cut(dots, tile)
        right_traits[spot] = cut(traits, tile)

    start = jnp.int32(0)
    for box in rights:
        traits, features, dots = box.traits(16.0, 0.0), box.right(), box.moments()
        tiles = dots.shape[1] // TILE
        for tile in range(tiles):
            put(start + tile, traits, features, dots, tile)
        start = start + box.live
    if own is not None:
        traits, features, dots = own.traits(0.0, FAR), own.right(), own.moments()
        first = start
        for tile in range(tiles):

            @pl.when(tile < own.live)
            def _():
                put(first + own.live - 1 - tile, traits, features, dots, tile)

        start = start + own.live
    put(start, traits, features, dots, 0)
    row = lax.broadcasted_iota(jnp.int32, right_traits.shape[1:], 0)
    right_traits[start] = jnp.where(row == 6, FAR, 0.0)


def starts(boxes):
    spots = [jnp.int32(0)]
    for box in boxes:
        spots.append(spots[-1] + box.live)
    return spots


def pair_blocks(lefts, rights, own, left_side, right_side, scratch):
    folded = len(lefts) == 2
    middle = 0 if folded else 1
    left, left_x, left_traits = left_side
    right, right_x, right_traits = right_side
    left_acc, right_acc, left_low, right_low, parts_a, parts_b, force_a, force_b = scratch
    tiles = lefts[0].rows.shape[1] // TILE
    left_start, right_start = starts(lefts), starts(rights)
    first_own, first_above, n_left = left_start[middle], left_start[middle + 1], left_start[-1]
    n_plate = right_start[-1]
    n_own = jnp.int32(0) if own is None else own.live
    empty = n_plate + n_own
    right_acc[...] = jnp.zeros(right_acc.shape, F32)

    def extent(t):
        if own is None:
            return n_plate
        own_part = jnp.where(t < first_above, n_own - 1 - (t - first_own), n_own)
        return n_plate + jnp.where(t < first_own, 0, own_part)

    def run(begin, stop, blocks, imaged):
        def following(block):
            t, p = block
            step = 2 * p + 2 < extent(t)
            return jnp.where(step, t, jnp.minimum(t + 1, stop)), jnp.where(step, p + 1, 0)

        def place(block):
            t, p = block
            inside = t < stop
            one = jnp.where(inside, 2 * p, empty)
            two = jnp.where(inside & (2 * p + 1 < extent(t)), 2 * p + 1, empty)
            return jnp.where(inside, t, begin), one, two

        def spread(spots):
            t, one, two = spots
            return dot(left[t], jnp.concatenate([right[one], right[two]], 1))

        def work(spots, parts):
            t, one, two = spots
            count = 4 if imaged else 3
            mine = [left_traits[t, trait] for trait in range(count)]
            forces, lowers = [], []
            for lanes, spot in ((slice(0, TILE), one), (slice(TILE, 2 * TILE), two)):
                theirs = [right_traits[spot, 3 + trait : 4 + trait, :] for trait in range(count)]
                length = parts[:, lanes]
                if imaged:
                    lower = mine[3] + theirs[3]
                    force = pair_force(length + jnp.minimum(lower, 0.0), mine, theirs)
                    lowers.append(jnp.where(lower < 0.0, force, 0.0))
                else:
                    force = pair_force(length, mine, theirs)
                forces.append(halves(force))
            return forces, lowers

        def take_down(spots, lowers):
            t, one, two = spots
            left_low[t] = left_low[t] + (lowers[0] + lowers[1])
            for spot, lower in zip((one, two), lowers):
                right_low[spot] = right_low[spot] + jnp.sum(lower.reshape(TILE // 8, 8, TILE), axis=0)

        def hold(split_force, forces):
            for side, (high, low) in enumerate(forces):
                split_force[0, :, side * TILE : (side + 1) * TILE] = high
                split_force[1, :, side * TILE : (side + 1) * TILE] = low

        def gather(spots, split_force):
            t, one, two = spots
            theirs_x = [right_x[one], right_x[two]]
            theirs_x = jnp.concatenate([*theirs_x, *theirs_x], 1)
            mine_x = jnp.concatenate([left_x[t], left_x[t]], 1)
            force = jnp.concatenate([split_force[0], split_force[1]], 1)
            back = dot(mine_x, split_force[...].reshape(2 * TILE, 2 * TILE))
            return dot_rows(theirs_x, force), back

        def collect(spots, sums):
            t, one, two = spots
            forward, back = sums
            left_acc[t] = left_acc[t] + forward
            right_acc[one] = right_acc[one] + back[:, :TILE]
            right_acc[two] = right_acc[two] + back[:, TILE:]

        def some_blocks(_, carry):
            block, before = carry
            spots = [before]
            for _ in range(UNROLL + 1):
                spots.append(place(block))
                ahead, block = block, following(block)
            stores = ((parts_a, force_a), (parts_b, force_b))
            for number in range(UNROLL):
                past, held, now = spots[number : number + 3]
                (parts, out), (into, back) = stores[number % 2], stores[1 - number % 2]
                lengths = spread(now)
                sums = gather(past, back)
                forces, lowers = work(held, parts)
                into[...] = lengths
                hold(out, forces)
                collect(past, sums)
                if imaged:
                    take_down(held, lowers)
            return ahead, spots[UNROLL]

        force_b[...] = jnp.zeros(force_b.shape, BF16)
        first = (begin, jnp.int32(0))
        parts_a[...] = spread(place(first))
        _, last = lax.fori_loop(
            0, (blocks + UNROLL - 1) // UNROLL, some_blocks, (first, (begin, empty, empty))
        )
        collect(last, gather(last, force_b))

    def pairs_of(count):
        return (count + 1) // 2

    left_acc[...] = jnp.zeros(left_acc.shape, F32)
    left_low[...] = jnp.zeros(left_low.shape, F32)
    right_low[...] = jnp.zeros(right_low.shape, F32)
    zero = jnp.int32(0)
    if own is not None:
        blocks = first_own * pairs_of(n_plate) + (n_left - first_above) * pairs_of(n_plate + n_own)
        for tile in range(tiles):
            blocks = blocks + jnp.where(tile < n_own, pairs_of(n_plate + tile), 0)
        run(zero, n_left, blocks, folded)
    elif folded:
        run(zero, first_above, first_above * pairs_of(n_plate), False)
        run(first_above, n_left, (n_left - first_above) * pairs_of(n_plate), True)
    else:
        run(zero, n_left, n_left * pairs_of(n_plate), False)

    if own is not None:
        for tile in range(tiles):
            t = first_own + tile
            spot = jnp.maximum(n_plate + n_own - 1 - tile, 0)
            mine = left[t]
            columns = [left_traits[t, trait] for trait in range(3)]
            theirs = [right_traits[spot, 3 + trait : 4 + trait, :] for trait in range(3)]
            force = pair_force(dot(mine, right[spot]), columns, theirs)
            row = lax.broadcasted_iota(jnp.int32, force.shape, 0)
            col = lax.broadcasted_iota(jnp.int32, force.shape, 1)
            high, low = halves(jnp.where((row != col) & (tile < n_own), force, 0.0))
            theirs_x = right_x[spot]
            left_acc[t] = left_acc[t] + dot_rows(theirs_x, high) + dot_rows(theirs_x, low)

    def alive(box, tile, force):
        return jnp.where(tile < box.live, force, 0.0)

    def left_force(number, tile):
        box, spot = lefts[number], left_start[number] + tile
        acc, lift = left_acc[spot], None
        if folded and number == 1:
            lift = -2.0 * jnp.sum(left_low[spot].T, axis=0, keepdims=True)
        force = resolve(acc, cut(box.rows, tile), lift)
        if own is not None and number == middle:
            force = force + pushed(box, jnp.maximum(n_plate + n_own - 1 - tile, 0), tile)
        return alive(box, tile, force)

    def pushed(box, spot, tile):
        acc, lift = right_acc[spot], None
        if folded:
            lift = 2.0 * jnp.sum(right_low[spot], axis=0, keepdims=True)
        return resolve(acc, cut(box.rows, tile), lift)

    def right_force(number, tile):
        box = rights[number]
        return alive(box, tile, pushed(box, right_start[number] + tile, tile))

    return left_force, right_force


BESIDE = (1, 0, 0)
ROW = ((-1, 0, 1), (0, 0, 1), (1, 0, 1))


def lane(tile):
    return slice(tile * TILE, (tile + 1) * TILE)


def feature_kernel(folded, below, own, above, beside, *sides):
    lefts = tower_boxes((below, own, above), folded)
    pack_left(lefts, *sides[:3])
    pack_right([Box(beside, BESIDE)], lefts[0 if folded else 1], *sides[3:])


def row_kernel(folded, below, own, above, *refs):
    rights, left_side, out_row, refs = refs[:3], refs[3:6], refs[6], refs[7:]
    lefts = tower_boxes((below, own, above), folded)
    outs, refs = refs[: len(lefts)], refs[len(lefts) :]
    right_side, scratch = refs[:3], refs[3:]
    boxes = [Box(ref, move) for ref, move in zip(rights, ROW)]
    pack_right(boxes, None, *right_side)
    left_force, right_force = pair_blocks(lefts, boxes, None, left_side, right_side, scratch)
    for tile in range(own.shape[1] // TILE):
        for number in range(3):
            out_row[3 * number : 3 * number + 3, lane(tile)] = right_force(number, tile)
        for number, out in enumerate(outs):
            out[:, lane(tile)] = left_force(number, tile)


def rest_kernel(folded, below, own, above, beside, *refs):
    left_side, right_side, refs = refs[:3], refs[3:6], refs[6:]
    lefts = tower_boxes((below, own, above), folded)
    adds, refs = refs[: len(lefts)], refs[len(lefts) :]
    out_beside, outs, scratch = refs[0], refs[1 : 1 + len(lefts)], refs[1 + len(lefts) :]
    left_force, right_force = pair_blocks(
        lefts, [Box(beside, BESIDE)], lefts[0 if folded else 1], left_side, right_side, scratch
    )
    for tile in range(own.shape[1] // TILE):
        out_beside[:, lane(tile)] = right_force(0, tile)
        for number, (out, add) in enumerate(zip(outs, adds)):
            out[:, lane(tile)] = left_force(number, tile) + add[:, lane(tile)]


def merge_kernel(row, beside, own, to_low, to_high, total):
    to_low[...] = row[0:3, :]
    to_high[...] = row[6:9, :] + beside[...]
    total[...] = row[3:6, :] + own[...]


def add_up(parts):
    force = parts[0][...]
    for ref in parts[1:]:
        force = force + ref[...]
    return force


def middle_kernel(record, half, *refs):
    force = add_up(refs[:-2])
    new_record, new_half = refs[-2:]
    velocity = half[...] + HALF_STEP * force
    velocity = velocity + HALF_STEP * force
    new_half[...] = velocity
    new_record[3:8, :] = record[3:8, :]
    new_record[0:3, :] = record[0:3, :] + TIME_STEP * velocity


def last_kernel(record, half, *refs):
    force = add_up(refs[:-3])
    places, velocity, pushing = refs[-3:]
    final = half[...] + HALF_STEP * force
    for axis in range(3):
        places[axis, 0, 0] = record[axis : axis + 1, :]
        velocity[axis, 0, 0] = final[axis : axis + 1, :]
        pushing[axis, 0, 0] = force[axis : axis + 1, :]


VMEM = pltpu.VMEM
SMEM = pltpu.SMEM
LIMIT = 32 * 1024 * 1024


def shape(*dims):
    return jax.ShapeDtypeStruct(dims, F32)


def whole(space=VMEM):
    return pl.BlockSpec(memory_space=space)


def call(kernel, outs, args, pairs=0, scratch=()):
    cost = pl.CostEstimate(
        flops=50 * pairs, bytes_accessed=14 * 32 * args[0].shape[1], transcendentals=2 * pairs
    )
    return pl.pallas_call(
        kernel,
        out_shape=outs,
        in_specs=[whole()] * len(args),
        out_specs=[whole()] * len(outs),
        scratch_shapes=list(scratch),
        compiler_params=pltpu.CompilerParams(vmem_limit_bytes=LIMIT),
        cost_estimate=cost,
    )(*args)


class Ring:
    def __init__(self, name, size):
        self.name, self.size = name, size

    def bring(self, value, offset):
        pairs = [((i + offset) % self.size, i) for i in range(self.size)]
        return lax.ppermute(value, self.name, pairs)

    def give(self, value, offset):
        return self.bring(value, -offset)


def step_forces(record, gx, gy, gz):
    slots = record.shape[1]
    one = shape(3, slots)
    up = gz.bring(record, 1)
    above = gy.bring(record, 1)
    below = above if gy.size == 2 else gy.bring(record, -1)
    beside = gx.bring(record, 1)
    row = (gx.bring(up, -1), up, gx.bring(up, 1))
    tower = (below, record, above)
    tiles = slots // TILE
    folded = gy.size == 2
    lefts, traits = (2, 4) if folded else (3, 3)

    def kept(*dims):
        return jax.ShapeDtypeStruct(dims, BF16)

    def sides(boxes):
        count = boxes * tiles + 1
        return kept(count, DEPTH, TILE), kept(count, 16, TILE), shape(count, 8, TILE)

    def scratch(boxes):
        return (
            VMEM((lefts * tiles, 16, TILE), F32),
            VMEM((boxes * tiles + 1, 16, TILE), F32),
            VMEM((lefts * tiles if folded else 1, TILE, TILE), F32),
            VMEM((boxes * tiles + 1, 8, TILE), F32),
            VMEM((TILE, 2 * TILE), F32),
            VMEM((TILE, 2 * TILE), F32),
            VMEM((2, TILE, 2 * TILE), BF16),
            VMEM((2, TILE, 2 * TILE), BF16),
        )

    outs = [kept(lefts * tiles, TILE, DEPTH), kept(lefts * tiles, 16, TILE)]
    outs += [shape(lefts * tiles, traits, TILE, TILE), *sides(2)]
    features = call(
        functools.partial(feature_kernel, folded), outs, (*tower, beside), pairs=slots * slots
    )
    out_row, *adds = call(
        functools.partial(row_kernel, folded),
        [shape(9, slots)] + [one] * lefts,
        (*tower, *row, *features[:3]),
        pairs=3 * lefts * slots * slots,
        scratch=[VMEM(side.shape, side.dtype) for side in sides(3)] + [*scratch(3)],
    )
    row_back = gz.give(out_row, 1)
    out_beside, *outs = call(
        functools.partial(rest_kernel, folded),
        [one] * (1 + lefts),
        (*tower, beside, *features, *adds),
        pairs=4 * slots * slots,
        scratch=scratch(2),
    )
    if folded:
        out_own, out_other = outs
        back = [gy.give(out_other, 1)]
    else:
        out_low, out_own, out_high = outs
        back = [gy.give(out_low, -1), gy.give(out_high, 1)]
    to_low, to_high, own = call(merge_kernel, [one] * 3, (row_back, out_beside, out_own))
    return [own, gx.give(to_low, -1), gx.give(to_high, 1), *back]


def on_device(axes, positions, velocities, forces, charges, types, counts, epsilon, sigma):
    slots = positions.shape[-1]
    rings = [Ring(name, size) for name, size in zip(("gx", "gy", "gz"), axes)]
    record, half = pl.pallas_call(
        start_kernel,
        out_shape=[shape(8, slots), shape(3, slots)],
        in_specs=[whole(SMEM)] * 3 + [whole()] * 5,
        out_specs=[whole()] * 2,
    )(counts, epsilon, sigma, positions, velocities, forces, charges, types)
    for step in range(STEPS):
        parts = step_forces(record, *rings)
        if step < STEPS - 1:
            outs = [shape(8, slots), shape(3, slots)]
            record, half = call(middle_kernel, outs, (record, half, *parts))
        else:
            outs = call(last_kernel, [shape(*positions.shape)] * 3, (record, half, *parts))
    return tuple(outs)


def solution(mesh):
    boxes = P(None, "gx", "gy", "gz", None)
    slot = P("gx", "gy", "gz", None)
    in_specs = (boxes, boxes, boxes, slot, slot, P("gx", "gy", "gz"), P(), P())
    axes = tuple(mesh.shape[name] for name in ("gx", "gy", "gz"))
    return jax.shard_map(
        functools.partial(on_device, axes),
        mesh=mesh,
        in_specs=in_specs,
        out_specs=(boxes, boxes, boxes),
        check_vma=False,
    )
```
